128 devices in a mesh: group: 4 (over y), sub: 32 (over x, z, core).
Axes of the slice: x: 4, y: 4, z: 4, core: 2. Of those that a mesh axis runs over, the one named last changes fastest.
Arguments:
- adjoint_start: float32 [6, 128, 12288], P(None, 'group', 'sub'), may hold values from -6 to 6
- objective_grad: float32 [6, 128, 12288], P(None, 'group', 'sub'), may hold values from -24 to 24
- diagonal: float32 [128, 12288], P('group', 'sub'), may hold values from 4 to 8
- connect: int32 [64, 43264], P(None, ('group', 'sub')), may hold values from 0 to 14819, as said below
- element_scale: float32 [64, 43264], P(None, ('group', 'sub')), may hold values from 0.5 to 2
- element_matrix: bfloat16 [64, 64], replicated, may hold values from -0.75 to 0.75
- traction_map: float32 [3, 6], replicated, may hold values from -2.5 to 2.5
- iface_node: int32 [262144], P(('group', 'sub')), may hold values from 0 to 12287
- iface_dest: int32 [262144, 1], P(('group', 'sub')), may hold values from 0 to 127; in each aligned block of 2048 rows (0 to 2047, 2048 to 4095, ...) at most 32 rows name the same one
- iface_target: int32 [262144], P(('group', 'sub')), may hold values from 0 to 2047
- iface_count: int32 [128], P(('group', 'sub')), may hold values from 1 to 2048, 196608 in all
Outputs:
- adjoint: float32 [6, 128, 12288], P(None, 'group', 'sub')
- struct_load: float32 [2, 3, 262144], P(None, None, ('group', 'sub'))
The draws below stay inside these ranges and needn't reach their ends.
Inputs may be any that keep to these rules, and one draw needn't show every extreme that they name: `connect`: the elements of one device tile its extended grid in an order drawn from the seed: element nodes are 4 consecutive rows by 16 consecutive columns, starting at row min(3 i, 34) and column min(15 j, 374) for every i below (36) // 3 + 1 and j below (388) // 15 + 1, each such element once. `iface_dest`: among the rows of one device, no structural device is named by more than 32 rows.
All inputs are finite; a program needn't handle non-finite values. No bound on the sum of `iface_count` on one device may be relied on, other than what follows from the above.
Results may differ from the reference program's by a relative error of at most 0.00091.
Values sent between devices are 32-bit elements; how exact they have to be, the bound alone decides.
A program may use at most 128 MiB of HBM per device.

```python
import math
import jax
import jax.numpy as jnp
import numpy as np
from jax import lax

COMP = 6
SPAN_DEV = 32
CROSS_DEV = 384
E_DEV = 338
IF_CAP = 2048
CAP = 32
S_DEV = 2048
ITERS = 2
SWEEPS = 2
NA = 128
NB = 12288
ELEMS = 43264
IFROWS = 262144
STRUCT = 262144
N_GROUP = 4
N_SUB = 32
DEVICES = 128


def draw_connect(key, part):
    key = jax.random.fold_in(key, 5)
    row_count = (SPAN_DEV + 4) // 3 + 1
    col_count = (CROSS_DEV + 4) // 15 + 1
    row_starts = jnp.minimum(3 * jnp.arange(row_count, dtype=jnp.int32), SPAN_DEV + 2)
    col_starts = jnp.minimum(15 * jnp.arange(col_count, dtype=jnp.int32), CROSS_DEV - 10)
    rows_flat = jnp.repeat(row_starts, col_count)
    cols_flat = jnp.tile(col_starts, row_count)
    device_keys = jax.random.split(key, DEVICES)
    orders = jax.vmap(lambda k: jax.random.permutation(k, E_DEV))(device_keys).astype(jnp.int32)
    rows_base = jnp.take(rows_flat, orders)
    cols_base = jnp.take(cols_flat, orders)
    offset_rows = jnp.repeat(jnp.arange(4, dtype=jnp.int32), 16)
    offset_cols = jnp.tile(jnp.arange(16, dtype=jnp.int32), 4)
    nodes = (rows_base[..., None] + offset_rows) * (CROSS_DEV + 6) + cols_base[..., None] + offset_cols
    return nodes.transpose(2, 0, 1).reshape(64, DEVICES * E_DEV).astype(jnp.int32)


def touch_ends(values, key, low, high):
    extent = values.shape
    index_at = [jax.random.randint(jax.random.fold_in(key, axis), (), 0, extent[axis]) for axis in range(len(extent))]
    values = values.at[tuple(index_at)].set(low)
    longest = extent.index(max(extent))
    index_at[longest] = (index_at[longest] + 1) % extent[longest]
    return values.at[tuple(index_at)].set(high)


def block_levels(own_key, dims, pieces, smallest, high):
    gain = 1.0
    for position, blocks in pieces:
        heights = jax.random.uniform(jax.random.fold_in(jax.random.fold_in(own_key, 6), position), (blocks,), jnp.float32, smallest / len(pieces), high / len(pieces))
        gain = gain * jnp.repeat(jnp.exp(heights), dims[position] // blocks).reshape((-1,) + (1,) * (len(dims) - 1 - position))
    return gain


def profile(count, total, reach, skew):
    weights = [(1 << 20) // math.isqrt(rank ** skew) + 1 for rank in range(2, count + 1)]
    rest, holding = total - reach - (count - 1), [1] * (count - 1)
    while rest > 0:
        candidates = [i for i in range(count - 1) if holding[i] < reach]
        mass, budget = sum([weights[i] for i in candidates]), rest
        for i in candidates:
            more = min(reach - holding[i], max(1, budget * weights[i] // mass), rest)
            holding[i] = holding[i] + more
            rest = rest - more
    return np.array([reach] + holding)


def uneven(key, number_of, total, bound, skew):
    if number_of == 2:
        one = jax.random.randint(key, (), max(1, total - bound), min(bound, total - 1) + 1)
        return jnp.stack([one, total - one])
    tallies = jnp.asarray(profile(number_of, total, bound, skew), jnp.int32)
    couples = (number_of - 1) // 2
    donor, sink = tallies[1:1 + 2 * couples:2], tallies[2:2 + 2 * couples:2]
    room = jnp.minimum(donor - 1, bound - sink)
    moved = jax.random.randint(jax.random.fold_in(key, 1), (couples,), 0, 1 << 20) % (room + 1)
    tallies = tallies.at[1:1 + 2 * couples:2].set(donor - moved).at[2:2 + 2 * couples:2].set(sink + moved)
    return tallies[jax.random.permutation(jax.random.fold_in(key, 2), number_of)]


def shared_out(own_key, own, number, rows, amount, top, bound, skew):
    sequence = jax.random.permutation(own_key, amount)
    packed, ordinary = shares(amount, rows * top, bound, skew, True), shares(amount, rows * top, bound, skew, False)
    places = jnp.arange(amount)

    def named(sizes, offset_by):
        used = int((sizes > 0).sum())
        fixed = max(1, used // 4)
        shifted = fixed + (places - fixed + offset_by * (used - fixed)) % max(1, amount - fixed)
        return jnp.zeros((amount,), jnp.int32).at[sequence[jnp.where(places < fixed, places, shifted)]].set(jnp.asarray(sizes, jnp.int32))

    sizes = jnp.where(number % 4 == 0, named(packed, number // 4), named(ordinary, number - number // 4 - 1))
    mixed = jax.random.permutation(jax.random.fold_in(own, 3), amount)
    giver, taker = mixed[0:amount // 2 * 2:2], mixed[1:amount // 2 * 2:2]
    margin = jnp.minimum(sizes[giver] - 1, bound - sizes[taker]) // 2
    margin = jnp.where((giver == sequence[0]) | (taker == sequence[0]) | (sizes[taker] == 0), 0, jnp.maximum(margin, 0))
    shifted = jax.random.randint(jax.random.fold_in(own, 4), (amount // 2,), 0, 1 << 20) % (margin + 1)
    sizes = sizes.at[giver].add(-shifted).at[taker].add(shifted)
    members = jnp.searchsorted(jnp.cumsum(sizes), jnp.arange(rows * top), side="right").astype(jnp.int32)
    listing = members.reshape(top, rows).T
    listing = listing[jax.random.permutation(jax.random.fold_in(own, 1), rows)]
    offset_by = jax.random.randint(jax.random.fold_in(own, 2), (rows, 1), 0, top)
    return jnp.take_along_axis(listing, (jnp.arange(top)[None, :] + offset_by) % top, axis=1)


def shares(amount, total, most, lean, full):
    portions = [(1 << 20) // math.isqrt(grade ** lean) + 1 for grade in range(1, amount + 1)]
    largest = most if full else min(most, max(-(-total // amount), total * portions[0] // sum(portions)))
    least = 1 if total - largest >= amount - 1 else 0
    counts, rest = [largest] + [least] * (amount - 1), total - largest - least * (amount - 1)
    while rest > 0:
        candidates = [i for i in range(1, amount) if counts[i] < largest] or [i for i in range(1, amount) if counts[i] < most]
        whole, left = sum([portions[i] for i in candidates]), rest
        for i in candidates:
            addition = min(most - counts[i], max(1, left * portions[i] // whole), rest)
            counts[i] = counts[i] + addition
            rest = rest - addition
    return np.array(counts)


def noise(rng, dims, scale, limit, cuts=(), kind=jnp.bfloat16):
    drawn = scale * jax.random.normal(rng, dims, jnp.float32)
    if cuts:
        drawn = drawn * block_levels(rng, dims, cuts, -0.22, 0.18)
    return jnp.clip(drawn, -limit, limit).astype(kind)


def setup_inputs(seed: int = 0) -> dict:
    key_list = jax.random.split(jax.random.key(seed), 12)
    adjoint_start = noise(key_list[0], (COMP, NA, NB), 1.0, 6.0, ((1, 4), (2, 32)), jnp.float32)
    objective_grad = noise(key_list[1], (COMP, NA, NB), 4.0, 24.0, ((1, 4), (2, 32)), jnp.float32)
    diagonal = jnp.clip(4.0 + 4.0 * jax.random.uniform(key_list[2], (NA, NB), jnp.float32) ** block_levels(key_list[2], (NA, NB), ((0, 4), (1, 32)), -0.2, 0.2), 4.0, 8.0)
    connect = draw_connect(jax.random.fold_in(key_list[11], 71), 0)
    element_scale = jnp.clip(jnp.exp(math.log(2.0) - 1.3862944 * jax.random.uniform(key_list[4], (64, ELEMS), jnp.float32) ** block_levels(key_list[4], (64, ELEMS), ((1, 128),), -0.2, 0.2)), 0.5, 2.0)
    element_matrix = noise(key_list[5], (64, 64), 64 ** -0.5, 0.75)
    traction_map = noise(key_list[6], (3, COMP), COMP ** -0.5, 2.5, (), jnp.float32)
    iface_node = touch_ends(jax.random.randint(key_list[7], (IFROWS,), 0, SPAN_DEV * CROSS_DEV), jax.random.fold_in(key_list[7], 1), 0, (SPAN_DEV * CROSS_DEV) - 1).astype(jnp.int32)
    iface_dest_keys = jax.random.split(jax.random.fold_in(key_list[8], 1), IFROWS // IF_CAP)
    iface_dest_turns = jax.random.permutation(jax.random.fold_in(key_list[8], 3), IFROWS // IF_CAP)
    iface_dest = jax.vmap(lambda own, number: shared_out(jax.random.fold_in(key_list[8], 2), own, number, IF_CAP, DEVICES, 1, CAP, 2))(iface_dest_keys, iface_dest_turns).reshape((IFROWS, 1))
    iface_target = touch_ends(jax.random.randint(key_list[9], (IFROWS,), 0, S_DEV), jax.random.fold_in(key_list[9], 1), 0, S_DEV - 1).astype(jnp.int32)
    iface_count = uneven(key_list[10], DEVICES, DEVICES * IF_CAP * 3 // 4, IF_CAP, 2).astype(jnp.int32)
    return dict(adjoint_start=adjoint_start, objective_grad=objective_grad, diagonal=diagonal, connect=connect, element_scale=element_scale, element_matrix=element_matrix, traction_map=traction_map, iface_node=iface_node, iface_dest=iface_dest, iface_target=iface_target, iface_count=iface_count)


def sweep_all(adjoint, objective_grad, diagonal, connect, element_scale, element_matrix):
    padded = jnp.pad(adjoint, ((0, 0), (3, 3), (3, 3)))
    wide = NB + 6
    flat = padded.reshape(COMP, -1)
    ext_cols = CROSS_DEV + 6
    conn_dev = connect.reshape(64, DEVICES, E_DEV)
    scale_dev = element_scale.reshape(64, DEVICES, E_DEV)
    matrix_f = element_matrix.astype(jnp.float32)

    def one_device(index):
        device = index.astype(jnp.int32)
        group_at = device // N_SUB
        sub_at = device % N_SUB
        local = lax.dynamic_index_in_dim(conn_dev, device, 1, False)
        factor = lax.dynamic_index_in_dim(scale_dev, device, 1, False)
        row_ext = local // ext_cols
        col_ext = local % ext_cols
        global_idx = (group_at * SPAN_DEV + row_ext) * wide + sub_at * CROSS_DEV + col_ext
        gathered = jnp.take(flat, global_idx.reshape(-1), axis=1).reshape(COMP, 64, E_DEV)
        scaled = (gathered * factor[None]).astype(jnp.bfloat16)
        elem_out = jnp.einsum("cje,jk->cke", scaled.astype(jnp.float32), matrix_f)
        elem_out = elem_out.reshape(COMP, 64 * E_DEV)
        inside = (row_ext >= 3) & (row_ext < SPAN_DEV + 3) & (col_ext >= 3) & (col_ext < CROSS_DEV + 3)
        target = jnp.where(inside, (row_ext - 3) * CROSS_DEV + col_ext - 3, SPAN_DEV * CROSS_DEV).reshape(-1)
        summed = jax.vmap(lambda values: jax.ops.segment_sum(values, target, SPAN_DEV * CROSS_DEV + 1))(elem_out)
        return summed[:, :SPAN_DEV * CROSS_DEV]

    blocks = lax.map(one_device, jnp.arange(DEVICES, dtype=jnp.int32))
    blocks = blocks.reshape(N_GROUP, N_SUB, COMP, SPAN_DEV, CROSS_DEV)
    assembled = blocks.transpose(2, 0, 3, 1, 4).reshape(COMP, NA, NB)
    return (objective_grad - assembled) / diagonal[None]


def tractions(adjoint, traction_map, iface_node, iface_dest, iface_target, iface_count):
    blocks = adjoint.reshape(COMP, N_GROUP, SPAN_DEV, N_SUB, CROSS_DEV).transpose(1, 3, 0, 2, 4)
    blocks = blocks.reshape(DEVICES, COMP, SPAN_DEV * CROSS_DEV)
    nodes = iface_node.reshape(DEVICES, IF_CAP)
    values = jax.vmap(lambda block, node: jnp.take(block, node, axis=1))(blocks, nodes)
    traction = jnp.einsum("kc,dcr->drk", traction_map, values, precision=lax.Precision.HIGHEST)
    live = jnp.arange(IF_CAP, dtype=jnp.int32)[None, :] < iface_count[:, None]
    traction = jnp.where(live[..., None], traction, 0.0).reshape(IFROWS, 3)
    target = iface_dest[:, 0] * S_DEV + iface_target
    load = jax.ops.segment_sum(traction, target, STRUCT)
    return load.T


def reference(adjoint_start, objective_grad, diagonal, connect, element_scale, element_matrix, traction_map, iface_node, iface_dest, iface_target, iface_count):
    adjoint = adjoint_start
    loads = []
    for outer in range(ITERS):
        for inner in range(SWEEPS):
            adjoint = sweep_all(adjoint, objective_grad, diagonal, connect, element_scale, element_matrix)
        loads.append(tractions(adjoint, traction_map, iface_node, iface_dest, iface_target, iface_count))
    return adjoint, jnp.stack(loads)
```

```python
import functools
import jax
import jax.numpy as jnp
from jax import lax
from jax.experimental import pallas as pl
from jax.experimental.pallas import tpu as pltpu
from jax.sharding import PartitionSpec as P

COMP = 6
ROWS = 32
COLS = 384
ELEMS = 338
IF_CAP = 2048
CAP = 32
ITERS = 2
SWEEPS = 2
LANES = 512
W = 8
F32 = jnp.float32
BF16 = jnp.bfloat16
MESH = pl.DeviceIdType.MESH
NT = (((1,), (1,)), ((), ()))


def iota(shape, dim):
    return lax.broadcasted_iota(jnp.int32, shape, dim)


def onehot(mask):
    return jnp.where(mask, 1.0, 0.0).astype(BF16)


def mm(a, b):
    return jnp.dot(a, b, preferred_element_type=F32)


def mm_nt(a, b):
    return lax.dot_general(a, b, NT, preferred_element_type=F32)


def pieces(x, n):
    out = []
    for k in range(n):
        p = x.astype(BF16)
        out.append(p)
        if k + 1 < n:
            x = x - p.astype(F32)
    return out


def total(terms):
    terms = list(terms)
    while len(terms) > 1:
        terms = [
            terms[i] + terms[i + 1] if i + 1 < len(terms) else terms[i]
            for i in range(0, len(terms), 2)
        ]
    return terms[0]


def pick(x, sel, n=3):
    return total([mm(p, sel) for p in pieces(x, n)])


def pick_rows(sel, x, n=3):
    return total([mm(sel, p) for p in pieces(x, n)])


def ext_col(lane):
    j = lane >> 4
    return jnp.where(j == 25, 374, 15 * j) + (lane & 15)


def kernel(
    G,
    S,
    adj_ref,
    obj_ref,
    diag_ref,
    conn_ref,
    scale_ref,
    em_ref,
    tm_ref,
    node_ref,
    dest_ref,
    target_ref,
    count_ref,
    out_ref,
    load_ref,
    state,
    asm,
    scale_x,
    oi,
    inv,
    wmat,
    conn_raw,
    conn_sem,
    conn_pad,
    scale_pad,
    colhot,
    desthot,
    slot_s,
    rowsend,
    rowrecv,
    colsend,
    colrecv,
    abuf,
    r1,
    r1t,
    r3,
    halo_send,
    halo_recv,
    a1_send,
    a1_recv,
    a2_send,
    a2_recv,
):
    X = S // W
    D = G * S
    g = lax.axis_index("group")
    s = lax.axis_index("sub")
    x = s // W
    w = s % W

    def at(dg, ds):
        return (lax.rem(g + dg + G, G), lax.rem(s + ds + S, S))

    def at_gx(dg, dx):
        return (lax.rem(g + dg, G), lax.rem(x + dx, X) * W + w)

    def at_w(dw):
        return (g, x * W + lax.rem(w + dw, W))

    halo_partners = [(-1, 0), (1, 0)] + [(dg, ds) for ds in (-1, 1) for dg in (-1, 0, 1)]
    gx_partners = [(dg, dx) for dg in range(G) for dx in range(X)][1:]
    barrier = pltpu.get_barrier_semaphore()
    targets = [at(*p) for p in halo_partners]
    targets += [at_gx(*p) for p in gx_partners] + [at_w(dw) for dw in range(1, W)]
    for t in targets:
        pl.semaphore_signal(barrier, inc=1, device_id=t, device_id_type=MESH)

    conn_copy = pltpu.make_async_copy(conn_ref.at[0:8], conn_raw, conn_sem)
    conn_copy.start()
    lane8 = iota((8, 128), 1)

    def halo_copies(t):
        copies = []

        def add(src, dst, dev):
            n = len(copies)
            copies.append(
                pltpu.make_async_remote_copy(
                    src_ref=src,
                    dst_ref=dst,
                    send_sem=halo_send.at[t, n],
                    recv_sem=halo_recv.at[t, n],
                    device_id=dev,
                    device_id_type=MESH,
                )
            )

        add(rowsend.at[t, 0], rowrecv.at[t, 1], at(-1, 0))
        add(rowsend.at[t, 1], rowrecv.at[t, 0], at(1, 0))
        for side, ds in ((0, -1), (1, 1)):
            for dg in (-1, 0, 1):
                add(colsend.at[t, side], colrecv.at[t, 1 - side, 1 - dg], at(dg, ds))
        return copies

    def halo_start(t):
        rowsend[t, 0] = state[1]
        rowsend[t, 1, 0] = state[10, 2]
        rowsend[t, 1, 1] = state[11, 0]
        rowsend[t, 1, 2] = state[11, 1]
        left, right = [], []
        for p in range(ROWS):
            i, a = divmod(p + 3, 3)
            v = jnp.where((lane8 >= 3) & (lane8 < 6), state[i, a, :, 0:128], 0.0)
            left.append(pltpu.roll(v, (3 * p - 3) % 128, 1))
            v = jnp.where((lane8 >= 26) & (lane8 < 29), state[i, a, :, 384:512], 0.0)
            right.append(pltpu.roll(v, (3 * p - 26) % 128, 1))
        colsend[t, 0] = total(left)
        colsend[t, 1] = total(right)
        copies = halo_copies(t)
        if t == 0:
            pl.semaphore_wait(barrier, len(targets))
        for c in copies:
            c.start()
        return copies

    def halo_finish(t, copies):
        for c in copies:
            c.wait_recv()
        state[0] = rowrecv[t, 0]
        state[11, 2] = rowrecv[t, 1, 0]
        state[12, 0] = rowrecv[t, 1, 1]
        state[12, 1] = rowrecv[t, 1, 2]
        bufs = [[colrecv[t, side, k] for k in range(3)] for side in range(2)]
        for r in range(ROWS + 6):
            i, a = divmod(r, 3)
            k, p = (0, 29 + r) if r < 3 else ((1, r - 3) if r < 35 else (2, r - 35))
            v = pltpu.roll(bufs[0][k], (-3 * p) % 128, 1)
            state[i, a, :, 0:128] = state[i, a, :, 0:128] + jnp.where(lane8 < 3, v, 0.0)
            v = pltpu.roll(bufs[1][k], (29 - 3 * p) % 128, 1)
            state[i, a, :, 384:512] = state[i, a, :, 384:512] + jnp.where(
                (lane8 >= 29) & (lane8 < 32), v, 0.0
            )

    lane = iota((COLS, LANES), 1)
    sel = onehot((ext_col(lane) == iota((COLS, LANES), 0) + 3) & (lane < 416))
    m = iota((ROWS * 8, COMP * ROWS), 0)
    perm = onehot(((m & 7) * ROWS + (m >> 3) == iota((ROWS * 8, COMP * ROWS), 1)) & ((m & 7) < COMP))

    def set_own(ref, value):
        v = value.reshape(ROWS, 8, LANES)
        ref[1:11] = v[:30].reshape(10, 3, 8, LANES)
        ref[11, 0:2] = v[30:]

    state[...] = jnp.zeros_like(state)
    first = pick_rows(perm, adj_ref[...].reshape(COMP * ROWS, COLS))
    set_own(state, pick(first, sel))
    copies = halo_start(0)

    inverse = 1.0 / diag_ref[...]
    scaled_obj = obj_ref[...] * inverse[None]
    oi[...] = jnp.zeros_like(oi)
    inv[...] = jnp.zeros_like(inv)
    set_own(oi, pick(pick_rows(perm, scaled_obj.reshape(COMP * ROWS, COLS)), sel))
    rows_8 = jnp.broadcast_to(inverse[:, None, :], (ROWS, 8, COLS)).reshape(ROWS * 8, COLS)
    set_own(inv, pick(rows_8, sel))

    conn_pad[...] = jnp.full_like(conn_pad, -1)
    conn_copy.wait()
    conn_pad[:, 0:ELEMS] = conn_raw[...]
    scale_pad[...] = jnp.zeros_like(scale_pad)
    scale_pad[:, 0:ELEMS] = scale_ref[...]
    node0 = conn_pad[0:1]
    row0 = lax.div(node0, jnp.int32(390))
    col0 = node0 - row0 * 390
    elem_i = jnp.where(node0 >= 0, lax.div(row0 + 2, jnp.int32(3)), -1)
    elem_j = jnp.where(node0 >= 0, lax.div(col0 + 14, jnp.int32(15)), -1)
    row_hot = onehot(elem_i == (iota((112, 384), 0) >> 3))
    i_of = iota((112, LANES), 0) >> 3
    start_row = jnp.minimum(3 * i_of, ROWS + 2)
    lane = iota((112, LANES), 1)
    off_left = (s == 0) & (lane < 3)
    off_right = (s == S - 1) & (lane >= 413)
    j_mask = elem_j[:, None, :] == iota((32, 16, 384), 0)
    for a in range(4):
        sc = scale_pad[16 * a : 16 * a + 16]
        out = []
        for p in pieces(sc, 3):
            p = jnp.where(j_mask, p.astype(F32)[None], 0.0).reshape(LANES, 384)
            out.append(mm_nt(row_hot, p.astype(BF16)))
        r = start_row + a
        off = ((g == 0) & (r < 3)) | ((g == G - 1) & (r >= ROWS + 3)) | off_left | off_right
        scale_x[a] = jnp.where(off, 0.0, total(out)).reshape(14, 8, LANES)

    r = iota((LANES, 64), 0)
    e_hot = onehot((r >> 7) * 16 + (r & 15) == iota((LANES, 64), 1))
    left = mm(e_hot, em_ref[...]).astype(BF16)
    rr, cc = iota((LANES, LANES), 0), iota((LANES, LANES), 1)
    wide = mm_nt(left, e_hot)
    wmat[...] = jnp.where(((rr >> 4) & 7) == ((cc >> 4) & 7), wide, 0.0).astype(BF16)

    def sweep():
        for q in range(4):
            cols = slice(128 * q, 128 * q + 128)
            parts = []
            for a in range(4):
                main = state[0:12, a, :, cols] if a < 3 else state[1:13, 0, :, cols]
                i, b = [(11, 1), (11, 2), (12, 0), (12, 1)][a]
                last = state[i, b, :, cols][None]
                v = jnp.concatenate([main, last, jnp.zeros_like(last)], axis=0)
                v = v * scale_x[a, :, :, cols]
                parts.append(v.reshape(112, 128).astype(BF16))
            o = mm(jnp.concatenate(parts, axis=1), wmat[...])
            o = [o[:, 128 * a : 128 * a + 128].reshape(14, 8, 128) for a in range(4)]
            asm[:, 0, :, cols] = o[0][1:12] + o[3][0:11]
            asm[0:10, 1, :, cols] = o[1][1:11]
            asm[10, 1, :, cols] = o[1][11] + o[0][12]
            asm[:, 2, :, cols] = o[2][1:12]
        lane = iota((24, 128), 1)
        low = lane & 15
        for i in range(11):
            tiles = [asm[i, :, :, 128 * q : 128 * q + 128].reshape(24, 128) for q in range(4)]
            up = [pltpu.roll(v, 1, 1) for v in tiles]
            down = [pltpu.roll(v, 127, 1) for v in tiles]
            for q in range(4):
                before = up[q] if q == 0 else jnp.where(lane == 0, up[q - 1], up[q])
                after = down[q] if q == 3 else jnp.where(lane == 127, down[q + 1], down[q])
                if q < 3:
                    more = jnp.where(low == 0, before, jnp.where(low == 15, after, 0.0))
                    if q == 0:
                        more = jnp.where(lane == 0, 0.0, more)
                else:
                    more = jnp.where(lane == 0, before, 0.0)
                    more = jnp.where(
                        (lane == 14) | (lane == 15), pltpu.roll(tiles[3], 126, 1), more
                    )
                    more = jnp.where(
                        (lane == 16) | (lane == 17), pltpu.roll(tiles[3], 2, 1), more
                    )
                cols = slice(128 * q, 128 * q + 128)
                whole = (tiles[q] + more).reshape(3, 8, 128)
                state[i + 1, :, :, cols] = oi[i + 1, :, :, cols] - whole * inv[i + 1, :, :, cols]

    CH = 512
    node = node_ref[...]
    node_row = lax.div(node, jnp.int32(COLS))
    e_col = node - node_row * COLS + 3
    e_lane = jnp.where(e_col < 375, e_col + lax.div(e_col, jnp.int32(15)), e_col + 26)

    def setup_rows():
        live = iota((1, IF_CAP), 1) < count_ref[0]
        dest = jnp.where(live, dest_ref[...], -1)
        tri = onehot(iota((256, 256), 0) < iota((256, 256), 1))
        carry = jnp.zeros((D, 1), F32)
        for b in range(IF_CAP // 256):
            cols = slice(256 * b, 256 * b + 256)
            hot = jnp.where(dest[:, cols] == iota((D, 256), 0), 1.0, 0.0)
            desthot[:, cols] = hot.astype(BF16)
            before = mm(hot.astype(BF16), tri) + carry
            slot_s[:, cols] = jnp.sum(before * hot, axis=0, keepdims=True)
            carry = carry + jnp.sum(hot, axis=1, keepdims=True)
        for b in range(IF_CAP // CH):
            cols = slice(CH * b, CH * b + CH)
            colhot[:, cols] = onehot(e_lane[:, cols] == iota((LANES, CH), 0))

    def gather(t):
        lane = iota((1, 256), 1)
        trac = []
        for k in range(3):
            row = jnp.zeros((1, 256), F32)
            for c in range(COMP):
                row = jnp.where((lane & 7) == c, tm_ref[k, c], row)
            trac.append(jnp.where((iota((32, 256), 1) >> 3) == iota((32, 256), 0), row, 0.0))
        trac = jnp.concatenate(trac, axis=0)
        own = jnp.concatenate(
            [state[1:11].reshape(240, LANES), state[11, 0:2].reshape(16, LANES)], axis=0
        )
        field = jnp.dot(trac, own, precision=lax.Precision.HIGHEST, preferred_element_type=F32)
        field = jnp.concatenate(pieces(field, 2), axis=0)
        acc = jnp.zeros((D, 128), F32)
        for b in range(IF_CAP // CH):
            cols = slice(CH * b, CH * b + CH)
            v = mm(field, colhot[:, cols])
            v = (v[:96] + v[96:]).reshape(3, 32, CH)
            v = jnp.where(node_row[:, cols][None] == iota((3, 32, CH), 1), v, 0.0)
            v = jnp.sum(v, axis=1, keepdims=True)
            v = jnp.concatenate([v, target_ref[:, cols].astype(F32)[None]], axis=0)
            slots = slot_s[:, cols].astype(jnp.int32)[None] == iota((4, CAP, CH), 1)
            v = jnp.where(slots, v, 0.0).reshape(4 * CAP, CH)
            for p in pieces(v, 2):
                acc = acc + mm_nt(desthot[:, cols], p)
        abuf[t] = acc.reshape(D // 8, 8, 128)

    def a2a_1(t):
        copies = []
        for o, (dg, dx) in enumerate(gx_partners):
            to_g, to_s = at_gx(dg, dx)
            copies.append(
                pltpu.make_async_remote_copy(
                    src_ref=abuf.at[t, to_g * X + to_s // W],
                    dst_ref=r1.at[t, pl.ds(8 * (o + 1), 8)],
                    send_sem=a1_send.at[t, o],
                    recv_sem=a1_recv.at[t, o],
                    device_id=(to_g, to_s),
                    device_id_type=MESH,
                )
            )
            copies[-1].start()
        r1[t, 0:8] = abuf[t, g * X + x]
        return copies

    def a2a_2(t, first):
        for c in first:
            c.wait_recv()
        for d in range(W):
            r1t[t, d] = r1[t, pl.ds(d, D // W, stride=W), :]
        copies = []
        for dw in range(1, W):
            to = at_w(dw)
            copies.append(
                pltpu.make_async_remote_copy(
                    src_ref=r1t.at[t, lax.rem(w + dw, W)],
                    dst_ref=r3.at[t, dw],
                    send_sem=a2_send.at[t, dw - 1],
                    recv_sem=a2_recv.at[t, dw - 1],
                    device_id=to,
                    device_id_type=MESH,
                )
            )
            copies[-1].start()
        r3[t, 0] = r1t[t, w]
        return copies

    def place(t, second):
        for c in second:
            c.wait_recv()
        got = r3[t].reshape(D, 128).T
        name = got[96:128]
        high = jnp.floor(name * (1.0 / 128.0))
        low = name - 128.0 * high
        acc = jnp.zeros((96, 128), F32)
        for q in range(CAP // 4):
            left, right = [], []
            for z in range(4 * q, 4 * q + 4):
                right.append(onehot(low[z : z + 1] == iota((128, D), 0).astype(F32)))
                hit = high[z : z + 1] == iota((16, D), 0).astype(F32)
                v = jnp.concatenate(
                    [jnp.where(hit, got[32 * k + z : 32 * k + z + 1], 0.0) for k in range(3)], axis=0
                )
                left.append(jnp.concatenate(pieces(v, 2), axis=0))
            acc = acc + mm_nt(jnp.concatenate(left, axis=1), jnp.concatenate(right, axis=1))
        acc = acc[:48] + acc[48:]
        for k in range(3):
            for h in range(16):
                load_ref[t, k : k + 1, 128 * h : 128 * h + 128] = acc[16 * k + h : 16 * k + h + 1]

    def write_adjoint():
        own = jnp.concatenate(
            [state[1:11].reshape(240, LANES), state[11, 0:2].reshape(16, LANES)], axis=0
        )
        lane = iota((LANES, COLS), 0)
        j, b = lane >> 4, lane & 15
        keep = ((j < 25) & (b < 15)) | ((j == 25) & (b > 0))
        back = onehot(keep & (ext_col(lane) == iota((LANES, COLS), 1) + 3))
        n = iota((COMP * ROWS, ROWS * 8), 1)
        unperm = onehot((n & 7) * ROWS + (n >> 3) == iota((COMP * ROWS, ROWS * 8), 0))
        out_ref[...] = pick_rows(unperm, pick(own, back)).reshape(COMP, ROWS, COLS)

    sent = list(copies)
    halo_finish(0, copies)
    sweep()
    copies = halo_start(1)
    sent += copies
    setup_rows()
    halo_finish(1, copies)
    sweep()
    copies = halo_start(2)
    sent += copies
    gather(0)
    first = a2a_1(0)
    sent += first
    halo_finish(2, copies)
    sweep()
    copies = halo_start(3)
    sent += copies
    second = a2a_2(0, first)
    sent += second
    halo_finish(3, copies)
    sweep()
    gather(1)
    first = a2a_1(1)
    sent += first
    place(0, second)
    second = a2a_2(1, first)
    sent += second
    write_adjoint()
    place(1, second)
    for c in sent:
        c.wait_send()


def on_device(
    G,
    S,
    adjoint_start,
    objective_grad,
    diagonal,
    connect,
    element_scale,
    element_matrix,
    traction_map,
    iface_node,
    iface_dest,
    iface_target,
    iface_count,
):
    vmem = pl.BlockSpec(memory_space=pltpu.VMEM)
    smem = pl.BlockSpec(memory_space=pltpu.SMEM)
    D = G * S
    XG = D // W
    dma = pltpu.SemaphoreType.DMA
    scratch = [
        pltpu.VMEM((13, 3, 8, LANES), F32),
        pltpu.VMEM((11, 3, 8, LANES), F32),
        pltpu.VMEM((4, 14, 8, LANES), F32),
        pltpu.VMEM((12, 3, 8, LANES), F32),
        pltpu.VMEM((12, 3, 8, LANES), F32),
        pltpu.VMEM((LANES, LANES), BF16),
        pltpu.VMEM((8, ELEMS), jnp.int32),
        dma,
        pltpu.VMEM((8, 384), jnp.int32),
        pltpu.VMEM((64, 384), F32),
        pltpu.VMEM((LANES, IF_CAP), BF16),
        pltpu.VMEM((D, IF_CAP), BF16),
        pltpu.VMEM((1, IF_CAP), F32),
        pltpu.VMEM((4, 2, 3, 8, LANES), F32),
        pltpu.VMEM((4, 2, 3, 8, LANES), F32),
        pltpu.VMEM((4, 2, 8, 128), F32),
        pltpu.VMEM((4, 2, 3, 8, 128), F32),
        pltpu.VMEM((ITERS, XG, 8, 128), F32),
        pltpu.VMEM((ITERS, D, 128), F32),
        pltpu.VMEM((ITERS, W, XG, 128), F32),
        pltpu.VMEM((ITERS, W, XG, 128), F32),
        dma((4, 8)),
        dma((4, 8)),
        dma((ITERS, XG - 1)),
        dma((ITERS, XG - 1)),
        dma((ITERS, W - 1)),
        dma((ITERS, W - 1)),
    ]
    call = pl.pallas_call(
        functools.partial(kernel, G, S),
        out_shape=(
            jax.ShapeDtypeStruct((COMP, ROWS, COLS), F32),
            jax.ShapeDtypeStruct((ITERS, 3, IF_CAP), F32),
        ),
        in_specs=[vmem, vmem, vmem, pl.BlockSpec(memory_space=pl.ANY), vmem, vmem, smem]
        + [vmem] * 3
        + [smem],
        out_specs=(vmem, vmem),
        scratch_shapes=scratch,
        compiler_params=pltpu.CompilerParams(
            collective_id=0, has_side_effects=True, vmem_limit_bytes=40 * 1024 * 1024
        ),
    )
    return call(
        adjoint_start,
        objective_grad,
        diagonal,
        connect,
        element_scale,
        element_matrix,
        traction_map,
        iface_node.reshape(1, IF_CAP),
        iface_dest.reshape(1, IF_CAP),
        iface_target.reshape(1, IF_CAP),
        iface_count,
    )


def solution(mesh):
    both = ("group", "sub")
    placed = (
        P(None, "group", "sub"),
        P(None, "group", "sub"),
        P("group", "sub"),
        P(None, both),
        P(None, both),
        P(),
        P(),
        P(both),
        P(both, None),
        P(both),
        P(both),
    )
    return jax.shard_map(
        functools.partial(on_device, mesh.shape["group"], mesh.shape["sub"]),
        mesh=mesh,
        in_specs=placed,
        out_specs=(P(None, "group", "sub"), P(None, None, both)),
        check_vma=False,
    )
```

```python
import functools
import jax
import jax.numpy as jnp
from jax import lax
from jax.experimental import pallas as pl
from jax.experimental.pallas import tpu as pltpu
from jax.sharding import PartitionSpec as P

COMP = 6
ROWS = 32
COLS = 384
ELEMS = 338
IF_CAP = 2048
CAP = 32
ITERS = 2
SWEEPS = 2
LANES = 512
UP, DOWN = 11, 10
O_UP, O_DOWN = 8, 7
STARTS = (
    [-11, -8, -5, -2, -1] + [min(3 * i, ROWS + 2) - 3 for i in range(13)] + [29, 32, 35, 38]
)
ACTIVE = [(0, 22), (1, 21), (2, 20), (4, 18)]
UPDATED = [(-8, 39), (-5, 36), (-3, 35), (0, 32)]
W = 8
F32 = jnp.float32
BF16 = jnp.bfloat16
MESH = pl.DeviceIdType.MESH
NT = (((1,), (1,)), ((), ()))


def iota(shape, dim):
    return lax.broadcasted_iota(jnp.int32, shape, dim)


def onehot(mask):
    return jnp.where(mask, 1.0, 0.0).astype(BF16)


def mm(a, b):
    return jnp.dot(a, b, preferred_element_type=F32)


def mm_nt(a, b):
    return lax.dot_general(a, b, NT, preferred_element_type=F32)


def pieces(x, n):
    out = []
    for k in range(n):
        p = x.astype(BF16)
        out.append(p)
        if k + 1 < n:
            x = x - p.astype(F32)
    return out


def total(terms):
    terms = list(terms)
    while len(terms) > 1:
        terms = [
            terms[i] + terms[i + 1] if i + 1 < len(terms) else terms[i]
            for i in range(0, len(terms), 2)
        ]
    return terms[0]


def pick(x, sel, n=3):
    return total([mm(p, sel) for p in pieces(x, n)])


def pick_rows(sel, x, n=3):
    return total([mm(sel, p) for p in pieces(x, n)])


def ext_col(lane):
    j = lane >> 4
    return jnp.where(j == 25, 374, 15 * j) + (lane & 15)


def owner(row):
    return 0 if row < 0 else (1 if row < ROWS else 2)


def block_of(e):
    return 0 if e < 5 else (1 if e < 18 else 2)


def kernel(
    G,
    S,
    adj_hbm,
    obj_hbm,
    diag_hbm,
    conn_hbm,
    scale_hbm,
    em_hbm,
    tm_hbm,
    node_hbm,
    dest_hbm,
    target_hbm,
    count_hbm,
    out_ref,
    load_ref,
    adj_ref,
    obj_ref,
    diag_ref,
    conn_ref,
    scale_ref,
    em_ref,
    tm_ref,
    node_ref,
    dest_ref,
    target_ref,
    count_ref,
    in_sem,
    state,
    oi,
    asm,
    scale_own,
    scale_up,
    scale_down,
    wmat,
    conn_pad,
    scale_pad,
    colhot,
    desthot,
    slot_s,
    side_send,
    side_recv,
    sscale_send,
    sscale_recv,
    abuf,
    r1,
    r1t,
    r3,
    halo_send,
    halo_recv,
    a1_send,
    a1_recv,
    a2_send,
    a2_recv,
):
    X = S // W
    D = G * S
    g = lax.axis_index("group")
    s = lax.axis_index("sub")
    x = s // W
    w = s % W

    def at(dg, ds):
        return (lax.rem(g + dg + G, G), lax.rem(s + ds + S, S))

    def at_gx(dg, dx):
        return (lax.rem(g + dg, G), lax.rem(x + dx, X) * W + w)

    def at_w(dw):
        return (g, x * W + lax.rem(w + dw, W))

    loads = [
        pltpu.make_async_copy(src, dst, in_sem.at[n])
        for n, (src, dst) in enumerate(
            [
                (adj_hbm, adj_ref),
                (diag_hbm, diag_ref),
                (obj_hbm, obj_ref),
                (conn_hbm.at[0:8], conn_ref),
                (scale_hbm, scale_ref),
                (em_hbm, em_ref),
                (tm_hbm, tm_ref),
                (node_hbm, node_ref),
                (dest_hbm, dest_ref),
                (target_hbm, target_ref),
                (count_hbm, count_ref),
            ]
        )
    ]
    for c in loads:
        c.start()
    gx_partners = [(dg, dx) for dg in range(G) for dx in range(X)][1:]
    barrier = pltpu.get_barrier_semaphore()
    targets = [at(0, -1), at(0, 1)]
    targets += [at_gx(*p) for p in gx_partners] + [at_w(dw) for dw in range(1, W)]
    for t in targets:
        pl.semaphore_signal(barrier, inc=1, device_id=t, device_id_type=MESH)

    lane = iota((COLS, LANES), 1)
    sel = onehot((ext_col(lane) == iota((COLS, LANES), 0) + 3) & (lane < 416))
    m = iota((ROWS * 8, COMP * ROWS), 0)
    perm = onehot(((m & 7) * ROWS + (m >> 3) == iota((ROWS * 8, COMP * ROWS), 1)) & ((m & 7) < COMP))
    loads[0].wait()
    first = pick_rows(perm, adj_ref[...].reshape(COMP * ROWS, COLS))
    state[UP : UP + ROWS] = pick(first, sel).reshape(ROWS, 8, LANES)

    loads[1].wait()
    loads[2].wait()
    inverse = 1.0 / diag_ref[...]
    scaled_obj = (obj_ref[...] * inverse[None]).reshape(COMP * ROWS, COLS)
    m = iota((ROWS * 8, ROWS), 0)
    perm_inv = onehot(((m & 7) == COMP) & ((m >> 3) == iota((ROWS * 8, ROWS), 1)))
    first = pick_rows(perm, scaled_obj) + pick_rows(perm_inv, inverse)
    oi[O_UP : O_UP + ROWS] = pick(first, sel).reshape(ROWS, 8, LANES)

    loads[3].wait()
    loads[4].wait()
    conn_pad[...] = jnp.full_like(conn_pad, -1)
    conn_pad[:, 0:ELEMS] = conn_ref[...]
    scale_pad[...] = jnp.zeros_like(scale_pad)
    scale_pad[:, 0:ELEMS] = scale_ref[...]
    node0 = conn_pad[0:1]
    row0 = lax.div(node0, jnp.int32(390))
    col0 = node0 - row0 * 390
    elem_i = jnp.where(node0 >= 0, lax.div(row0 + 2, jnp.int32(3)), -1)
    elem_j = jnp.where(node0 >= 0, lax.div(col0 + 14, jnp.int32(15)), -1)
    row_hot = onehot(elem_i == iota((16, 384), 0))
    start_row = jnp.minimum(3 * iota((16, LANES), 0), ROWS + 2)
    lane = iota((16, LANES), 1)
    off_side = ((s == 0) & (lane < 3)) | ((s == S - 1) & (lane >= 413))
    j_mask = elem_j[:, None, :] == iota((32, 16, 384), 0)
    for a in range(4):
        sc = scale_pad[16 * a : 16 * a + 16]
        out = []
        for p in pieces(sc, 3):
            p = jnp.where(j_mask, p.astype(F32)[None], 0.0).reshape(LANES, 384)
            out.append(mm_nt(row_hot, p.astype(BF16)))
        r = start_row + a
        off = ((g == 0) & (r < 3)) | ((g == G - 1) & (r >= ROWS + 3)) | off_side
        scale_own[a] = jnp.where(off, 0.0, total(out))

    def remote(n, src, dst, dev):
        return pltpu.make_async_remote_copy(
            src_ref=src,
            dst_ref=dst,
            send_sem=halo_send.at[n],
            recv_sem=halo_recv.at[n],
            device_id=dev,
            device_id_type=MESH,
        )

    def turn(v, n):
        return pltpu.roll(v, n % 128, v.ndim - 1)

    def pack_right(two, three, start):
        lane = iota(two.shape, two.ndim - 1)
        return jnp.where(lane < start + 16, turn(two, start - 112), turn(three, start + 16))

    for p in range(0, ROWS, 8):
        st = [state[UP + p : UP + p + 8, :, 128 * q : 128 * q + 128] for q in (0, 2, 3)]
        ob = [oi[O_UP + p : O_UP + p + 8, :, 128 * q : 128 * q + 128] for q in (0, 2, 3)]
        lane = iota((8, 8, 128), 2)
        side_send[0, p : p + 8] = jnp.where(lane < 80, turn(st[0], 32), turn(ob[0], 80))
        side_send[1, p : p + 8] = jnp.where(
            lane < 80, pack_right(ob[1], ob[2], 32), pack_right(st[1], st[2], 80)
        )
    for a in range(4):
        sscale_send[0, a] = turn(scale_own[a, :, 0:128], 32)
        sscale_send[1, a] = pack_right(scale_own[a, :, 256:384], scale_own[a, :, 384:512], 80)

    def row_copies(n, cols):
        up, down = at(-1, 0), at(1, 0)
        return [
            remote(n, state.at[UP + ROWS - UP : UP + ROWS, :, cols], state.at[0:UP, :, cols], down),
            remote(
                n + 1,
                state.at[UP : UP + DOWN, :, cols],
                state.at[UP + ROWS : UP + ROWS + DOWN, :, cols],
                up,
            ),
            remote(n + 2, oi.at[ROWS : O_UP + ROWS, :, cols], oi.at[0:O_UP, :, cols], down),
            remote(
                n + 3,
                oi.at[O_UP : O_UP + O_DOWN, :, cols],
                oi.at[O_UP + ROWS : O_UP + ROWS + O_DOWN, :, cols],
                up,
            ),
            remote(n + 4, scale_own.at[:, 8:16, cols], scale_up.at[:, :, cols], down),
            remote(n + 5, scale_own.at[:, 0:8, cols], scale_down.at[:, :, cols], up),
        ]

    pl.semaphore_wait(barrier, len(targets))
    side_copies = [
        remote(0, side_send.at[0], side_recv.at[0], at(0, -1)),
        remote(1, side_send.at[1], side_recv.at[1], at(0, 1)),
        remote(2, sscale_send.at[0], sscale_recv.at[0], at(0, -1)),
        remote(3, sscale_send.at[1], sscale_recv.at[1], at(0, 1)),
    ]
    for c in side_copies:
        c.start()
    row_early = row_copies(4, slice(0, 384))
    for c in row_early:
        c.start()

    loads[5].wait()
    r = iota((LANES, 64), 0)
    e_hot = onehot((r >> 7) * 16 + (r & 15) == iota((LANES, 64), 1))
    left = mm(e_hot, em_ref[...]).astype(BF16)
    rr, cc = iota((LANES, LANES), 0), iota((LANES, LANES), 1)
    wide = mm_nt(left, e_hot)
    wmat[...] = jnp.where(((rr >> 4) & 7) == ((cc >> 4) & 7), wide, 0.0).astype(BF16)

    def sides_finish():
        for c in side_copies:
            c.wait_recv()
        for p in range(0, ROWS, 8):
            lane = iota((8, 8, 128), 2)
            right, left = side_recv[0, p : p + 8], side_recv[1, p : p + 8]
            own = state[UP + p : UP + p + 8, :, 384:512]
            state[UP + p : UP + p + 8, :, 384:512] = jnp.where(
                lane < 32, own, jnp.where(lane < 80, right, left)
            )
            own = oi[O_UP + p : O_UP + p + 8, :, 384:512]
            both = jnp.where(lane < 80, left, right)
            oi[O_UP + p : O_UP + p + 8, :, 384:512] = jnp.where(
                lane < 32, own, jnp.where(lane < 80, turn(both, -48), turn(both, 48))
            )
        lane = iota((16, 128), 1)
        for a in range(4):
            scale_own[a, :, 384:512] = jnp.where(
                lane < 32,
                scale_own[a, :, 384:512],
                jnp.where(lane < 80, sscale_recv[0, a], sscale_recv[1, a]),
            )

    def fill(first, three):
        lane = iota(first.shape, first.ndim - 1)
        ahead = turn(three, 6)
        first_new = jnp.where(lane < 3, ahead, first)
        three_new = jnp.where((lane >= 32) & (lane < 35), ahead, three)
        three_new = jnp.where((lane >= 29) & (lane < 32), turn(three, -6), three_new)
        three_new = jnp.where(lane >= 125, turn(first, -6), three_new)
        return first_new, three_new

    def fill_rows(lo, hi):
        lo, hi = UP + lo, UP + hi
        state[lo:hi, :, 0:128], state[lo:hi, :, 384:512] = fill(
            state[lo:hi, :, 0:128], state[lo:hi, :, 384:512]
        )

    def scale_row(a, e, cols):
        if e < 5:
            v = scale_up[a, e : e + 1, cols]
        elif e < 18:
            v = scale_own[a, e - 5 : e - 4, cols]
        else:
            v = scale_down[a, e - 18 : e - 17, cols]
        return jnp.broadcast_to(v, (8, 128))

    def sweep(t):
        lo, hi = ACTIVE[t]
        rows = range(*UPDATED[t])
        count = hi - lo
        for q in range(4):
            cols = slice(128 * q, 128 * q + 128)
            parts = []
            for a in range(4):
                v = [
                    state[UP + STARTS[e] + a, :, cols] * scale_row(a, e, cols)
                    for e in range(lo, hi)
                ]
                parts.append(jnp.concatenate(v, axis=0).astype(BF16))
            o = mm(jnp.concatenate(parts, axis=1), wmat[...])
            for row in rows:
                terms = [
                    o[8 * (e - lo) : 8 * (e - lo) + 8, 128 * a : 128 * a + 128]
                    for e in range(lo, hi)
                    for a in range(4)
                    if STARTS[e] + a == row and block_of(e) == owner(row)
                ]
                asm[O_UP + row, :, cols] = total(terms)
        step = 4
        for r0 in range(UPDATED[t][0], UPDATED[t][1], step):
            n = min(step, UPDATED[t][1] - r0)
            lane = iota((n, 8, 128), 2)
            low = lane & 15
            a0 = O_UP + r0
            tiles = [asm[a0 : a0 + n, :, 128 * q : 128 * q + 128] for q in range(4)]
            ahead = [turn(v, 1) for v in tiles]
            back = [turn(v, -1) for v in tiles]
            new = []
            for q in range(4):
                before = jnp.where(lane == 0, ahead[(q + 3) % 4], ahead[q])
                after = jnp.where(lane == 127, back[(q + 1) % 4], back[q])
                more = jnp.where(low == 0, before, jnp.where(low == 15, after, 0.0))
                if q == 3:
                    pair = jnp.where(lane >= 96, lane - 96, lane)
                    more = jnp.where((pair == 14) | (pair == 15), turn(tiles[3], -2), more)
                    more = jnp.where((pair == 16) | (pair == 17), turn(tiles[3], 2), more)
                cols = slice(128 * q, 128 * q + 128)
                rhs = oi[a0 : a0 + n, :, cols]
                inv = jnp.broadcast_to(oi[a0 : a0 + n, COMP : COMP + 1, cols], (n, 8, 128))
                new.append(rhs - (tiles[q] + more) * inv)
            if t < 3:
                new[0], new[3] = fill(new[0], new[3])
            for q in range(4):
                state[UP + r0 : UP + r0 + n, :, 128 * q : 128 * q + 128] = new[q]

    CH = 512
    for c in loads[6:]:
        c.wait()
    node = node_ref[...]
    node_row = lax.div(node, jnp.int32(COLS))
    e_col = node - node_row * COLS + 3
    e_lane = jnp.where(e_col < 375, e_col + lax.div(e_col, jnp.int32(15)), e_col + 26)

    def setup_rows():
        live = iota((1, IF_CAP), 1) < count_ref[...]
        dest = jnp.where(live, dest_ref[...], -1)
        tri = onehot(iota((256, 256), 0) < iota((256, 256), 1))
        carry = jnp.zeros((D, 1), F32)
        for b in range(IF_CAP // 256):
            cols = slice(256 * b, 256 * b + 256)
            hot = jnp.where(dest[:, cols] == iota((D, 256), 0), 1.0, 0.0)
            desthot[:, cols] = hot.astype(BF16)
            before = mm(hot.astype(BF16), tri) + carry
            slot_s[:, cols] = jnp.sum(before * hot, axis=0, keepdims=True)
            carry = carry + jnp.sum(hot, axis=1, keepdims=True)
        for b in range(IF_CAP // CH):
            cols = slice(CH * b, CH * b + CH)
            colhot[:, cols] = onehot(e_lane[:, cols] == iota((LANES, CH), 0))

    def gather(t):
        lane = iota((1, 256), 1)
        trac = []
        for k in range(3):
            row = jnp.zeros((1, 256), F32)
            for c in range(COMP):
                row = jnp.where((lane & 7) == c, tm_ref[k : k + 1, c : c + 1], row)
            trac.append(jnp.where((iota((32, 256), 1) >> 3) == iota((32, 256), 0), row, 0.0))
        trac = jnp.concatenate(trac, axis=0)
        own = state[UP : UP + ROWS].reshape(ROWS * 8, LANES)
        field = jnp.dot(trac, own, precision=lax.Precision.HIGHEST, preferred_element_type=F32)
        field = jnp.concatenate(pieces(field, 2), axis=0)
        acc = jnp.zeros((D, 128), F32)
        for b in range(IF_CAP // CH):
            cols = slice(CH * b, CH * b + CH)
            v = mm(field, colhot[:, cols])
            v = (v[:96] + v[96:]).reshape(3, 32, CH)
            v = jnp.where(node_row[:, cols][None] == iota((3, 32, CH), 1), v, 0.0)
            v = jnp.sum(v, axis=1, keepdims=True)
            v = jnp.concatenate([v, target_ref[:, cols].astype(F32)[None]], axis=0)
            slots = slot_s[:, cols].astype(jnp.int32)[None] == iota((4, CAP, CH), 1)
            v = jnp.where(slots, v, 0.0).reshape(4 * CAP, CH)
            for p in pieces(v, 2):
                acc = acc + mm_nt(desthot[:, cols], p)
        abuf[t] = acc.reshape(D // 8, 8, 128)

    def a2a_1(t):
        copies = []
        for o, (dg, dx) in enumerate(gx_partners):
            to_g, to_s = at_gx(dg, dx)
            copies.append(
                pltpu.make_async_remote_copy(
                    src_ref=abuf.at[t, to_g * X + to_s // W],
                    dst_ref=r1.at[t, pl.ds(8 * (o + 1), 8)],
                    send_sem=a1_send.at[t, o],
                    recv_sem=a1_recv.at[t, o],
                    device_id=(to_g, to_s),
                    device_id_type=MESH,
                )
            )
            copies[-1].start()
        r1[t, 0:8] = abuf[t, g * X + x]
        return copies

    def a2a_2(t, first):
        for c in first:
            c.wait_recv()
        for d in range(W):
            r1t[t, d] = r1[t, pl.ds(d, D // W, stride=W), :]
        copies = []
        for dw in range(1, W):
            to = at_w(dw)
            copies.append(
                pltpu.make_async_remote_copy(
                    src_ref=r1t.at[t, lax.rem(w + dw, W)],
                    dst_ref=r3.at[t, dw],
                    send_sem=a2_send.at[t, dw - 1],
                    recv_sem=a2_recv.at[t, dw - 1],
                    device_id=to,
                    device_id_type=MESH,
                )
            )
            copies[-1].start()
        r3[t, 0] = r1t[t, w]
        return copies

    def place(t, second):
        for c in second:
            c.wait_recv()
        got = r3[t].reshape(D, 128).T
        name = got[96:128]
        high = jnp.floor(name * (1.0 / 128.0))
        low = name - 128.0 * high
        acc = jnp.zeros((96, 128), F32)
        for q in range(CAP // 4):
            left, right = [], []
            for z in range(4 * q, 4 * q + 4):
                right.append(onehot(low[z : z + 1] == iota((128, D), 0).astype(F32)))
                hit = high[z : z + 1] == iota((16, D), 0).astype(F32)
                v = jnp.concatenate(
                    [jnp.where(hit, got[32 * k + z : 32 * k + z + 1], 0.0) for k in range(3)], axis=0
                )
                left.append(jnp.concatenate(pieces(v, 2), axis=0))
            acc = acc + mm_nt(jnp.concatenate(left, axis=1), jnp.concatenate(right, axis=1))
        acc = acc[:48] + acc[48:]
        for k in range(3):
            for h in range(16):
                load_ref[t, k : k + 1, 128 * h : 128 * h + 128] = acc[16 * k + h : 16 * k + h + 1]

    def write_adjoint():
        own = state[UP : UP + ROWS].reshape(ROWS * 8, LANES)
        lane = iota((LANES, COLS), 0)
        j, b = lane >> 4, lane & 15
        keep = ((j < 25) & (b < 15)) | ((j == 25) & (b > 0))
        back = onehot(keep & (ext_col(lane) == iota((LANES, COLS), 1) + 3))
        n = iota((COMP * ROWS, ROWS * 8), 1)
        unperm = onehot((n & 7) * ROWS + (n >> 3) == iota((COMP * ROWS, ROWS * 8), 0))
        out_ref[...] = pick_rows(unperm, pick(own, back)).reshape(COMP, ROWS, COLS)

    setup_rows()
    sides_finish()
    row_late = row_copies(10, slice(384, 512))
    for c in row_late:
        c.start()
    fill_rows(UP, ROWS - DOWN - 1)
    for c in row_early + row_late:
        c.wait_recv()
    for c in row_late + row_early:
        c.wait_send()
    fill_rows(-UP, UP)
    fill_rows(ROWS - DOWN - 1, ROWS + DOWN)
    sweep(0)
    sweep(1)
    gather(0)
    first = a2a_1(0)
    sent = side_copies + first
    sweep(2)
    second = a2a_2(0, first)
    sent += second
    sweep(3)
    gather(1)
    first = a2a_1(1)
    sent += first
    place(0, second)
    second = a2a_2(1, first)
    sent += second
    write_adjoint()
    place(1, second)
    for c in sent:
        c.wait_send()


def on_device(
    G,
    S,
    adjoint_start,
    objective_grad,
    diagonal,
    connect,
    element_scale,
    element_matrix,
    traction_map,
    iface_node,
    iface_dest,
    iface_target,
    iface_count,
):
    vmem = pl.BlockSpec(memory_space=pltpu.VMEM)
    D = G * S
    XG = D // W
    dma = pltpu.SemaphoreType.DMA
    I32 = jnp.int32
    scratch = [
        pltpu.VMEM((COMP, ROWS, COLS), F32),
        pltpu.VMEM((COMP, ROWS, COLS), F32),
        pltpu.VMEM((ROWS, COLS), F32),
        pltpu.VMEM((8, ELEMS), I32),
        pltpu.VMEM((64, ELEMS), F32),
        pltpu.VMEM((64, 64), BF16),
        pltpu.VMEM((3, COMP), F32),
        pltpu.VMEM((1, IF_CAP), I32),
        pltpu.VMEM((1, IF_CAP), I32),
        pltpu.VMEM((1, IF_CAP), I32),
        pltpu.VMEM((1, 1), I32),
        dma((11,)),
        pltpu.VMEM((UP + ROWS + DOWN, 8, LANES), F32),
        pltpu.VMEM((O_UP + ROWS + O_DOWN, 8, LANES), F32),
        pltpu.VMEM((O_UP + ROWS + O_DOWN, 8, LANES), F32),
        pltpu.VMEM((4, 16, LANES), F32),
        pltpu.VMEM((4, 8, LANES), F32),
        pltpu.VMEM((4, 8, LANES), F32),
        pltpu.VMEM((LANES, LANES), BF16),
        pltpu.VMEM((8, 384), I32),
        pltpu.VMEM((64, 384), F32),
        pltpu.VMEM((LANES, IF_CAP), BF16),
        pltpu.VMEM((D, IF_CAP), BF16),
        pltpu.VMEM((1, IF_CAP), F32),
        pltpu.VMEM((2, ROWS, 8, 128), F32),
        pltpu.VMEM((2, ROWS, 8, 128), F32),
        pltpu.VMEM((2, 4, 16, 128), F32),
        pltpu.VMEM((2, 4, 16, 128), F32),
        pltpu.VMEM((ITERS, XG, 8, 128), F32),
        pltpu.VMEM((ITERS, D, 128), F32),
        pltpu.VMEM((ITERS, W, XG, 128), F32),
        pltpu.VMEM((ITERS, W, XG, 128), F32),
        dma((16,)),
        dma((16,)),
        dma((ITERS, XG - 1)),
        dma((ITERS, XG - 1)),
        dma((ITERS, W - 1)),
        dma((ITERS, W - 1)),
    ]
    call = pl.pallas_call(
        functools.partial(kernel, G, S),
        out_shape=(
            jax.ShapeDtypeStruct((COMP, ROWS, COLS), F32),
            jax.ShapeDtypeStruct((ITERS, 3, IF_CAP), F32),
        ),
        in_specs=[pl.BlockSpec(memory_space=pl.ANY)] * 11,
        out_specs=(vmem, vmem),
        scratch_shapes=scratch,
        compiler_params=pltpu.CompilerParams(
            collective_id=0, has_side_effects=True, vmem_limit_bytes=48 * 1024 * 1024
        ),
    )
    return call(
        adjoint_start,
        objective_grad,
        diagonal,
        connect,
        element_scale,
        element_matrix,
        traction_map,
        iface_node.reshape(1, IF_CAP),
        iface_dest.reshape(1, IF_CAP),
        iface_target.reshape(1, IF_CAP),
        iface_count.reshape(1, 1),
    )


def solution(mesh):
    both = ("group", "sub")
    placed = (
        P(None, "group", "sub"),
        P(None, "group", "sub"),
        P("group", "sub"),
        P(None, both),
        P(None, both),
        P(),
        P(),
        P(both),
        P(both, None),
        P(both),
        P(both),
    )
    return jax.shard_map(
        functools.partial(on_device, mesh.shape["group"], mesh.shape["sub"]),
        mesh=mesh,
        in_specs=placed,
        out_specs=(P(None, "group", "sub"), P(None, None, both)),
        check_vma=False,
    )
```

```python
import functools
import jax
import jax.numpy as jnp
from jax import lax
from jax.experimental import pallas as pl
from jax.experimental.pallas import tpu as pltpu
from jax.sharding import PartitionSpec as P

COMP = 6
ROWS = 32
COLS = 384
ELEMS = 338
IF_CAP = 2048
CAP = 32
ITERS = 2
SWEEPS = 2
LANES = 512
UP, DOWN = 11, 10
O_UP, O_DOWN = 8, 7
STARTS = (
    [-11, -8, -5, -2, -1] + [min(3 * i, ROWS + 2) - 3 for i in range(13)] + [29, 32, 35, 38]
)
ACTIVE = [(0, 22), (1, 21), (2, 20), (4, 18)]
UPDATED = [(-8, 39), (-5, 36), (-3, 35), (0, 32)]
W = 8
F32 = jnp.float32
BF16 = jnp.bfloat16
MESH = pl.DeviceIdType.MESH
NT = (((1,), (1,)), ((), ()))


def iota(shape, dim):
    return lax.broadcasted_iota(jnp.int32, shape, dim)


def onehot(mask):
    return jnp.where(mask, 1.0, 0.0).astype(BF16)


def mm(a, b):
    return jnp.dot(a, b, preferred_element_type=F32)


def mm_nt(a, b):
    return lax.dot_general(a, b, NT, preferred_element_type=F32)


def pieces(x, n):
    out = []
    for k in range(n):
        p = x.astype(BF16)
        out.append(p)
        if k + 1 < n:
            x = x - p.astype(F32)
    return out


def total(terms):
    terms = list(terms)
    while len(terms) > 1:
        terms = [
            terms[i] + terms[i + 1] if i + 1 < len(terms) else terms[i]
            for i in range(0, len(terms), 2)
        ]
    return terms[0]


def pick(x, sel, n=3):
    return total([mm(p, sel) for p in pieces(x, n)])


def pick_rows(sel, x, n=3):
    return total([mm(sel, p) for p in pieces(x, n)])


def ext_col(lane):
    j = lane >> 4
    return jnp.where(j == 25, 374, 15 * j) + (lane & 15)


def owner(row):
    return 0 if row < 0 else (1 if row < ROWS else 2)


def block_of(e):
    return 0 if e < 5 else (1 if e < 18 else 2)


def kernel(
    G,
    S,
    adj_hbm,
    obj_hbm,
    diag_hbm,
    conn_hbm,
    scale_hbm,
    em_hbm,
    tm_hbm,
    node_hbm,
    dest_hbm,
    target_hbm,
    count_hbm,
    out_ref,
    load_ref,
    adj_ref,
    obj_ref,
    diag_ref,
    conn_ref,
    scale_ref,
    em_ref,
    tm_ref,
    node_ref,
    dest_ref,
    target_ref,
    count_ref,
    in_sem,
    state,
    oi,
    asm,
    scale_own,
    scale_up,
    scale_down,
    wmat,
    conn_pad,
    scale_pad,
    colhot,
    desthot,
    slot_s,
    side_send,
    side_recv,
    sscale_send,
    sscale_recv,
    abuf,
    r1,
    r1t,
    r3,
    halo_send,
    halo_recv,
    a1_send,
    a1_recv,
    a2_send,
    a2_recv,
):
    X = S // W
    D = G * S
    g = lax.axis_index("group")
    s = lax.axis_index("sub")
    x = s // W
    w = s % W

    def at(dg, ds):
        return (lax.rem(g + dg + G, G), lax.rem(s + ds + S, S))

    def at_gx(dg, dx):
        return (lax.rem(g + dg, G), lax.rem(x + dx, X) * W + w)

    def at_w(dw):
        return (g, x * W + lax.rem(w + dw, W))

    loads = [
        pltpu.make_async_copy(src, dst, in_sem.at[n])
        for n, (src, dst) in enumerate(
            [
                (adj_hbm, adj_ref),
                (diag_hbm, diag_ref),
                (obj_hbm, obj_ref),
                (conn_hbm.at[0:8], conn_ref),
                (scale_hbm, scale_ref),
                (em_hbm, em_ref),
                (tm_hbm, tm_ref),
                (node_hbm, node_ref),
                (dest_hbm, dest_ref),
                (target_hbm, target_ref),
                (count_hbm, count_ref),
            ]
        )
    ]
    for c in loads:
        c.start()
    gx_partners = [(dg, dx) for dg in range(G) for dx in range(X)][1:]
    barrier = pltpu.get_barrier_semaphore()
    targets = [at(0, -1), at(0, 1)]
    targets += [at_gx(*p) for p in gx_partners] + [at_w(dw) for dw in range(1, W)]
    for t in targets:
        pl.semaphore_signal(barrier, inc=1, device_id=t, device_id_type=MESH)

    lane = iota((COLS, LANES), 1)
    sel = onehot((ext_col(lane) == iota((COLS, LANES), 0) + 3) & (lane < 416))
    m = iota((ROWS * 8, COMP * ROWS), 0)
    perm = onehot(((m & 7) * ROWS + (m >> 3) == iota((ROWS * 8, COMP * ROWS), 1)) & ((m & 7) < COMP))
    loads[0].wait()
    first = pick_rows(perm, adj_ref[...].reshape(COMP * ROWS, COLS))
    state[UP : UP + ROWS] = pick(first, sel).reshape(ROWS, 8, LANES)

    loads[1].wait()
    loads[2].wait()
    inverse = 1.0 / diag_ref[...]
    scaled_obj = (obj_ref[...] * inverse[None]).reshape(COMP * ROWS, COLS)
    m = iota((ROWS * 8, ROWS), 0)
    perm_inv = onehot(((m & 7) == COMP) & ((m >> 3) == iota((ROWS * 8, ROWS), 1)))
    first = pick_rows(perm, scaled_obj) + pick_rows(perm_inv, inverse)
    oi[O_UP : O_UP + ROWS] = pick(first, sel).reshape(ROWS, 8, LANES)

    def remote(n, src, dst, dev):
        return pltpu.make_async_remote_copy(
            src_ref=src,
            dst_ref=dst,
            send_sem=halo_send.at[n],
            recv_sem=halo_recv.at[n],
            device_id=dev,
            device_id_type=MESH,
        )

    def turn(v, n):
        return pltpu.roll(v, n % 128, v.ndim - 1)

    def pack_right(two, three, start):
        lane = iota(two.shape, two.ndim - 1)
        return jnp.where(lane < start + 16, turn(two, start - 112), turn(three, start + 16))

    for p in range(0, ROWS, 8):
        st = [state[UP + p : UP + p + 8, :, 128 * q : 128 * q + 128] for q in (0, 2, 3)]
        ob = [oi[O_UP + p : O_UP + p + 8, :, 128 * q : 128 * q + 128] for q in (0, 2, 3)]
        lane = iota((8, 8, 128), 2)
        side_send[0, p : p + 8] = jnp.where(lane < 80, turn(st[0], 32), turn(ob[0], 80))
        side_send[1, p : p + 8] = jnp.where(
            lane < 80, pack_right(ob[1], ob[2], 32), pack_right(st[1], st[2], 80)
        )
    def row_copies(n, cols):
        up, down = at(-1, 0), at(1, 0)
        return [
            remote(n, state.at[UP + ROWS - UP : UP + ROWS, :, cols], state.at[0:UP, :, cols], down),
            remote(
                n + 1,
                state.at[UP : UP + DOWN, :, cols],
                state.at[UP + ROWS : UP + ROWS + DOWN, :, cols],
                up,
            ),
            remote(n + 2, oi.at[ROWS : O_UP + ROWS, :, cols], oi.at[0:O_UP, :, cols], down),
            remote(
                n + 3,
                oi.at[O_UP : O_UP + O_DOWN, :, cols],
                oi.at[O_UP + ROWS : O_UP + ROWS + O_DOWN, :, cols],
                up,
            ),
            remote(n + 4, scale_own.at[:, 8:16, cols], scale_up.at[:, :, cols], down),
            remote(n + 5, scale_own.at[:, 0:8, cols], scale_down.at[:, :, cols], up),
        ]

    pl.semaphore_wait(barrier, len(targets))
    side_copies = [
        remote(0, side_send.at[0], side_recv.at[0], at(0, -1)),
        remote(1, side_send.at[1], side_recv.at[1], at(0, 1)),
        remote(2, sscale_send.at[0], sscale_recv.at[0], at(0, -1)),
        remote(3, sscale_send.at[1], sscale_recv.at[1], at(0, 1)),
    ]
    row_early = row_copies(4, slice(0, 384))
    for c in side_copies[:2] + row_early[:4]:
        c.start()

    loads[3].wait()
    loads[4].wait()
    conn_pad[...] = jnp.full_like(conn_pad, -1)
    conn_pad[:, 0:ELEMS] = conn_ref[...]
    scale_pad[...] = jnp.zeros_like(scale_pad)
    scale_pad[:, 0:ELEMS] = scale_ref[...]
    node0 = conn_pad[0:1]
    row0 = lax.div(node0, jnp.int32(390))
    col0 = node0 - row0 * 390
    elem_i = jnp.where(node0 >= 0, lax.div(row0 + 2, jnp.int32(3)), -1)
    elem_j = jnp.where(node0 >= 0, lax.div(col0 + 14, jnp.int32(15)), -1)
    row_hot = onehot(elem_i == iota((16, 384), 0))
    start_row = jnp.minimum(3 * iota((16, LANES), 0), ROWS + 2)
    lane = iota((16, LANES), 1)
    off_side = ((s == 0) & (lane < 3)) | ((s == S - 1) & (lane >= 413))
    j_mask = elem_j[:, None, :] == iota((32, 16, 384), 0)
    for a in range(4):
        sc = scale_pad[16 * a : 16 * a + 16]
        out = []
        for p in pieces(sc, 3):
            p = jnp.where(j_mask, p.astype(F32)[None], 0.0).reshape(LANES, 384)
            out.append(mm_nt(row_hot, p.astype(BF16)))
        r = start_row + a
        off = ((g == 0) & (r < 3)) | ((g == G - 1) & (r >= ROWS + 3)) | off_side
        scale_own[a] = jnp.where(off, 0.0, total(out))
    for a in range(4):
        sscale_send[0, a] = turn(scale_own[a, :, 0:128], 32)
        sscale_send[1, a] = pack_right(scale_own[a, :, 256:384], scale_own[a, :, 384:512], 80)
    for c in side_copies[2:] + row_early[4:]:
        c.start()

    loads[5].wait()
    r = iota((LANES, 64), 0)
    e_hot = onehot((r >> 7) * 16 + (r & 15) == iota((LANES, 64), 1))
    left = mm(e_hot, em_ref[...]).astype(BF16)
    rr, cc = iota((LANES, LANES), 0), iota((LANES, LANES), 1)
    wide = mm_nt(left, e_hot)
    wmat[...] = jnp.where(((rr >> 4) & 7) == ((cc >> 4) & 7), wide, 0.0).astype(BF16)

    def sides_finish():
        for c in side_copies:
            c.wait_recv()
        for p in range(0, ROWS, 8):
            lane = iota((8, 8, 128), 2)
            right, left = side_recv[0, p : p + 8], side_recv[1, p : p + 8]
            own = state[UP + p : UP + p + 8, :, 384:512]
            state[UP + p : UP + p + 8, :, 384:512] = jnp.where(
                lane < 32, own, jnp.where(lane < 80, right, left)
            )
            own = oi[O_UP + p : O_UP + p + 8, :, 384:512]
            both = jnp.where(lane < 80, left, right)
            oi[O_UP + p : O_UP + p + 8, :, 384:512] = jnp.where(
                lane < 32, own, jnp.where(lane < 80, turn(both, -48), turn(both, 48))
            )
        lane = iota((16, 128), 1)
        for a in range(4):
            scale_own[a, :, 384:512] = jnp.where(
                lane < 32,
                scale_own[a, :, 384:512],
                jnp.where(lane < 80, sscale_recv[0, a], sscale_recv[1, a]),
            )

    def fill(first, three):
        lane = iota(first.shape, first.ndim - 1)
        ahead = turn(three, 6)
        first_new = jnp.where(lane < 3, ahead, first)
        three_new = jnp.where((lane >= 32) & (lane < 35), ahead, three)
        three_new = jnp.where((lane >= 29) & (lane < 32), turn(three, -6), three_new)
        three_new = jnp.where(lane >= 125, turn(first, -6), three_new)
        return first_new, three_new

    def fill_rows(lo, hi):
        lo, hi = UP + lo, UP + hi
        state[lo:hi, :, 0:128], state[lo:hi, :, 384:512] = fill(
            state[lo:hi, :, 0:128], state[lo:hi, :, 384:512]
        )

    def scale_row(a, e, cols):
        if e < 5:
            v = scale_up[a, e : e + 1, cols]
        elif e < 18:
            v = scale_own[a, e - 5 : e - 4, cols]
        else:
            v = scale_down[a, e - 18 : e - 17, cols]
        return jnp.broadcast_to(v, (8, 128))

    def sweep(t):
        lo, hi = ACTIVE[t]
        rows = range(*UPDATED[t])
        count = hi - lo
        for q in range(4):
            cols = slice(128 * q, 128 * q + 128)
            parts = []
            for a in range(4):
                v = [
                    state[UP + STARTS[e] + a, :, cols] * scale_row(a, e, cols)
                    for e in range(lo, hi)
                ]
                parts.append(jnp.concatenate(v, axis=0).astype(BF16))
            o = mm(jnp.concatenate(parts, axis=1), wmat[...])
            for row in rows:
                terms = [
                    o[8 * (e - lo) : 8 * (e - lo) + 8, 128 * a : 128 * a + 128]
                    for e in range(lo, hi)
                    for a in range(4)
                    if STARTS[e] + a == row and block_of(e) == owner(row)
                ]
                asm[O_UP + row, :, cols] = total(terms)
        step = 4
        for r0 in range(UPDATED[t][0], UPDATED[t][1], step):
            n = min(step, UPDATED[t][1] - r0)
            lane = iota((n, 8, 128), 2)
            low = lane & 15
            a0 = O_UP + r0
            tiles = [asm[a0 : a0 + n, :, 128 * q : 128 * q + 128] for q in range(4)]
            ahead = [turn(v, 1) for v in tiles]
            back = [turn(v, -1) for v in tiles]
            new = []
            for q in range(4):
                before = jnp.where(lane == 0, ahead[(q + 3) % 4], ahead[q])
                after = jnp.where(lane == 127, back[(q + 1) % 4], back[q])
                more = jnp.where(low == 0, before, jnp.where(low == 15, after, 0.0))
                if q == 3:
                    pair = jnp.where(lane >= 96, lane - 96, lane)
                    more = jnp.where((pair == 14) | (pair == 15), turn(tiles[3], -2), more)
                    more = jnp.where((pair == 16) | (pair == 17), turn(tiles[3], 2), more)
                cols = slice(128 * q, 128 * q + 128)
                rhs = oi[a0 : a0 + n, :, cols]
                inv = jnp.broadcast_to(oi[a0 : a0 + n, COMP : COMP + 1, cols], (n, 8, 128))
                new.append(rhs - (tiles[q] + more) * inv)
            if t < 3:
                new[0], new[3] = fill(new[0], new[3])
            for q in range(4):
                state[UP + r0 : UP + r0 + n, :, 128 * q : 128 * q + 128] = new[q]

    CH = 512
    for c in loads[6:]:
        c.wait()
    node = node_ref[...]
    node_row = lax.div(node, jnp.int32(COLS))
    e_col = node - node_row * COLS + 3
    e_lane = jnp.where(e_col < 375, e_col + lax.div(e_col, jnp.int32(15)), e_col + 26)

    def setup_rows():
        live = iota((1, IF_CAP), 1) < count_ref[...]
        dest = jnp.where(live, dest_ref[...], -1)
        tri = onehot(iota((256, 256), 0) < iota((256, 256), 1))
        carry = jnp.zeros((D, 1), F32)
        for b in range(IF_CAP // 256):
            cols = slice(256 * b, 256 * b + 256)
            hot = jnp.where(dest[:, cols] == iota((D, 256), 0), 1.0, 0.0)
            desthot[:, cols] = hot.astype(BF16)
            before = mm(hot.astype(BF16), tri) + carry
            slot_s[:, cols] = jnp.sum(before * hot, axis=0, keepdims=True)
            carry = carry + jnp.sum(hot, axis=1, keepdims=True)
        for b in range(IF_CAP // CH):
            cols = slice(CH * b, CH * b + CH)
            colhot[:, cols] = onehot(e_lane[:, cols] == iota((LANES, CH), 0))

    def gather(t):
        lane = iota((1, 256), 1)
        trac = []
        for k in range(3):
            row = jnp.zeros((1, 256), F32)
            for c in range(COMP):
                row = jnp.where((lane & 7) == c, tm_ref[k : k + 1, c : c + 1], row)
            trac.append(jnp.where((iota((32, 256), 1) >> 3) == iota((32, 256), 0), row, 0.0))
        trac = jnp.concatenate(trac, axis=0)
        own = state[UP : UP + ROWS].reshape(ROWS * 8, LANES)
        field = jnp.dot(trac, own, precision=lax.Precision.HIGHEST, preferred_element_type=F32)
        field = jnp.concatenate(pieces(field, 2), axis=0)
        acc = jnp.zeros((D, 128), F32)
        for b in range(IF_CAP // CH):
            cols = slice(CH * b, CH * b + CH)
            v = mm(field, colhot[:, cols])
            v = (v[:96] + v[96:]).reshape(3, 32, CH)
            v = jnp.where(node_row[:, cols][None] == iota((3, 32, CH), 1), v, 0.0)
            v = jnp.sum(v, axis=1, keepdims=True)
            v = jnp.concatenate([v, target_ref[:, cols].astype(F32)[None]], axis=0)
            slots = slot_s[:, cols].astype(jnp.int32)[None] == iota((4, CAP, CH), 1)
            v = jnp.where(slots, v, 0.0).reshape(4 * CAP, CH)
            for p in pieces(v, 2):
                acc = acc + mm_nt(desthot[:, cols], p)
        abuf[t] = acc.reshape(D // 8, 8, 128)

    def a2a_1(t):
        copies = []
        for o, (dg, dx) in enumerate(gx_partners):
            to_g, to_s = at_gx(dg, dx)
            copies.append(
                pltpu.make_async_remote_copy(
                    src_ref=abuf.at[t, to_g * X + to_s // W],
                    dst_ref=r1.at[t, pl.ds(8 * (o + 1), 8)],
                    send_sem=a1_send.at[t, o],
                    recv_sem=a1_recv.at[t, o],
                    device_id=(to_g, to_s),
                    device_id_type=MESH,
                )
            )
            copies[-1].start()
        r1[t, 0:8] = abuf[t, g * X + x]
        return copies

    def a2a_2(t, first):
        for c in first:
            c.wait_recv()
        for d in range(W):
            r1t[t, d] = r1[t, pl.ds(d, D // W, stride=W), :]
        copies = []
        for dw in range(1, W):
            to = at_w(dw)
            copies.append(
                pltpu.make_async_remote_copy(
                    src_ref=r1t.at[t, lax.rem(w + dw, W)],
                    dst_ref=r3.at[t, dw],
                    send_sem=a2_send.at[t, dw - 1],
                    recv_sem=a2_recv.at[t, dw - 1],
                    device_id=to,
                    device_id_type=MESH,
                )
            )
            copies[-1].start()
        r3[t, 0] = r1t[t, w]
        return copies

    def place(t, second):
        for c in second:
            c.wait_recv()
        got = r3[t].reshape(D, 128).T
        name = got[96:128]
        high = jnp.floor(name * (1.0 / 128.0))
        low = name - 128.0 * high
        acc = jnp.zeros((96, 128), F32)
        for q in range(CAP // 4):
            left, right = [], []
            for z in range(4 * q, 4 * q + 4):
                right.append(onehot(low[z : z + 1] == iota((128, D), 0).astype(F32)))
                hit = high[z : z + 1] == iota((16, D), 0).astype(F32)
                v = jnp.concatenate(
                    [jnp.where(hit, got[32 * k + z : 32 * k + z + 1], 0.0) for k in range(3)], axis=0
                )
                left.append(jnp.concatenate(pieces(v, 2), axis=0))
            acc = acc + mm_nt(jnp.concatenate(left, axis=1), jnp.concatenate(right, axis=1))
        acc = acc[:48] + acc[48:]
        for k in range(3):
            for h in range(16):
                load_ref[t, k : k + 1, 128 * h : 128 * h + 128] = acc[16 * k + h : 16 * k + h + 1]

    def write_adjoint():
        own = state[UP : UP + ROWS].reshape(ROWS * 8, LANES)
        lane = iota((LANES, COLS), 0)
        j, b = lane >> 4, lane & 15
        keep = ((j < 25) & (b < 15)) | ((j == 25) & (b > 0))
        back = onehot(keep & (ext_col(lane) == iota((LANES, COLS), 1) + 3))
        n = iota((COMP * ROWS, ROWS * 8), 1)
        unperm = onehot((n & 7) * ROWS + (n >> 3) == iota((COMP * ROWS, ROWS * 8), 0))
        out_ref[...] = pick_rows(unperm, pick(own, back)).reshape(COMP, ROWS, COLS)

    setup_rows()
    sides_finish()
    row_late = row_copies(10, slice(384, 512))
    for c in row_late:
        c.start()
    fill_rows(UP, ROWS - DOWN - 1)
    for c in row_early + row_late:
        c.wait_recv()
    for c in row_late + row_early:
        c.wait_send()
    fill_rows(-UP, UP)
    fill_rows(ROWS - DOWN - 1, ROWS + DOWN)
    sweep(0)
    sweep(1)
    gather(0)
    first_0 = a2a_1(0)
    sweep(2)
    sweep(3)
    gather(1)
    first_1 = a2a_1(1)
    second_0 = a2a_2(0, first_0)
    write_adjoint()
    second_1 = a2a_2(1, first_1)
    place(0, second_0)
    place(1, second_1)
    for c in side_copies + first_0 + first_1 + second_0 + second_1:
        c.wait_send()


def on_device(
    G,
    S,
    adjoint_start,
    objective_grad,
    diagonal,
    connect,
    element_scale,
    element_matrix,
    traction_map,
    iface_node,
    iface_dest,
    iface_target,
    iface_count,
):
    vmem = pl.BlockSpec(memory_space=pltpu.VMEM)
    D = G * S
    XG = D // W
    dma = pltpu.SemaphoreType.DMA
    I32 = jnp.int32
    scratch = [
        pltpu.VMEM((COMP, ROWS, COLS), F32),
        pltpu.VMEM((COMP, ROWS, COLS), F32),
        pltpu.VMEM((ROWS, COLS), F32),
        pltpu.VMEM((8, ELEMS), I32),
        pltpu.VMEM((64, ELEMS), F32),
        pltpu.VMEM((64, 64), BF16),
        pltpu.VMEM((3, COMP), F32),
        pltpu.VMEM((1, IF_CAP), I32),
        pltpu.VMEM((1, IF_CAP), I32),
        pltpu.VMEM((1, IF_CAP), I32),
        pltpu.VMEM((1, 1), I32),
        dma((11,)),
        pltpu.VMEM((UP + ROWS + DOWN, 8, LANES), F32),
        pltpu.VMEM((O_UP + ROWS + O_DOWN, 8, LANES), F32),
        pltpu.VMEM((O_UP + ROWS + O_DOWN, 8, LANES), F32),
        pltpu.VMEM((4, 16, LANES), F32),
        pltpu.VMEM((4, 8, LANES), F32),
        pltpu.VMEM((4, 8, LANES), F32),
        pltpu.VMEM((LANES, LANES), BF16),
        pltpu.VMEM((8, 384), I32),
        pltpu.VMEM((64, 384), F32),
        pltpu.VMEM((LANES, IF_CAP), BF16),
        pltpu.VMEM((D, IF_CAP), BF16),
        pltpu.VMEM((1, IF_CAP), F32),
        pltpu.VMEM((2, ROWS, 8, 128), F32),
        pltpu.VMEM((2, ROWS, 8, 128), F32),
        pltpu.VMEM((2, 4, 16, 128), F32),
        pltpu.VMEM((2, 4, 16, 128), F32),
        pltpu.VMEM((ITERS, XG, 8, 128), F32),
        pltpu.VMEM((ITERS, D, 128), F32),
        pltpu.VMEM((ITERS, W, XG, 128), F32),
        pltpu.VMEM((ITERS, W, XG, 128), F32),
        dma((16,)),
        dma((16,)),
        dma((ITERS, XG - 1)),
        dma((ITERS, XG - 1)),
        dma((ITERS, W - 1)),
        dma((ITERS, W - 1)),
    ]
    call = pl.pallas_call(
        functools.partial(kernel, G, S),
        out_shape=(
            jax.ShapeDtypeStruct((COMP, ROWS, COLS), F32),
            jax.ShapeDtypeStruct((ITERS, 3, IF_CAP), F32),
        ),
        in_specs=[pl.BlockSpec(memory_space=pl.ANY)] * 11,
        out_specs=(vmem, vmem),
        scratch_shapes=scratch,
        compiler_params=pltpu.CompilerParams(
            collective_id=0, has_side_effects=True, vmem_limit_bytes=62 * 1024 * 1024
        ),
    )
    return call(
        adjoint_start,
        objective_grad,
        diagonal,
        connect,
        element_scale,
        element_matrix,
        traction_map,
        iface_node.reshape(1, IF_CAP),
        iface_dest.reshape(1, IF_CAP),
        iface_target.reshape(1, IF_CAP),
        iface_count.reshape(1, 1),
    )


def solution(mesh):
    both = ("group", "sub")
    placed = (
        P(None, "group", "sub"),
        P(None, "group", "sub"),
        P("group", "sub"),
        P(None, both),
        P(None, both),
        P(),
        P(),
        P(both),
        P(both, None),
        P(both),
        P(both),
    )
    return jax.shard_map(
        functools.partial(on_device, mesh.shape["group"], mesh.shape["sub"]),
        mesh=mesh,
        in_specs=placed,
        out_specs=(P(None, "group", "sub"), P(None, None, both)),
        check_vma=False,
    )
```

```python
import functools
import jax
import jax.numpy as jnp
from jax import lax
from jax.experimental import pallas as pl
from jax.experimental.pallas import tpu as pltpu
from jax.sharding import PartitionSpec as P

COMP = 6
ROWS = 32
COLS = 384
ELEMS = 338
IF_CAP = 2048
CAP = 32
ITERS = 2
SWEEPS = 2
LANES = 512
UP, DOWN = 11, 10
O_UP, O_DOWN = 8, 7
STARTS = (
    [-11, -8, -5, -2, -1] + [min(3 * i, ROWS + 2) - 3 for i in range(13)] + [29, 32, 35, 38]
)
ACTIVE = [(0, 22), (1, 21), (2, 20), (4, 18)]
UPDATED = [(-8, 39), (-5, 36), (-3, 35), (0, 32)]
F32 = jnp.float32
BF16 = jnp.bfloat16
MESH = pl.DeviceIdType.MESH
NT = (((1,), (1,)), ((), ()))


def iota(shape, dim):
    return lax.broadcasted_iota(jnp.int32, shape, dim)


def onehot(mask):
    return jnp.where(mask, 1.0, 0.0).astype(BF16)


def mm(a, b):
    return jnp.dot(a, b, preferred_element_type=F32)


def mm_nt(a, b):
    return lax.dot_general(a, b, NT, preferred_element_type=F32)


def pieces(x, n):
    out = []
    for k in range(n):
        p = x.astype(BF16)
        out.append(p)
        if k + 1 < n:
            x = x - p.astype(F32)
    return out


def total(terms):
    terms = list(terms)
    while len(terms) > 1:
        terms = [
            terms[i] + terms[i + 1] if i + 1 < len(terms) else terms[i]
            for i in range(0, len(terms), 2)
        ]
    return terms[0]


def pick(x, sel, n=3):
    return total([mm(p, sel) for p in pieces(x, n)])


def pick_rows(sel, x, n=3):
    return total([mm(sel, p) for p in pieces(x, n)])


def ext_col(lane):
    j = lane >> 4
    return jnp.where(j == 25, 374, 15 * j) + (lane & 15)


def owner(row):
    return 0 if row < 0 else (1 if row < ROWS else 2)


def block_of(e):
    return 0 if e < 5 else (1 if e < 18 else 2)


def kernel(
    G,
    S,
    adj_hbm,
    obj_hbm,
    diag_hbm,
    conn_hbm,
    scale_hbm,
    em_hbm,
    tm_hbm,
    node_hbm,
    dest_hbm,
    target_hbm,
    count_hbm,
    out_hbm,
    load_hbm,
    out_ref,
    load_ref,
    out_sem,
    adj_ref,
    obj_ref,
    diag_ref,
    conn_ref,
    scale_ref,
    em_ref,
    tm_ref,
    node_ref,
    dest_ref,
    target_ref,
    count_ref,
    in_sem,
    state_a,
    state_b,
    field_s,
    oi,
    asm,
    scale_own,
    scale_up,
    scale_down,
    wmat,
    conn_pad,
    scale_pad,
    colhot,
    desthot,
    slot_s,
    side_send,
    side_recv,
    sscale_send,
    sscale_recv,
    abuf,
    arrived,
    halo_send,
    halo_recv,
    all_send,
    all_recv,
):
    D = G * S
    states = (state_a, state_b)
    state = state_a
    g = lax.axis_index("group")
    s = lax.axis_index("sub")

    def at(dg, ds):
        return (lax.rem(g + dg + G, G), lax.rem(s + ds + S, S))

    loads = [
        pltpu.make_async_copy(src, dst, in_sem.at[n])
        for n, (src, dst) in enumerate(
            [
                (adj_hbm, adj_ref),
                (diag_hbm, diag_ref),
                (obj_hbm, obj_ref),
                (conn_hbm.at[0:8], conn_ref),
                (scale_hbm, scale_ref),
                (em_hbm, em_ref),
                (tm_hbm, tm_ref),
                (node_hbm, node_ref),
                (dest_hbm, dest_ref),
                (target_hbm, target_ref),
                (count_hbm, count_ref),
            ]
        )
    ]
    for c in loads:
        c.start()
    barrier = pltpu.get_barrier_semaphore()
    others = [at(dg, ds) for ds in range(S) for dg in range(G)][1:]
    for t in others:
        pl.semaphore_signal(barrier, inc=1, device_id=t, device_id_type=MESH)

    lane = iota((COLS, LANES), 1)
    sel = onehot((ext_col(lane) == iota((COLS, LANES), 0) + 3) & (lane < 416))
    m = iota((ROWS * 8, COMP * ROWS), 0)
    perm = onehot(((m & 7) * ROWS + (m >> 3) == iota((ROWS * 8, COMP * ROWS), 1)) & ((m & 7) < COMP))
    loads[0].wait()
    first = pick_rows(perm, adj_ref[...].reshape(COMP * ROWS, COLS))
    state[UP : UP + ROWS] = pick(first, sel).reshape(ROWS, 8, LANES)

    loads[1].wait()
    loads[2].wait()
    inverse = 1.0 / diag_ref[...]
    scaled_obj = (obj_ref[...] * inverse[None]).reshape(COMP * ROWS, COLS)
    m = iota((ROWS * 8, ROWS), 0)
    perm_inv = onehot(((m & 7) == COMP) & ((m >> 3) == iota((ROWS * 8, ROWS), 1)))
    first = pick_rows(perm, scaled_obj) + pick_rows(perm_inv, inverse)
    oi[O_UP : O_UP + ROWS] = pick(first, sel).reshape(ROWS, 8, LANES)

    def remote(n, src, dst, dev):
        return pltpu.make_async_remote_copy(
            src_ref=src,
            dst_ref=dst,
            send_sem=halo_send.at[n],
            recv_sem=halo_recv.at[n],
            device_id=dev,
            device_id_type=MESH,
        )

    def turn(v, n):
        return pltpu.roll(v, n % 128, v.ndim - 1)

    def pack_right(two, three, start):
        lane = iota(two.shape, two.ndim - 1)
        return jnp.where(lane < start + 16, turn(two, start - 112), turn(three, start + 16))

    for p in range(0, ROWS, 8):
        st = [state[UP + p : UP + p + 8, :, 128 * q : 128 * q + 128] for q in (0, 2, 3)]
        ob = [oi[O_UP + p : O_UP + p + 8, :, 128 * q : 128 * q + 128] for q in (0, 2, 3)]
        lane = iota((8, 8, 128), 2)
        side_send[0, p : p + 8] = jnp.where(lane < 80, turn(st[0], 32), turn(ob[0], 80))
        side_send[1, p : p + 8] = jnp.where(
            lane < 80, pack_right(ob[1], ob[2], 32), pack_right(st[1], st[2], 80)
        )
    def pair(n, ref, up_to, down_rows, up_rows, cols):
        lo, hi = down_rows
        first, last = up_rows
        return [
            remote(n, ref.at[lo:hi, :, cols], ref.at[0 : hi - lo, :, cols], at(1, 0)),
            remote(
                n + 1,
                ref.at[first:last, :, cols],
                ref.at[up_to : up_to + last - first, :, cols],
                at(-1, 0),
            ),
        ]

    def state_rows(n, cols):
        return pair(n, state, UP + ROWS, (ROWS, UP + ROWS), (UP, UP + DOWN), cols)

    def oi_rows(n, cols):
        return pair(
            n, oi, O_UP + ROWS, (ROWS, O_UP + ROWS), (O_UP, O_UP + O_DOWN), cols
        )

    def scale_rows(n, cols):
        return [
            remote(n, scale_own.at[:, 8:16, cols], scale_up.at[:, :, cols], at(1, 0)),
            remote(n + 1, scale_own.at[:, 0:8, cols], scale_down.at[:, :, cols], at(-1, 0)),
        ]

    loads[3].wait()
    loads[4].wait()
    conn_pad[...] = jnp.full_like(conn_pad, -1)
    conn_pad[:, 0:ELEMS] = conn_ref[...]
    scale_pad[...] = jnp.zeros_like(scale_pad)
    scale_pad[:, 0:ELEMS] = scale_ref[...]
    node0 = conn_pad[0:1]
    row0 = lax.div(node0, jnp.int32(390))
    col0 = node0 - row0 * 390
    elem_i = jnp.where(node0 >= 0, lax.div(row0 + 2, jnp.int32(3)), -1)
    elem_j = jnp.where(node0 >= 0, lax.div(col0 + 14, jnp.int32(15)), -1)
    row_hot = onehot(elem_i == iota((16, 384), 0))
    start_row = jnp.minimum(3 * iota((16, LANES), 0), ROWS + 2)
    lane = iota((16, LANES), 1)
    off_side = ((s == 0) & (lane < 3)) | ((s == S - 1) & (lane >= 413))
    j_mask = elem_j[:, None, :] == iota((32, 16, 384), 0)
    for a in range(4):
        sc = scale_pad[16 * a : 16 * a + 16]
        out = []
        for p in pieces(sc, 3):
            p = jnp.where(j_mask, p.astype(F32)[None], 0.0).reshape(LANES, 384)
            out.append(mm_nt(row_hot, p.astype(BF16)))
        r = start_row + a
        off = ((g == 0) & (r < 3)) | ((g == G - 1) & (r >= ROWS + 3)) | off_side
        scale_own[a] = jnp.where(off, 0.0, total(out))
    for a in range(4):
        sscale_send[0, a] = turn(scale_own[a, :, 0:128], 32)
        sscale_send[1, a] = pack_right(scale_own[a, :, 256:384], scale_own[a, :, 384:512], 80)
    pl.semaphore_wait(barrier, len(others))
    side_copies = [
        remote(0, side_send.at[0], side_recv.at[0], at(0, -1)),
        remote(1, side_send.at[1], side_recv.at[1], at(0, 1)),
        remote(2, sscale_send.at[0], sscale_recv.at[0], at(0, -1)),
        remote(3, sscale_send.at[1], sscale_recv.at[1], at(0, 1)),
    ]
    early, last_tile = slice(0, 384), slice(384, 512)
    row_early = state_rows(4, slice(128, 384)) + oi_rows(6, early) + scale_rows(8, early)
    for c in side_copies + row_early:
        c.start()

    loads[5].wait()
    r = iota((LANES, 64), 0)
    e_hot = onehot((r >> 7) * 16 + (r & 15) == iota((LANES, 64), 1))
    left = mm(e_hot, em_ref[...]).astype(BF16)
    rr, cc = iota((LANES, LANES), 0), iota((LANES, LANES), 1)
    wide = mm_nt(left, e_hot)
    wmat[...] = jnp.where(((rr >> 4) & 7) == ((cc >> 4) & 7), wide, 0.0).astype(BF16)

    def sides_finish():
        for c in side_copies:
            c.wait_recv()
        for p in range(0, ROWS, 8):
            lane = iota((8, 8, 128), 2)
            right, left = side_recv[0, p : p + 8], side_recv[1, p : p + 8]
            own = state[UP + p : UP + p + 8, :, 384:512]
            state[UP + p : UP + p + 8, :, 384:512] = jnp.where(
                lane < 32, own, jnp.where(lane < 80, right, left)
            )
            own = oi[O_UP + p : O_UP + p + 8, :, 384:512]
            both = jnp.where(lane < 80, left, right)
            oi[O_UP + p : O_UP + p + 8, :, 384:512] = jnp.where(
                lane < 32, own, jnp.where(lane < 80, turn(both, -48), turn(both, 48))
            )
        lane = iota((16, 128), 1)
        for a in range(4):
            scale_own[a, :, 384:512] = jnp.where(
                lane < 32,
                scale_own[a, :, 384:512],
                jnp.where(lane < 80, sscale_recv[0, a], sscale_recv[1, a]),
            )

    def fill(first, three):
        lane = iota(first.shape, first.ndim - 1)
        ahead = turn(three, 6)
        first_new = jnp.where(lane < 3, ahead, first)
        three_new = jnp.where((lane >= 32) & (lane < 35), ahead, three)
        three_new = jnp.where((lane >= 29) & (lane < 32), turn(three, -6), three_new)
        three_new = jnp.where(lane >= 125, turn(first, -6), three_new)
        return first_new, three_new

    def fill_rows():
        for r in range(UP, UP + ROWS, 8):
            state[r : r + 8, :, 0:128], state[r : r + 8, :, 384:512] = fill(
                state[r : r + 8, :, 0:128], state[r : r + 8, :, 384:512]
            )

    def scale_row(a, e, cols):
        if e < 5:
            v = scale_up[a, e : e + 1, cols]
        elif e < 18:
            v = scale_own[a, e - 5 : e - 4, cols]
        else:
            v = scale_down[a, e - 18 : e - 17, cols]
        return jnp.broadcast_to(v, (8, 128))

    def products(t, elems, rows, begun=()):
        src = states[t % 2]
        for q in range(4):
            cols = slice(128 * q, 128 * q + 128)
            parts = []
            for a in range(4):
                v = [src[UP + STARTS[e] + a, :, cols] * scale_row(a, e, cols) for e in elems]
                parts.append(jnp.concatenate(v, axis=0).astype(BF16))
            o = mm(jnp.concatenate(parts, axis=1), wmat[...])
            for row in rows:
                terms = [
                    o[8 * n : 8 * n + 8, 128 * a : 128 * a + 128]
                    for n, e in enumerate(elems)
                    for a in range(4)
                    if STARTS[e] + a == row and block_of(e) == owner(row)
                ]
                if row in begun:
                    terms.append(asm[O_UP + row, :, cols])
                asm[O_UP + row, :, cols] = total(terms)

    def update(t, first, last):
        dst = states[(t + 1) % 2]
        step = 4
        for r0 in range(first, last, step):
            n = min(step, last - r0)
            lane = iota((n, 8, 128), 2)
            low = lane & 15
            a0 = O_UP + r0
            tiles = [asm[a0 : a0 + n, :, 128 * q : 128 * q + 128] for q in range(4)]
            ahead = [turn(v, 1) for v in tiles]
            back = [turn(v, -1) for v in tiles]
            new = []
            for q in range(4):
                before = jnp.where(lane == 0, ahead[(q + 3) % 4], ahead[q])
                after = jnp.where(lane == 127, back[(q + 1) % 4], back[q])
                more = jnp.where(low == 0, before, jnp.where(low == 15, after, 0.0))
                if q == 3:
                    pair = jnp.where(lane >= 96, lane - 96, lane)
                    more = jnp.where((pair == 14) | (pair == 15), turn(tiles[3], -2), more)
                    more = jnp.where((pair == 16) | (pair == 17), turn(tiles[3], 2), more)
                cols = slice(128 * q, 128 * q + 128)
                rhs = oi[a0 : a0 + n, :, cols]
                inv = jnp.broadcast_to(oi[a0 : a0 + n, COMP : COMP + 1, cols], (n, 8, 128))
                new.append(rhs - (tiles[q] + more) * inv)
            if t < 3:
                new[0], new[3] = fill(new[0], new[3])
            for q in range(4):
                dst[UP + r0 : UP + r0 + n, :, 128 * q : 128 * q + 128] = new[q]

    def sweep(t):
        products(t, range(*ACTIVE[t]), range(*UPDATED[t]))
        update(t, *UPDATED[t])

    INNER = range(6, 16)

    def sweep_0_inner():
        products(0, INNER, range(0, 31))
        update(0, 1, 30)

    def sweep_0_outer():
        rows = [r for r in range(*UPDATED[0]) if r < 1 or r > 29]
        products(0, [e for e in range(*ACTIVE[0]) if e not in INNER], rows, (0, 30))
        update(0, UPDATED[0][0], 1)
        update(0, 30, UPDATED[0][1])


    CH = 512
    for c in loads[6:]:
        c.wait()
    node = node_ref[...]
    node_row = lax.div(node, jnp.int32(COLS))
    e_col = node - node_row * COLS + 3
    e_lane = jnp.where(e_col < 375, e_col + lax.div(e_col, jnp.int32(15)), e_col + 26)

    def setup_rows():
        live = iota((1, IF_CAP), 1) < count_ref[...]
        dest = jnp.where(live, dest_ref[...], -1)
        tri = onehot(iota((256, 256), 0) < iota((256, 256), 1))
        carry = jnp.zeros((D, 1), F32)
        for b in range(IF_CAP // 256):
            cols = slice(256 * b, 256 * b + 256)
            hot = jnp.where(dest[:, cols] == iota((D, 256), 0), 1.0, 0.0)
            desthot[:, cols] = hot.astype(BF16)
            before = mm(hot.astype(BF16), tri) + carry
            slot_s[:, cols] = jnp.sum(before * hot, axis=0, keepdims=True)
            carry = carry + jnp.sum(hot, axis=1, keepdims=True)
        for b in range(IF_CAP // CH):
            cols = slice(CH * b, CH * b + CH)
            colhot[:, cols] = onehot(e_lane[:, cols] == iota((LANES, CH), 0))

    def tractions(t):
        lane = iota((1, 256), 1)
        trac = []
        for k in range(3):
            row = jnp.zeros((1, 256), F32)
            for c in range(COMP):
                row = jnp.where((lane & 7) == c, tm_ref[k : k + 1, c : c + 1], row)
            trac.append(jnp.where((iota((32, 256), 1) >> 3) == iota((32, 256), 0), row, 0.0))
        high, low = pieces(jnp.concatenate(trac, axis=0), 2)
        own = state[UP : UP + ROWS].reshape(ROWS * 8, LANES)
        own_high, own_low = pieces(own, 2)
        field = mm(high, own_high) + (mm(high, own_low) + mm(low, own_high))
        field_s[192 * t : 192 * t + 192] = jnp.concatenate(pieces(field, 2), axis=0)

    def gather():
        acc = jnp.zeros((D, 256), F32)
        for b in range(IF_CAP // CH):
            cols = slice(CH * b, CH * b + CH)
            v = mm(field_s[...], colhot[:, cols])
            v = jnp.concatenate([v[:96] + v[96:192], v[192:288] + v[288:]], axis=0)
            v = v.reshape(6, 32, CH)
            v = jnp.where(node_row[:, cols][None] == iota((1, 32, CH), 1), v, 0.0)
            v = jnp.sum(v, axis=1, keepdims=True)
            name = target_ref[:, cols].astype(F32)[None]
            v = jnp.concatenate([v[:3], name, v[3:]], axis=0)
            slots = slot_s[:, cols].astype(jnp.int32)[None] == iota((1, CAP, CH), 1)
            v = jnp.where(slots, v, 0.0).reshape(7 * CAP, CH)
            v = jnp.concatenate([v, jnp.zeros((CAP, CH), F32)], axis=0)
            for p in pieces(v, 2):
                acc = acc + mm_nt(desthot[:, cols], p)
        abuf[:, 0, :] = acc[:, 0:128]
        abuf[:, 1, :] = acc[:, 128:256]

    def all_to_all():
        for n, (to_g, to_s) in enumerate(others):
            pltpu.make_async_remote_copy(
                src_ref=abuf.at[to_g * S + to_s],
                dst_ref=arrived.at[n + 1],
                send_sem=all_send,
                recv_sem=all_recv,
                device_id=(to_g, to_s),
                device_id_type=MESH,
            ).start()
        arrived[0] = abuf[g * S + s]
        return pltpu.make_async_remote_copy(
            src_ref=abuf.at[0 : D - 1],
            dst_ref=arrived.at[1:D],
            send_sem=all_send,
            recv_sem=all_recv,
            device_id=others[0],
            device_id_type=MESH,
        )

    def place():
        got = [arrived[:, t, :].T for t in range(ITERS)]
        name = got[0][96:128]
        high = jnp.floor(name * (1.0 / 128.0))
        low = name - 128.0 * high
        upper = [v.astype(BF16).astype(F32) for v in got]
        lower = [v - u for v, u in zip(got, upper)]
        acc = jnp.zeros((192, 128), F32)
        for q in range(CAP // 4):
            left, right = [], []
            for z in range(4 * q, 4 * q + 4):
                right.append(onehot(low[z : z + 1] == iota((128, D), 0).astype(F32)))
                hit = high[z : z + 1] == iota((16, D), 0).astype(F32)
                v = [
                    jnp.where(hit, part[t][32 * k + z : 32 * k + z + 1], 0.0)
                    for part in (upper, lower)
                    for t in range(ITERS)
                    for k in range(3)
                ]
                left.append(jnp.concatenate(v, axis=0).astype(BF16))
            acc = acc + mm_nt(jnp.concatenate(left, axis=1), jnp.concatenate(right, axis=1))
        acc = acc[:96] + acc[96:]
        for t in range(ITERS):
            for k in range(3):
                for h in range(16):
                    n = (3 * t + k) * 16 + h
                    load_ref[k, t : t + 1, 128 * h : 128 * h + 128] = acc[n : n + 1]

    def write_adjoint():
        own = state[UP : UP + ROWS].reshape(ROWS * 8, LANES)
        lane = iota((LANES, COLS), 0)
        j, b = lane >> 4, lane & 15
        keep = ((j < 25) & (b < 15)) | ((j == 25) & (b > 0))
        back = onehot(keep & (ext_col(lane) == iota((LANES, COLS), 1) + 3))
        n = iota((COMP * ROWS, ROWS * 8), 1)
        unperm = onehot((n & 7) * ROWS + (n >> 3) == iota((COMP * ROWS, ROWS * 8), 0))
        out_ref[...] = pick_rows(unperm, pick(own, back)).reshape(COMP, ROWS, COLS)

    setup_rows()
    sides_finish()
    fill_rows()
    row_late = (
        state_rows(10, last_tile)
        + state_rows(12, slice(0, 128))
        + oi_rows(14, last_tile)
        + scale_rows(16, last_tile)
    )
    for c in row_late:
        c.start()
    sweep_0_inner()
    for c in row_early + row_late:
        c.wait_recv()
    sweep_0_outer()
    for c in side_copies + row_early + row_late:
        c.wait_send()
    sweep(1)
    tractions(0)
    sweep(2)
    sweep(3)
    tractions(1)
    gather()
    exchange = all_to_all()
    write_adjoint()
    out_copy = pltpu.make_async_copy(out_ref, out_hbm, out_sem.at[0])
    out_copy.start()
    exchange.wait_recv()
    place()
    load_copy = pltpu.make_async_copy(load_ref, load_hbm, out_sem.at[1])
    load_copy.start()
    exchange.wait_send()
    out_copy.wait()
    load_copy.wait()


def on_device(
    G,
    S,
    adjoint_start,
    objective_grad,
    diagonal,
    connect,
    element_scale,
    element_matrix,
    traction_map,
    iface_node,
    iface_dest,
    iface_target,
    iface_count,
):
    hbm = pl.BlockSpec(memory_space=pl.ANY)
    D = G * S
    dma = pltpu.SemaphoreType.DMA
    I32 = jnp.int32
    scratch = [
        pltpu.VMEM((COMP, ROWS, COLS), F32),
        pltpu.VMEM((3, ITERS, IF_CAP), F32),
        dma((2,)),
        pltpu.VMEM((COMP, ROWS, COLS), F32),
        pltpu.VMEM((COMP, ROWS, COLS), F32),
        pltpu.VMEM((ROWS, COLS), F32),
        pltpu.VMEM((8, ELEMS), I32),
        pltpu.VMEM((64, ELEMS), F32),
        pltpu.VMEM((64, 64), BF16),
        pltpu.VMEM((3, COMP), F32),
        pltpu.VMEM((1, IF_CAP), I32),
        pltpu.VMEM((1, IF_CAP), I32),
        pltpu.VMEM((1, IF_CAP), I32),
        pltpu.VMEM((1, 1), I32),
        dma((11,)),
        pltpu.VMEM((UP + ROWS + DOWN, 8, LANES), F32),
        pltpu.VMEM((UP + ROWS + DOWN, 8, LANES), F32),
        pltpu.VMEM((ITERS * 192, LANES), BF16),
        pltpu.VMEM((O_UP + ROWS + O_DOWN, 8, LANES), F32),
        pltpu.VMEM((O_UP + ROWS + O_DOWN, 8, LANES), F32),
        pltpu.VMEM((4, 16, LANES), F32),
        pltpu.VMEM((4, 8, LANES), F32),
        pltpu.VMEM((4, 8, LANES), F32),
        pltpu.VMEM((LANES, LANES), BF16),
        pltpu.VMEM((8, 384), I32),
        pltpu.VMEM((64, 384), F32),
        pltpu.VMEM((LANES, IF_CAP), BF16),
        pltpu.VMEM((D, IF_CAP), BF16),
        pltpu.VMEM((1, IF_CAP), F32),
        pltpu.VMEM((2, ROWS, 8, 128), F32),
        pltpu.VMEM((2, ROWS, 8, 128), F32),
        pltpu.VMEM((2, 4, 16, 128), F32),
        pltpu.VMEM((2, 4, 16, 128), F32),
        pltpu.VMEM((D, ITERS, 128), F32),
        pltpu.VMEM((D, ITERS, 128), F32),
        dma((18,)),
        dma((18,)),
        dma,
        dma,
    ]
    call = pl.pallas_call(
        functools.partial(kernel, G, S),
        out_shape=(
            jax.ShapeDtypeStruct((COMP, ROWS, COLS), F32),
            jax.ShapeDtypeStruct((3, ITERS, IF_CAP), F32),
        ),
        in_specs=[hbm] * 11,
        out_specs=(hbm, hbm),
        scratch_shapes=scratch,
        compiler_params=pltpu.CompilerParams(
            collective_id=0, has_side_effects=True, vmem_limit_bytes=62 * 1024 * 1024
        ),
    )
    adjoint, load = call(
        adjoint_start,
        objective_grad,
        diagonal,
        connect,
        element_scale,
        element_matrix,
        traction_map,
        iface_node.reshape(1, IF_CAP),
        iface_dest.reshape(1, IF_CAP),
        iface_target.reshape(1, IF_CAP),
        iface_count.reshape(1, 1),
    )
    adjoint, load = hand_out(adjoint, load)
    return adjoint, load.transpose(1, 0, 2)


def hand_out_kernel(a, b, a_out, b_out, a_v, b_v, sem):
    for start, end in (((a, b), (a_v, b_v)), ((a_v, b_v), (a_out, b_out))):
        copies = [pltpu.make_async_copy(start[i], end[i], sem.at[i]) for i in range(2)]
        for c in copies:
            c.start()
        for c in copies:
            c.wait()


def hand_out(a, b):
    hbm = pl.BlockSpec(memory_space=pl.ANY)
    return pl.pallas_call(
        hand_out_kernel,
        out_shape=(jax.ShapeDtypeStruct(a.shape, F32), jax.ShapeDtypeStruct(b.shape, F32)),
        in_specs=[hbm, hbm],
        out_specs=(hbm, hbm),
        scratch_shapes=[
            pltpu.VMEM(a.shape, F32),
            pltpu.VMEM(b.shape, F32),
            pltpu.SemaphoreType.DMA((2,)),
        ],
        compiler_params=pltpu.CompilerParams(vmem_limit_bytes=62 * 1024 * 1024),
    )(a, b)


def solution(mesh):
    both = ("group", "sub")
    placed = (
        P(None, "group", "sub"),
        P(None, "group", "sub"),
        P("group", "sub"),
        P(None, both),
        P(None, both),
        P(),
        P(),
        P(both),
        P(both, None),
        P(both),
        P(both),
    )
    return jax.shard_map(
        functools.partial(on_device, mesh.shape["group"], mesh.shape["sub"]),
        mesh=mesh,
        in_specs=placed,
        out_specs=(P(None, "group", "sub"), P(None, None, both)),
        check_vma=False,
    )
```

```python
import functools
import jax
import jax.numpy as jnp
from jax import lax
from jax.experimental import pallas as pl
from jax.experimental.pallas import tpu as pltpu
from jax.sharding import PartitionSpec as P

COMP = 6
ROWS = 32
COLS = 384
ELEMS = 338
IF_CAP = 2048
CAP = 32
ITERS = 2
W = 8
LANES = 512
UP, DOWN = 11, 10
O_UP, O_DOWN = 8, 7
STARTS = (
    [-11, -8, -5, -2, -1] + [min(3 * i, ROWS + 2) - 3 for i in range(13)] + [29, 32, 35, 38]
)
ACTIVE = [(0, 22), (1, 21), (2, 20), (4, 18)]
UPDATED = [(-8, 39), (-5, 36), (-3, 35), (0, 32)]
F32 = jnp.float32
BF16 = jnp.bfloat16
MESH = pl.DeviceIdType.MESH
NT = (((1,), (1,)), ((), ()))


def iota(shape, dim):
    return lax.broadcasted_iota(jnp.int32, shape, dim)


def onehot(mask):
    return jnp.where(mask, 1.0, 0.0).astype(BF16)


def mm(a, b):
    return jnp.dot(a, b, preferred_element_type=F32)


def mm_nt(a, b):
    return lax.dot_general(a, b, NT, preferred_element_type=F32)


def pieces(x, n):
    out = []
    for k in range(n):
        p = x.astype(BF16)
        out.append(p)
        if k + 1 < n:
            x = x - p.astype(F32)
    return out


def total(terms):
    terms = list(terms)
    while len(terms) > 1:
        terms = [
            terms[i] + terms[i + 1] if i + 1 < len(terms) else terms[i]
            for i in range(0, len(terms), 2)
        ]
    return terms[0]


def pick(x, sel, n=3):
    return total([mm(p, sel) for p in pieces(x, n)])


def pick_rows(sel, x, n=3):
    return total([mm(sel, p) for p in pieces(x, n)])


def ext_col(lane):
    j = lane >> 4
    return jnp.where(j == 25, 374, 15 * j) + (lane & 15)


def owner(row):
    return 0 if row < 0 else (1 if row < ROWS else 2)


def block_of(e):
    return 0 if e < 5 else (1 if e < 18 else 2)


def kernel(
    G,
    S,
    adj_hbm,
    obj_hbm,
    diag_hbm,
    conn_hbm,
    scale_hbm,
    em_hbm,
    tm_hbm,
    node_hbm,
    dest_hbm,
    target_hbm,
    count_hbm,
    out_hbm,
    load_hbm,
    out_ref,
    load_ref,
    out_sem,
    adj_ref,
    obj_ref,
    diag_ref,
    conn_ref,
    scale_ref,
    em_ref,
    tm_ref,
    node_ref,
    dest_ref,
    target_ref,
    count_ref,
    in_sem,
    state_a,
    state_b,
    field_s,
    oi,
    asm,
    scale_own,
    scale_up,
    scale_down,
    wmat,
    conn_pad,
    scale_pad,
    colhot,
    desthot,
    slot_s,
    names,
    tile_0,
    know_x,
    know_y,
    side_send,
    side_recv,
    sscale_send,
    sscale_recv,
    abuf,
    arrived,
    halo_send,
    halo_recv,
    all_send,
    all_recv,
):
    D = G * S
    states = (state_a, state_b)
    state = state_a
    g = lax.axis_index("group")
    s = lax.axis_index("sub")

    def at(dg, ds):
        return (lax.rem(g + dg + G, G), lax.rem(s + ds + S, S))

    loads = [
        pltpu.make_async_copy(src, dst, in_sem.at[n])
        for n, (src, dst) in enumerate(
            [
                (adj_hbm, adj_ref),
                (diag_hbm, diag_ref),
                (obj_hbm, obj_ref),
                (conn_hbm.at[0:8], conn_ref),
                (scale_hbm, scale_ref),
                (em_hbm, em_ref),
                (tm_hbm, tm_ref),
                (node_hbm, node_ref),
                (dest_hbm, dest_ref),
                (target_hbm, target_ref),
                (count_hbm, count_ref),
            ]
        )
    ]
    for c in loads:
        c.start()
    barrier = pltpu.get_barrier_semaphore()
    X, Z = S // W, W // 2
    x, z, core = s // W, lax.rem(s, W) // 2, lax.rem(s, 2)

    def hops(offset):
        dg, dx, dz, dc = offset
        steps = [min(dg, G - dg), min(dx, X - dx), min(dz, Z - dz)]
        return (sum(n > 0 for n in steps), sum(steps), dc)

    offsets = [
        (dg, dx, dz, dc) for dz in range(Z) for dx in range(X) for dg in range(G) for dc in range(2)
    ]
    others = [
        (
            lax.rem(g + dg, G),
            (lax.rem(x + dx, X) * Z + lax.rem(z + dz, Z)) * 2 + lax.rem(core + dc, 2),
        )
        for dg, dx, dz, dc in sorted(offsets[1:], key=hops, reverse=True)
    ]
    here = s % W
    line_w = [(g, s - here + lax.rem(here + n, W)) for n in range(1, W)]
    line_x = [at(0, W * n) for n in range(1, S // W)]
    line_y = [at(n, 0) for n in range(1, G)]
    near = line_y + [at(0, -1), at(0, 1)] + line_w + line_x
    for t in near:
        pl.semaphore_signal(barrier, inc=1, device_id=t, device_id_type=MESH)

    lane = iota((COLS, LANES), 1)
    sel = onehot((ext_col(lane) == iota((COLS, LANES), 0) + 3) & (lane < 416))
    m = iota((ROWS * 8, COMP * ROWS), 0)
    perm = onehot(((m & 7) * ROWS + (m >> 3) == iota((ROWS * 8, COMP * ROWS), 1)) & ((m & 7) < COMP))
    loads[0].wait()
    first = pick_rows(perm, adj_ref[...].reshape(COMP * ROWS, COLS))
    state[UP : UP + ROWS] = pick(first, sel).reshape(ROWS, 8, LANES)

    loads[1].wait()
    loads[2].wait()
    inverse = 1.0 / diag_ref[...]
    scaled_obj = (obj_ref[...] * inverse[None]).reshape(COMP * ROWS, COLS)
    m = iota((ROWS * 8, ROWS), 0)
    perm_inv = onehot(((m & 7) == COMP) & ((m >> 3) == iota((ROWS * 8, ROWS), 1)))
    first = pick_rows(perm, scaled_obj) + pick_rows(perm_inv, inverse)
    oi[O_UP : O_UP + ROWS] = pick(first, sel).reshape(ROWS, 8, LANES)

    def remote(n, src, dst, dev):
        return pltpu.make_async_remote_copy(
            src_ref=src,
            dst_ref=dst,
            send_sem=halo_send.at[n],
            recv_sem=halo_recv.at[n],
            device_id=dev,
            device_id_type=MESH,
        )

    def turn(v, n):
        return pltpu.roll(v, n % 128, v.ndim - 1)

    def pack_right(two, three, start):
        lane = iota(two.shape, two.ndim - 1)
        return jnp.where(lane < start + 16, turn(two, start - 112), turn(three, start + 16))

    for p in range(0, ROWS, 8):
        st = [state[UP + p : UP + p + 8, :, 128 * q : 128 * q + 128] for q in (0, 2, 3)]
        ob = [oi[O_UP + p : O_UP + p + 8, :, 128 * q : 128 * q + 128] for q in (0, 2, 3)]
        lane = iota((8, 8, 128), 2)
        side_send[0, p : p + 8] = jnp.where(lane < 80, turn(st[0], 32), turn(ob[0], 80))
        side_send[1, p : p + 8] = jnp.where(
            lane < 80, pack_right(ob[1], ob[2], 32), pack_right(st[1], st[2], 80)
        )
    def pair(n, ref, up_to, down_rows, up_rows, cols):
        lo, hi = down_rows
        first, last = up_rows
        return [
            remote(n, ref.at[lo:hi, :, cols], ref.at[0 : hi - lo, :, cols], at(1, 0)),
            remote(
                n + 1,
                ref.at[first:last, :, cols],
                ref.at[up_to : up_to + last - first, :, cols],
                at(-1, 0),
            ),
        ]

    def state_rows(n, cols):
        return pair(n, state, UP + ROWS, (ROWS, UP + ROWS), (UP, UP + DOWN), cols)

    def oi_rows(n, cols):
        return pair(
            n, oi, O_UP + ROWS, (ROWS, O_UP + ROWS), (O_UP, O_UP + O_DOWN), cols
        )

    def scale_rows(n, cols):
        return [
            remote(n, scale_own.at[:, 8:16, cols], scale_up.at[:, :, cols], at(1, 0)),
            remote(n + 1, scale_own.at[:, 0:8, cols], scale_down.at[:, :, cols], at(-1, 0)),
        ]

    pl.semaphore_wait(barrier, len(near))
    edges = (slice(0, DOWN), slice(ROWS - UP, ROWS))
    middle = slice(DOWN, ROWS - UP)
    sides = (at(0, -1), at(0, 1))

    def side_rows(n, rows):
        return [
            remote(n + k, side_send.at[k, rows], side_recv.at[k, rows], sides[k]) for k in range(2)
        ]

    side_edges = side_rows(0, edges[0]) + side_rows(2, edges[1])
    side_edges += [remote(4 + k, sscale_send.at[k], sscale_recv.at[k], sides[k]) for k in range(2)]
    side_middle = side_rows(6, middle)
    tile_0[0:UP] = state[ROWS : UP + ROWS, :, 0:128]
    tile_0[UP:] = state[UP : UP + DOWN, :, 0:128]
    early, last_tile = slice(0, 384), slice(384, 512)
    row_early = state_rows(8, slice(128, 384)) + oi_rows(10, early) + scale_rows(12, early)
    row_early += [
        remote(14, tile_0.at[0:UP], state.at[0:UP, :, 0:128], at(1, 0)),
        remote(15, tile_0.at[UP:], state.at[UP + ROWS :, :, 0:128], at(-1, 0)),
    ]
    scale_early = side_edges[4:] + row_early[4:6]
    for c in side_edges[:4] + row_early[:4] + row_early[6:] + side_middle:
        c.start()
    for t in line_x:
        pl.semaphore_signal(know_x, inc=1, device_id=t, device_id_type=MESH)

    loads[3].wait()
    loads[4].wait()
    conn_pad[...] = jnp.full_like(conn_pad, -1)
    conn_pad[:, 0:ELEMS] = conn_ref[...]
    scale_pad[...] = jnp.zeros_like(scale_pad)
    scale_pad[:, 0:ELEMS] = scale_ref[...]
    node0 = conn_pad[0:1]
    row0 = lax.div(node0, jnp.int32(390))
    col0 = node0 - row0 * 390
    elem_i = jnp.where(node0 >= 0, lax.div(row0 + 2, jnp.int32(3)), -1)
    elem_j = jnp.where(node0 >= 0, lax.div(col0 + 14, jnp.int32(15)), -1)
    row_hot = onehot(elem_i == iota((16, 384), 0))
    start_row = jnp.minimum(3 * iota((16, LANES), 0), ROWS + 2)
    lane = iota((16, LANES), 1)
    off_side = ((s == 0) & (lane < 3)) | ((s == S - 1) & (lane >= 413))
    j_mask = elem_j[:, None, :] == iota((32, 16, 384), 0)
    for a in range(4):
        sc = scale_pad[16 * a : 16 * a + 16]
        out = []
        for p in pieces(sc, 3):
            p = jnp.where(j_mask, p.astype(F32)[None], 0.0).reshape(LANES, 384)
            out.append(mm_nt(row_hot, p.astype(BF16)))
        r = start_row + a
        off = ((g == 0) & (r < 3)) | ((g == G - 1) & (r >= ROWS + 3)) | off_side
        scale_own[a] = jnp.where(off, 0.0, total(out))
    for a in range(4):
        sscale_send[0, a] = turn(scale_own[a, :, 0:128], 32)
        sscale_send[1, a] = pack_right(scale_own[a, :, 256:384], scale_own[a, :, 384:512], 80)
    for c in scale_early:
        c.start()

    loads[5].wait()
    r = iota((LANES, 64), 0)
    e_hot = onehot((r >> 7) * 16 + (r & 15) == iota((LANES, 64), 1))
    left = mm(e_hot, em_ref[...]).astype(BF16)
    rr, cc = iota((LANES, LANES), 0), iota((LANES, LANES), 1)
    wide = mm_nt(left, e_hot)
    wmat[...] = jnp.where(((rr >> 4) & 7) == ((cc >> 4) & 7), wide, 0.0).astype(BF16)

    def sides_merge(rows):
        lo, hi = rows.start, rows.stop
        lane = iota((hi - lo, 8, 128), 2)
        right, left = side_recv[0, rows], side_recv[1, rows]
        st, ob = slice(UP + lo, UP + hi), slice(O_UP + lo, O_UP + hi)
        own = state[st, :, 384:512]
        own = jnp.where(lane < 32, own, jnp.where(lane < 80, right, left))
        state[st, :, 0:128], state[st, :, 384:512] = fill(state[st, :, 0:128], own)
        both = jnp.where(lane < 80, left, right)
        oi[ob, :, 384:512] = jnp.where(
            lane < 32,
            oi[ob, :, 384:512],
            jnp.where(lane < 80, turn(both, -48), turn(both, 48)),
        )

    def sides_merge_scale():
        lane = iota((16, 128), 1)
        for a in range(4):
            scale_own[a, :, 384:512] = jnp.where(
                lane < 32,
                scale_own[a, :, 384:512],
                jnp.where(lane < 80, sscale_recv[0, a], sscale_recv[1, a]),
            )

    def fill(first, three):
        lane = iota(first.shape, first.ndim - 1)
        ahead = turn(three, 6)
        first_new = jnp.where(lane < 3, ahead, first)
        three_new = jnp.where((lane >= 32) & (lane < 35), ahead, three)
        three_new = jnp.where((lane >= 29) & (lane < 32), turn(three, -6), three_new)
        three_new = jnp.where(lane >= 125, turn(first, -6), three_new)
        return first_new, three_new

    def fill_arrived(lo, hi):
        v = state[lo:hi, :, 0:128]
        lane = iota(v.shape, 2)
        state[lo:hi, :, 0:128] = jnp.where(lane < 3, turn(state[lo:hi, :, 384:512], 6), v)

    def scale_row(a, e, cols):
        if e < 5:
            v = scale_up[a, e : e + 1, cols]
        elif e < 18:
            v = scale_own[a, e - 5 : e - 4, cols]
        else:
            v = scale_down[a, e - 18 : e - 17, cols]
        return jnp.broadcast_to(v, (8, 128))

    def products(t, elems, rows, begun=()):
        src = states[t % 2]
        for q in range(4):
            cols = slice(128 * q, 128 * q + 128)
            parts = []
            for a in range(4):
                v = [src[UP + STARTS[e] + a, :, cols] * scale_row(a, e, cols) for e in elems]
                parts.append(jnp.concatenate(v, axis=0).astype(BF16))
            o = mm(jnp.concatenate(parts, axis=1), wmat[...])
            for row in rows:
                terms = [
                    o[8 * n : 8 * n + 8, 128 * a : 128 * a + 128]
                    for n, e in enumerate(elems)
                    for a in range(4)
                    if STARTS[e] + a == row and block_of(e) == owner(row)
                ]
                if row in begun:
                    terms.append(asm[O_UP + row, :, cols])
                asm[O_UP + row, :, cols] = total(terms)

    def update(t, first, last):
        dst = states[(t + 1) % 2]
        step = 4
        for r0 in range(first, last, step):
            n = min(step, last - r0)
            lane = iota((n, 8, 128), 2)
            low = lane & 15
            a0 = O_UP + r0
            tiles = [asm[a0 : a0 + n, :, 128 * q : 128 * q + 128] for q in range(4)]
            ahead = [turn(v, 1) for v in tiles]
            back = [turn(v, -1) for v in tiles]
            new = []
            for q in range(4):
                before = jnp.where(lane == 0, ahead[(q + 3) % 4], ahead[q])
                after = jnp.where(lane == 127, back[(q + 1) % 4], back[q])
                more = jnp.where(low == 0, before, jnp.where(low == 15, after, 0.0))
                if q == 3:
                    pair = jnp.where(lane >= 96, lane - 96, lane)
                    more = jnp.where((pair == 14) | (pair == 15), turn(tiles[3], -2), more)
                    more = jnp.where((pair == 16) | (pair == 17), turn(tiles[3], 2), more)
                cols = slice(128 * q, 128 * q + 128)
                rhs = oi[a0 : a0 + n, :, cols]
                inv = jnp.broadcast_to(oi[a0 : a0 + n, COMP : COMP + 1, cols], (n, 8, 128))
                new.append(rhs - (tiles[q] + more) * inv)
            if t < 3:
                new[0], new[3] = fill(new[0], new[3])
            for q in range(4):
                dst[UP + r0 : UP + r0 + n, :, 128 * q : 128 * q + 128] = new[q]

    def sweep(t):
        products(t, range(*ACTIVE[t]), range(*UPDATED[t]))
        update(t, *UPDATED[t])

    INNER = range(6, 16)

    def sweep_0_inner():
        products(0, INNER, range(0, 31))
        update(0, 1, 30)

    def sweep_0_outer():
        rows = [r for r in range(*UPDATED[0]) if r < 1 or r > 29]
        products(0, [e for e in range(*ACTIVE[0]) if e not in INNER], rows, (0, 30))
        update(0, UPDATED[0][0], 1)
        update(0, 30, UPDATED[0][1])


    CH = 512
    for c in loads[6:]:
        c.wait()
    node = node_ref[...]
    node_row = lax.div(node, jnp.int32(COLS))
    e_col = node - node_row * COLS + 3
    e_lane = jnp.where(e_col < 375, e_col + lax.div(e_col, jnp.int32(15)), e_col + 26)

    def setup_rows():
        live = iota((1, IF_CAP), 1) < count_ref[...]
        dest = jnp.where(live, dest_ref[...], -1)
        tri = onehot(iota((256, 256), 0) < iota((256, 256), 1))
        carry = jnp.zeros((D, 1), F32)
        for b in range(IF_CAP // 256):
            cols = slice(256 * b, 256 * b + 256)
            hot = jnp.where(dest[:, cols] == iota((D, 256), 0), 1.0, 0.0)
            desthot[:, cols] = hot.astype(BF16)
            before = mm(hot.astype(BF16), tri) + carry
            slot_s[:, cols] = jnp.sum(before * hot, axis=0, keepdims=True)
            carry = carry + jnp.sum(hot, axis=1, keepdims=True)
        name = jnp.zeros((D, 128), F32)
        for b in range(IF_CAP // CH):
            cols = slice(CH * b, CH * b + CH)
            colhot[:, cols] = onehot(e_lane[:, cols] == iota((LANES, CH), 0))
            slots = slot_s[:, cols].astype(jnp.int32) + 96 == iota((128, CH), 0)
            for p in pieces(target_ref[:, cols].astype(F32), 2):
                p = jnp.where(slots, p.astype(F32), 0.0).astype(BF16)
                name = name + mm_nt(desthot[:, cols], p)
        names[...] = name

    def tractions(t):
        lane = iota((1, 256), 1)
        trac = []
        for k in range(3):
            row = jnp.zeros((1, 256), F32)
            for c in range(COMP):
                row = jnp.where((lane & 7) == c, tm_ref[k : k + 1, c : c + 1], row)
            trac.append(jnp.where((iota((32, 256), 1) >> 3) == iota((32, 256), 0), row, 0.0))
        high, low = pieces(jnp.concatenate(trac, axis=0), 2)
        own = state[UP : UP + ROWS].reshape(ROWS * 8, LANES)
        own_high, own_low = pieces(own, 2)
        field = mm(high, own_high) + (mm(high, own_low) + mm(low, own_high))
        field_s[192 * t : 192 * t + 192] = jnp.concatenate(pieces(field, 2), axis=0)

    def gather():
        acc = jnp.zeros((D, 256), F32)
        for b in range(IF_CAP // CH):
            cols = slice(CH * b, CH * b + CH)
            v = mm(field_s[...], colhot[:, cols])
            v = jnp.concatenate([v[:96] + v[96:192], v[192:288] + v[288:]], axis=0)
            v = v.reshape(6, 32, CH)
            v = jnp.where(node_row[:, cols][None] == iota((1, 32, CH), 1), v, 0.0)
            v = jnp.sum(v, axis=1, keepdims=True)
            slots = slot_s[:, cols].astype(jnp.int32)[None] == iota((1, CAP, CH), 1)
            none = jnp.zeros((CAP, CH), BF16)
            for p in pieces(v, 2):
                p = jnp.where(slots, p.astype(F32), 0.0).astype(BF16).reshape(2, 3 * CAP, CH)
                p = jnp.concatenate([p[0], none, p[1], none], axis=0)
                acc = acc + mm_nt(desthot[:, cols], p)
        abuf[:, 0, :] = acc[:, 0:128] + names[...]
        abuf[:, 1, :] = acc[:, 128:256]

    def all_to_all():
        for n, (to_g, to_s) in enumerate(others):
            pltpu.make_async_remote_copy(
                src_ref=abuf.at[to_g * S + to_s],
                dst_ref=arrived.at[n + 1],
                send_sem=all_send,
                recv_sem=all_recv,
                device_id=(to_g, to_s),
                device_id_type=MESH,
            ).start()
        arrived[0] = abuf[g * S + s]
        return pltpu.make_async_remote_copy(
            src_ref=abuf.at[0 : D - 1],
            dst_ref=arrived.at[1:D],
            send_sem=all_send,
            recv_sem=all_recv,
            device_id=others[0],
            device_id_type=MESH,
        )

    def place():
        got = [arrived[:, t, :].T for t in range(ITERS)]
        name = got[0][96:128]
        high = jnp.floor(name * (1.0 / 128.0))
        low = name - 128.0 * high
        upper = [v.astype(BF16).astype(F32) for v in got]
        lower = [v - u for v, u in zip(got, upper)]
        acc = jnp.zeros((192, 128), F32)
        for q in range(CAP // 4):
            left, right = [], []
            for z in range(4 * q, 4 * q + 4):
                right.append(onehot(low[z : z + 1] == iota((128, D), 0).astype(F32)))
                hit = high[z : z + 1] == iota((16, D), 0).astype(F32)
                v = [
                    jnp.where(hit, part[t][32 * k + z : 32 * k + z + 1], 0.0)
                    for part in (upper, lower)
                    for t in range(ITERS)
                    for k in range(3)
                ]
                left.append(jnp.concatenate(v, axis=0).astype(BF16))
            acc = acc + mm_nt(jnp.concatenate(left, axis=1), jnp.concatenate(right, axis=1))
        acc = acc[:96] + acc[96:]
        for t in range(ITERS):
            for k in range(3):
                for h in range(16):
                    n = (3 * t + k) * 16 + h
                    load_ref[k, t : t + 1, 128 * h : 128 * h + 128] = acc[n : n + 1]

    def write_adjoint():
        own = state[UP : UP + ROWS].reshape(ROWS * 8, LANES)
        lane = iota((LANES, COLS), 0)
        j, b = lane >> 4, lane & 15
        keep = ((j < 25) & (b < 15)) | ((j == 25) & (b > 0))
        back = onehot(keep & (ext_col(lane) == iota((LANES, COLS), 1) + 3))
        n = iota((COMP * ROWS, ROWS * 8), 1)
        unperm = onehot((n & 7) * ROWS + (n >> 3) == iota((COMP * ROWS, ROWS * 8), 0))
        out_ref[...] = pick_rows(unperm, pick(own, back)).reshape(COMP, ROWS, COLS)

    setup_rows()
    for c in side_edges:
        c.wait_recv()
    for rows in edges:
        sides_merge(rows)
    sides_merge_scale()
    row_late = state_rows(16, last_tile) + oi_rows(18, last_tile) + scale_rows(20, last_tile)
    for c in row_late:
        c.start()
    pl.semaphore_wait(know_x, len(line_x))
    for t in line_y:
        pl.semaphore_signal(know_y, inc=1, device_id=t, device_id_type=MESH)
    for c in side_middle:
        c.wait_recv()
    sides_merge(middle)
    sweep_0_inner()
    for c in row_early + row_late:
        c.wait_recv()
    fill_arrived(0, UP)
    fill_arrived(UP + ROWS, UP + ROWS + DOWN)
    sweep_0_outer()
    for c in side_edges + side_middle + row_early + row_late:
        c.wait_send()
    sweep(1)
    tractions(0)
    sweep(2)
    sweep(3)
    tractions(1)
    gather()
    pl.semaphore_wait(know_y, len(line_y))
    exchange = all_to_all()
    write_adjoint()
    out_copy = pltpu.make_async_copy(out_ref, out_hbm, out_sem.at[0])
    out_copy.start()
    exchange.wait_recv()
    place()
    load_copy = pltpu.make_async_copy(load_ref, load_hbm, out_sem.at[1])
    load_copy.start()
    exchange.wait_send()
    out_copy.wait()
    load_copy.wait()


def on_device(
    G,
    S,
    adjoint_start,
    objective_grad,
    diagonal,
    connect,
    element_scale,
    element_matrix,
    traction_map,
    iface_node,
    iface_dest,
    iface_target,
    iface_count,
):
    hbm = pl.BlockSpec(memory_space=pl.ANY)
    D = G * S
    dma = pltpu.SemaphoreType.DMA
    I32 = jnp.int32
    scratch = [
        pltpu.VMEM((COMP, ROWS, COLS), F32),
        pltpu.VMEM((3, ITERS, IF_CAP), F32),
        dma((2,)),
        pltpu.VMEM((COMP, ROWS, COLS), F32),
        pltpu.VMEM((COMP, ROWS, COLS), F32),
        pltpu.VMEM((ROWS, COLS), F32),
        pltpu.VMEM((8, ELEMS), I32),
        pltpu.VMEM((64, ELEMS), F32),
        pltpu.VMEM((64, 64), BF16),
        pltpu.VMEM((3, COMP), F32),
        pltpu.VMEM((1, IF_CAP), I32),
        pltpu.VMEM((1, IF_CAP), I32),
        pltpu.VMEM((1, IF_CAP), I32),
        pltpu.VMEM((1, 1), I32),
        dma((11,)),
        pltpu.VMEM((UP + ROWS + DOWN, 8, LANES), F32),
        pltpu.VMEM((UP + ROWS + DOWN, 8, LANES), F32),
        pltpu.VMEM((ITERS * 192, LANES), BF16),
        pltpu.VMEM((O_UP + ROWS + O_DOWN, 8, LANES), F32),
        pltpu.VMEM((O_UP + ROWS + O_DOWN, 8, LANES), F32),
        pltpu.VMEM((4, 16, LANES), F32),
        pltpu.VMEM((4, 8, LANES), F32),
        pltpu.VMEM((4, 8, LANES), F32),
        pltpu.VMEM((LANES, LANES), BF16),
        pltpu.VMEM((8, 384), I32),
        pltpu.VMEM((64, 384), F32),
        pltpu.VMEM((LANES, IF_CAP), BF16),
        pltpu.VMEM((D, IF_CAP), BF16),
        pltpu.VMEM((1, IF_CAP), F32),
        pltpu.VMEM((D, 128), F32),
        pltpu.VMEM((UP + DOWN, 8, 128), F32),
        pltpu.SemaphoreType.REGULAR,
        pltpu.SemaphoreType.REGULAR,
        pltpu.VMEM((2, ROWS, 8, 128), F32),
        pltpu.VMEM((2, ROWS, 8, 128), F32),
        pltpu.VMEM((2, 4, 16, 128), F32),
        pltpu.VMEM((2, 4, 16, 128), F32),
        pltpu.VMEM((D, ITERS, 128), F32),
        pltpu.VMEM((D, ITERS, 128), F32),
        dma((22,)),
        dma((22,)),
        dma,
        dma,
    ]
    call = pl.pallas_call(
        functools.partial(kernel, G, S),
        out_shape=(
            jax.ShapeDtypeStruct((COMP, ROWS, COLS), F32),
            jax.ShapeDtypeStruct((3, ITERS, IF_CAP), F32),
        ),
        in_specs=[hbm] * 11,
        out_specs=(hbm, hbm),
        scratch_shapes=scratch,
        compiler_params=pltpu.CompilerParams(
            collective_id=0, has_side_effects=True, vmem_limit_bytes=62 * 1024 * 1024
        ),
    )
    adjoint, load = call(
        adjoint_start,
        objective_grad,
        diagonal,
        connect,
        element_scale,
        element_matrix,
        traction_map,
        iface_node.reshape(1, IF_CAP),
        iface_dest.reshape(1, IF_CAP),
        iface_target.reshape(1, IF_CAP),
        iface_count.reshape(1, 1),
    )
    adjoint, load = hand_out(adjoint, load)
    return adjoint, load.transpose(1, 0, 2)


def hand_out_kernel(a, b, a_out, b_out, a_v, b_v, sem):
    parts = [(a.at[c], a_v.at[c], a_out.at[c]) for c in range(COMP)] + [(b, b_v, b_out)]
    parts = parts[-1:] + parts[:-1]
    loads = [pltpu.make_async_copy(p[0], p[1], sem.at[0, n]) for n, p in enumerate(parts)]
    stores = [pltpu.make_async_copy(p[1], p[2], sem.at[1, n]) for n, p in enumerate(parts)]
    for c in loads:
        c.start()
    for load, store in zip(loads, stores):
        load.wait()
        store.start()
    for c in stores:
        c.wait()


def hand_out(a, b):
    hbm = pl.BlockSpec(memory_space=pl.ANY)
    return pl.pallas_call(
        hand_out_kernel,
        out_shape=(jax.ShapeDtypeStruct(a.shape, F32), jax.ShapeDtypeStruct(b.shape, F32)),
        in_specs=[hbm, hbm],
        out_specs=(hbm, hbm),
        scratch_shapes=[
            pltpu.VMEM(a.shape, F32),
            pltpu.VMEM(b.shape, F32),
            pltpu.SemaphoreType.DMA((2, COMP + 1)),
        ],
        compiler_params=pltpu.CompilerParams(vmem_limit_bytes=62 * 1024 * 1024),
    )(a, b)


def solution(mesh):
    both = ("group", "sub")
    placed = (
        P(None, "group", "sub"),
        P(None, "group", "sub"),
        P("group", "sub"),
        P(None, both),
        P(None, both),
        P(),
        P(),
        P(both),
        P(both, None),
        P(both),
        P(both),
    )
    return jax.shard_map(
        functools.partial(on_device, mesh.shape["group"], mesh.shape["sub"]),
        mesh=mesh,
        in_specs=placed,
        out_specs=(P(None, "group", "sub"), P(None, None, both)),
        check_vma=False,
    )
```

```python
import functools
import jax
import jax.numpy as jnp
from jax import lax
from jax.experimental import pallas as pl
from jax.experimental.pallas import tpu as pltpu
from jax.sharding import PartitionSpec as P

COMP = 6
ROWS = 32
COLS = 384
ELEMS = 338
IF_CAP = 2048
CAP = 32
ITERS = 2
W = 8
LANES = 512
UP, DOWN = 11, 10
O_UP, O_DOWN = 8, 7
STARTS = (
    [-11, -8, -5, -2, -1] + [min(3 * i, ROWS + 2) - 3 for i in range(13)] + [29, 32, 35, 38]
)
ACTIVE = [(0, 22), (1, 21), (2, 20), (4, 18)]
UPDATED = [(-8, 39), (-5, 36), (-3, 35), (0, 32)]
F32 = jnp.float32
BF16 = jnp.bfloat16
MESH = pl.DeviceIdType.MESH
NT = (((1,), (1,)), ((), ()))


def iota(shape, dim):
    return lax.broadcasted_iota(jnp.int32, shape, dim)


def onehot(mask):
    return jnp.where(mask, 1.0, 0.0).astype(BF16)


def mm(a, b):
    return jnp.dot(a, b, preferred_element_type=F32)


def mm_nt(a, b):
    return lax.dot_general(a, b, NT, preferred_element_type=F32)


def pieces(x, n):
    out = []
    for k in range(n):
        p = x.astype(BF16)
        out.append(p)
        if k + 1 < n:
            x = x - p.astype(F32)
    return out


def total(terms):
    terms = list(terms)
    while len(terms) > 1:
        terms = [
            terms[i] + terms[i + 1] if i + 1 < len(terms) else terms[i]
            for i in range(0, len(terms), 2)
        ]
    return terms[0]


def pick(x, sel, n=3):
    return total([mm(p, sel) for p in pieces(x, n)])


def pick_rows(sel, x, n=3):
    return total([mm(sel, p) for p in pieces(x, n)])


def ext_col(lane):
    j = lane >> 4
    return jnp.where(j == 25, 374, 15 * j) + (lane & 15)


def owner(row):
    return 0 if row < 0 else (1 if row < ROWS else 2)


def block_of(e):
    return 0 if e < 5 else (1 if e < 18 else 2)


def kernel(
    G,
    S,
    adj_hbm,
    obj_hbm,
    diag_hbm,
    conn_hbm,
    scale_hbm,
    em_hbm,
    tm_hbm,
    node_hbm,
    dest_hbm,
    target_hbm,
    count_hbm,
    out_hbm,
    arrived,
    out_ref,
    out_sem,
    adj_ref,
    obj_ref,
    diag_ref,
    conn_ref,
    scale_ref,
    em_ref,
    tm_ref,
    node_ref,
    dest_ref,
    target_ref,
    count_ref,
    in_sem,
    state_a,
    state_b,
    field_s,
    oi,
    asm,
    scale_own,
    scale_up,
    scale_down,
    wmat,
    conn_pad,
    scale_pad,
    colhot,
    desthot,
    slot_s,
    slothot,
    rowhot,
    names,
    tile_0,
    know_x,
    know_y,
    side_send,
    side_recv,
    sscale_send,
    sscale_recv,
    abuf,
    halo_send,
    halo_recv,
    all_send,
    all_recv,
):
    D = G * S
    states = (state_a, state_b)
    state = state_a
    g = lax.axis_index("group")
    s = lax.axis_index("sub")

    def at(dg, ds):
        return (lax.rem(g + dg + G, G), lax.rem(s + ds + S, S))

    loads = [
        pltpu.make_async_copy(src, dst, in_sem.at[n])
        for n, (src, dst) in enumerate(
            [
                (adj_hbm, adj_ref),
                (diag_hbm, diag_ref),
                (obj_hbm, obj_ref),
                (conn_hbm.at[0:8], conn_ref),
                (scale_hbm, scale_ref),
                (em_hbm, em_ref),
                (tm_hbm, tm_ref),
                (node_hbm, node_ref),
                (dest_hbm, dest_ref),
                (target_hbm, target_ref),
                (count_hbm, count_ref),
            ]
        )
    ]
    for c in loads:
        c.start()
    barrier = pltpu.get_barrier_semaphore()
    X, Z = S // W, W // 2
    x, z, core = s // W, lax.rem(s, W) // 2, lax.rem(s, 2)

    def hops(offset):
        dg, dx, dz, dc = offset
        steps = [min(dg, G - dg), min(dx, X - dx), min(dz, Z - dz)]
        return (sum(n > 0 for n in steps), sum(steps), dc)

    offsets = [
        (dg, dx, dz, dc) for dz in range(Z) for dx in range(X) for dg in range(G) for dc in range(2)
    ]
    others = [
        (
            lax.rem(g + dg, G),
            (lax.rem(x + dx, X) * Z + lax.rem(z + dz, Z)) * 2 + lax.rem(core + dc, 2),
        )
        for dg, dx, dz, dc in sorted(offsets[1:], key=hops, reverse=True)
    ]
    here = s % W
    line_w = [(g, s - here + lax.rem(here + n, W)) for n in range(1, W)]
    line_x = [at(0, W * n) for n in range(1, S // W)]
    line_y = [at(n, 0) for n in range(1, G)]
    near = line_y + [at(0, -1), at(0, 1)] + line_w + line_x
    for t in near:
        pl.semaphore_signal(barrier, inc=1, device_id=t, device_id_type=MESH)

    lane = iota((COLS, LANES), 1)
    sel = onehot((ext_col(lane) == iota((COLS, LANES), 0) + 3) & (lane < 416))
    m = iota((ROWS * 8, COMP * ROWS), 0)
    perm = onehot(((m & 7) * ROWS + (m >> 3) == iota((ROWS * 8, COMP * ROWS), 1)) & ((m & 7) < COMP))
    loads[0].wait()
    first = pick_rows(perm, adj_ref[...].reshape(COMP * ROWS, COLS))
    state[UP : UP + ROWS] = pick(first, sel).reshape(ROWS, 8, LANES)

    loads[1].wait()
    loads[2].wait()
    inverse = 1.0 / diag_ref[...]
    scaled_obj = (obj_ref[...] * inverse[None]).reshape(COMP * ROWS, COLS)
    m = iota((ROWS * 8, ROWS), 0)
    perm_inv = onehot(((m & 7) == COMP) & ((m >> 3) == iota((ROWS * 8, ROWS), 1)))
    first = pick_rows(perm, scaled_obj, 2) + pick_rows(perm_inv, inverse, 2)
    oi[O_UP : O_UP + ROWS] = pick(first, sel, 2).reshape(ROWS, 8, LANES)

    def remote(n, src, dst, dev):
        return pltpu.make_async_remote_copy(
            src_ref=src,
            dst_ref=dst,
            send_sem=halo_send.at[n],
            recv_sem=halo_recv.at[n],
            device_id=dev,
            device_id_type=MESH,
        )

    def turn(v, n):
        return pltpu.roll(v, n % 128, v.ndim - 1)

    def pack_right(two, three, start):
        lane = iota(two.shape, two.ndim - 1)
        return jnp.where(lane < start + 16, turn(two, start - 112), turn(three, start + 16))

    for p in range(0, ROWS, 8):
        st = [state[UP + p : UP + p + 8, :, 128 * q : 128 * q + 128] for q in (0, 2, 3)]
        ob = [oi[O_UP + p : O_UP + p + 8, :, 128 * q : 128 * q + 128] for q in (0, 2, 3)]
        lane = iota((8, 8, 128), 2)
        side_send[0, p : p + 8] = jnp.where(lane < 80, turn(st[0], 32), turn(ob[0], 80))
        side_send[1, p : p + 8] = jnp.where(
            lane < 80, pack_right(ob[1], ob[2], 32), pack_right(st[1], st[2], 80)
        )
    def pair(n, ref, up_to, down_rows, up_rows, cols):
        lo, hi = down_rows
        first, last = up_rows
        return [
            remote(n, ref.at[lo:hi, :, cols], ref.at[0 : hi - lo, :, cols], at(1, 0)),
            remote(
                n + 1,
                ref.at[first:last, :, cols],
                ref.at[up_to : up_to + last - first, :, cols],
                at(-1, 0),
            ),
        ]

    def state_rows(n, cols):
        return pair(n, state, UP + ROWS, (ROWS, UP + ROWS), (UP, UP + DOWN), cols)

    def oi_rows(n, cols):
        return pair(
            n, oi, O_UP + ROWS, (ROWS, O_UP + ROWS), (O_UP, O_UP + O_DOWN), cols
        )

    def scale_rows(n, cols):
        return [
            remote(n, scale_own.at[:, 8:16, cols], scale_up.at[:, :, cols], at(1, 0)),
            remote(n + 1, scale_own.at[:, 0:8, cols], scale_down.at[:, :, cols], at(-1, 0)),
        ]

    pl.semaphore_wait(barrier, len(near))
    edges = (slice(0, DOWN), slice(ROWS - UP, ROWS))
    middle = slice(DOWN, ROWS - UP)
    sides = (at(0, -1), at(0, 1))

    def side_rows(n, rows):
        return [
            remote(n + k, side_send.at[k, rows], side_recv.at[k, rows], sides[k]) for k in range(2)
        ]

    side_edges = side_rows(0, edges[0]) + side_rows(2, edges[1])
    side_edges += [remote(4 + k, sscale_send.at[k], sscale_recv.at[k], sides[k]) for k in range(2)]
    side_middle = side_rows(6, middle)
    tile_0[0:UP] = state[ROWS : UP + ROWS, :, 0:128]
    tile_0[UP:] = state[UP : UP + DOWN, :, 0:128]
    early, last_tile = slice(0, 384), slice(384, 512)
    row_early = state_rows(8, slice(128, 384)) + oi_rows(10, early) + scale_rows(12, early)
    row_early += [
        remote(14, tile_0.at[0:UP], state.at[0:UP, :, 0:128], at(1, 0)),
        remote(15, tile_0.at[UP:], state.at[UP + ROWS :, :, 0:128], at(-1, 0)),
    ]
    scale_early = side_edges[4:] + row_early[4:6]
    for c in side_edges[:4] + row_early[:4] + row_early[6:] + side_middle:
        c.start()
    for t in line_x:
        pl.semaphore_signal(know_x, inc=1, device_id=t, device_id_type=MESH)

    loads[3].wait()
    loads[4].wait()
    conn_pad[...] = jnp.full_like(conn_pad, -1)
    conn_pad[:, 0:ELEMS] = conn_ref[...]
    scale_pad[...] = jnp.zeros_like(scale_pad)
    scale_pad[:, 0:ELEMS] = scale_ref[...]
    node0 = conn_pad[0:1]
    row0 = lax.div(node0, jnp.int32(390))
    col0 = node0 - row0 * 390
    elem_i = jnp.where(node0 >= 0, lax.div(row0 + 2, jnp.int32(3)), -1)
    elem_j = jnp.where(node0 >= 0, lax.div(col0 + 14, jnp.int32(15)), -1)
    row_hot = onehot(elem_i == iota((16, 384), 0))
    start_row = jnp.minimum(3 * iota((16, LANES), 0), ROWS + 2)
    lane = iota((16, LANES), 1)
    off_side = ((s == 0) & (lane < 3)) | ((s == S - 1) & (lane >= 413))
    j_mask = elem_j[:, None, :] == iota((32, 16, 384), 0)
    for a in range(4):
        sc = scale_pad[16 * a : 16 * a + 16]
        out = []
        for p in pieces(sc, 3):
            p = jnp.where(j_mask, p.astype(F32)[None], 0.0).reshape(LANES, 384)
            out.append(mm_nt(row_hot, p.astype(BF16)))
        r = start_row + a
        off = ((g == 0) & (r < 3)) | ((g == G - 1) & (r >= ROWS + 3)) | off_side
        scale_own[a] = jnp.where(off, 0.0, total(out))
    for a in range(4):
        sscale_send[0, a] = turn(scale_own[a, :, 0:128], 32)
        sscale_send[1, a] = pack_right(scale_own[a, :, 256:384], scale_own[a, :, 384:512], 80)
    for c in scale_early:
        c.start()

    loads[5].wait()
    r, n = iota((LANES, 64), 0), iota((LANES, 64), 1)
    r_b, r_a = r & 15, (r >> 7) * 16
    left = mm(onehot(r_a + r_b == n), em_ref[...]).astype(BF16)

    def columns(mask):
        return mm_nt(left, onehot(mask))

    rr, cc = (iota((LANES, LANES), 0) >> 4) & 7, (iota((LANES, LANES), 1) >> 4) & 7
    same = jnp.where(rr == cc, columns(r_a + r_b == n), 0.0)
    after, before = rr == cc - 1, rr == cc + 1
    one_after = jnp.where(after, columns((r_a + 15 == n) & (r_b == 0)), 0.0)
    one_before = jnp.where(before, columns((r_a == n) & (r_b == 15)), 0.0)
    two_after = jnp.where(after, columns((r_a + r_b + 14 == n) & (r_b < 2)), 0.0)
    two_before = jnp.where(before, columns((r_a + r_b - 14 == n) & (r_b >= 14)), 0.0)
    wmat[0] = (same + one_after + one_before).astype(BF16)
    first, second = (cc == 0) | (cc == 6), (cc == 1) | (cc == 7)
    shared = jnp.where(second, two_after, one_after) + jnp.where(first, two_before, one_before)
    wmat[1] = (same + shared).astype(BF16)

    def sides_merge(rows):
        lo, hi = rows.start, rows.stop
        lane = iota((hi - lo, 8, 128), 2)
        right, left = side_recv[0, rows], side_recv[1, rows]
        st, ob = slice(UP + lo, UP + hi), slice(O_UP + lo, O_UP + hi)
        own = state[st, :, 384:512]
        own = jnp.where(lane < 32, own, jnp.where(lane < 80, right, left))
        state[st, :, 0:128], state[st, :, 384:512] = fill(state[st, :, 0:128], own)
        both = jnp.where(lane < 80, left, right)
        oi[ob, :, 384:512] = jnp.where(
            lane < 32,
            oi[ob, :, 384:512],
            jnp.where(lane < 80, turn(both, -48), turn(both, 48)),
        )

    def sides_merge_scale():
        lane = iota((16, 128), 1)
        for a in range(4):
            scale_own[a, :, 384:512] = jnp.where(
                lane < 32,
                scale_own[a, :, 384:512],
                jnp.where(lane < 80, sscale_recv[0, a], sscale_recv[1, a]),
            )

    def fill(first, three):
        lane = iota(first.shape, first.ndim - 1)
        ahead = turn(three, 6)
        first_new = jnp.where(lane < 3, ahead, first)
        three_new = jnp.where((lane >= 32) & (lane < 35), ahead, three)
        three_new = jnp.where((lane >= 29) & (lane < 32), turn(three, -6), three_new)
        three_new = jnp.where(lane >= 125, turn(first, -6), three_new)
        return first_new, three_new

    def fill_arrived(lo, hi):
        v = state[lo:hi, :, 0:128]
        lane = iota(v.shape, 2)
        state[lo:hi, :, 0:128] = jnp.where(lane < 3, turn(state[lo:hi, :, 384:512], 6), v)

    def scale_row(a, e, cols):
        if e < 5:
            v = scale_up[a, e : e + 1, cols]
        elif e < 18:
            v = scale_own[a, e - 5 : e - 4, cols]
        else:
            v = scale_down[a, e - 18 : e - 17, cols]
        return jnp.broadcast_to(v, (8, 128))

    def products(t, elems, rows, begun=()):
        src = states[t % 2]
        for q in range(4):
            cols = slice(128 * q, 128 * q + 128)
            parts = []
            for a in range(4):
                v = [src[UP + STARTS[e] + a, :, cols] * scale_row(a, e, cols) for e in elems]
                parts.append(jnp.concatenate(v, axis=0).astype(BF16))
            o = mm(jnp.concatenate(parts, axis=1), wmat[q // 3])
            for row in rows:
                terms = [
                    o[8 * n : 8 * n + 8, 128 * a : 128 * a + 128]
                    for n, e in enumerate(elems)
                    for a in range(4)
                    if STARTS[e] + a == row and block_of(e) == owner(row)
                ]
                if row in begun:
                    terms.append(asm[O_UP + row, :, cols])
                asm[O_UP + row, :, cols] = total(terms)

    def update(t, first, last):
        dst = states[(t + 1) % 2]
        step = 4
        for r0 in range(first, last, step):
            n = min(step, last - r0)
            lane = iota((n, 8, 128), 2)
            a0 = O_UP + r0
            tiles = [asm[a0 : a0 + n, :, 128 * q : 128 * q + 128] for q in range(4)]
            ahead = [turn(v, 1) for v in tiles]
            back = [turn(v, -1) for v in tiles]
            new = []
            for q in range(4):
                more = jnp.where(
                    lane == 0,
                    ahead[(q + 3) % 4],
                    jnp.where(lane == 127, back[(q + 1) % 4], 0.0),
                )
                cols = slice(128 * q, 128 * q + 128)
                rhs = oi[a0 : a0 + n, :, cols]
                inv = jnp.broadcast_to(oi[a0 : a0 + n, COMP : COMP + 1, cols], (n, 8, 128))
                new.append(rhs - (tiles[q] + more) * inv)
            if t < 3:
                new[0], new[3] = fill(new[0], new[3])
            for q in range(4):
                dst[UP + r0 : UP + r0 + n, :, 128 * q : 128 * q + 128] = new[q]

    def sweep(t):
        products(t, range(*ACTIVE[t]), range(*UPDATED[t]))
        update(t, *UPDATED[t])

    INNER = range(6, 16)

    def sweep_0_inner():
        products(0, INNER, range(0, 31))
        update(0, 1, 30)

    def sweep_0_outer():
        rows = [r for r in range(*UPDATED[0]) if r < 1 or r > 29]
        products(0, [e for e in range(*ACTIVE[0]) if e not in INNER], rows, (0, 30))
        update(0, UPDATED[0][0], 1)
        update(0, 30, UPDATED[0][1])


    CH = 512
    for c in loads[6:]:
        c.wait()
    node = node_ref[...]
    node_row = lax.div(node, jnp.int32(COLS))
    e_col = node - node_row * COLS + 3
    e_lane = jnp.where(e_col < 375, e_col + lax.div(e_col, jnp.int32(15)), e_col + 26)

    def setup_rows():
        live = iota((1, IF_CAP), 1) < count_ref[...]
        dest = jnp.where(live, dest_ref[...], -1)
        tri = onehot(iota((256, 256), 0) < iota((256, 256), 1))
        carry = jnp.zeros((D, 1), F32)
        for b in range(IF_CAP // 256):
            cols = slice(256 * b, 256 * b + 256)
            hot = jnp.where(dest[:, cols] == iota((D, 256), 0), 1.0, 0.0)
            desthot[:, cols] = hot.astype(BF16)
            before = mm(hot.astype(BF16), tri) + carry
            slot_s[:, cols] = jnp.sum(before * hot, axis=0, keepdims=True)
            carry = carry + jnp.sum(hot, axis=1, keepdims=True)
        name = jnp.zeros((D, 128), F32)
        for b in range(IF_CAP // CH):
            cols = slice(CH * b, CH * b + CH)
            colhot[:, cols] = onehot(e_lane[:, cols] == iota((LANES, CH), 0))
            slots = slot_s[:, cols].astype(jnp.int32) + 96 == iota((128, CH), 0)
            slothot[:, cols] = onehot(slot_s[:, cols].astype(jnp.int32) == iota((CAP, CH), 0))
            rowhot[:, cols] = jnp.where(node_row[:, cols] == iota((32, CH), 0), 1.0, 0.0)
            for p in pieces(target_ref[:, cols].astype(F32), 2):
                p = jnp.where(slots, p.astype(F32), 0.0).astype(BF16)
                name = name + mm_nt(desthot[:, cols], p)
        names[...] = name

    def tractions(t):
        lane = iota((1, 256), 1)
        trac = []
        for k in range(3):
            row = jnp.zeros((1, 256), F32)
            for c in range(COMP):
                row = jnp.where((lane & 7) == c, tm_ref[k : k + 1, c : c + 1], row)
            trac.append(jnp.where((iota((32, 256), 1) >> 3) == iota((32, 256), 0), row, 0.0))
        high, low = pieces(jnp.concatenate(trac, axis=0), 2)
        own = state[UP : UP + ROWS].reshape(ROWS * 8, LANES)
        own_high, own_low = pieces(own, 2)
        field = mm(high, own_high) + (mm(high, own_low) + mm(low, own_high))
        field_s[192 * t : 192 * t + 192] = jnp.concatenate(pieces(field, 2), axis=0)

    def gather():
        acc = jnp.zeros((D, 256), F32)
        for b in range(IF_CAP // CH):
            cols = slice(CH * b, CH * b + CH)
            v = mm(field_s[...], colhot[:, cols])
            v = jnp.concatenate([v[:96] + v[96:192], v[192:288] + v[288:]], axis=0)
            v = v.reshape(6, 32, CH) * rowhot[:, cols][None]
            v = jnp.sum(v, axis=1, keepdims=True)
            none = jnp.zeros((CAP, CH), BF16)
            for p in pieces(v, 2):
                p = jnp.broadcast_to(p.astype(F32), (6, CAP, CH)).astype(BF16)
                p = (p * slothot[:, cols][None]).reshape(2, 3 * CAP, CH)
                p = jnp.concatenate([p[0], none, p[1], none], axis=0)
                acc = acc + mm_nt(desthot[:, cols], p)
        abuf[:, 0, :] = acc[:, 0:128] + names[...]
        abuf[:, 1, :] = acc[:, 128:256]

    def all_to_all():
        for n, (to_g, to_s) in enumerate(others):
            pltpu.make_async_remote_copy(
                src_ref=abuf.at[to_g * S + to_s],
                dst_ref=arrived.at[n + 1],
                send_sem=all_send,
                recv_sem=all_recv,
                device_id=(to_g, to_s),
                device_id_type=MESH,
            ).start()
        own = pltpu.make_async_copy(abuf.at[g * S + s], arrived.at[0], out_sem.at[1])
        own.start()
        return own, pltpu.make_async_remote_copy(
            src_ref=abuf.at[0 : D - 1],
            dst_ref=arrived.at[1:D],
            send_sem=all_send,
            recv_sem=all_recv,
            device_id=others[0],
            device_id_type=MESH,
        )

    def write_adjoint():
        own = state[UP : UP + ROWS].reshape(ROWS * 8, LANES)
        lane = iota((LANES, COLS), 0)
        j, b = lane >> 4, lane & 15
        keep = ((j < 25) & (b < 15)) | ((j == 25) & (b > 0))
        back = onehot(keep & (ext_col(lane) == iota((LANES, COLS), 1) + 3))
        n = iota((COMP * ROWS, ROWS * 8), 1)
        unperm = onehot((n & 7) * ROWS + (n >> 3) == iota((COMP * ROWS, ROWS * 8), 0))
        out_ref[...] = pick_rows(unperm, pick(own, back)).reshape(COMP, ROWS, COLS)

    setup_rows()
    for c in side_edges:
        c.wait_recv()
    for rows in edges:
        sides_merge(rows)
    sides_merge_scale()
    row_late = state_rows(16, last_tile) + oi_rows(18, last_tile) + scale_rows(20, last_tile)
    for c in row_late:
        c.start()
    pl.semaphore_wait(know_x, len(line_x))
    for t in line_y:
        pl.semaphore_signal(know_y, inc=1, device_id=t, device_id_type=MESH)
    for c in side_middle:
        c.wait_recv()
    sides_merge(middle)
    sweep_0_inner()
    for c in row_early + row_late:
        c.wait_recv()
    fill_arrived(0, UP)
    fill_arrived(UP + ROWS, UP + ROWS + DOWN)
    sweep_0_outer()
    for c in side_edges + side_middle + row_early + row_late:
        c.wait_send()
    sweep(1)
    tractions(0)
    sweep(2)
    sweep(3)
    tractions(1)
    gather()
    pl.semaphore_wait(know_y, len(line_y))
    own, exchange = all_to_all()
    write_adjoint()
    out_copy = pltpu.make_async_copy(out_ref, out_hbm, out_sem.at[0])
    out_copy.start()
    exchange.wait_recv()
    own.wait()
    exchange.wait_send()
    out_copy.wait()


def on_device(
    G,
    S,
    adjoint_start,
    objective_grad,
    diagonal,
    connect,
    element_scale,
    element_matrix,
    traction_map,
    iface_node,
    iface_dest,
    iface_target,
    iface_count,
):
    hbm = pl.BlockSpec(memory_space=pl.ANY)
    D = G * S
    dma = pltpu.SemaphoreType.DMA
    I32 = jnp.int32
    scratch = [
        pltpu.VMEM((COMP, ROWS, COLS), F32),
        dma((2,)),
        pltpu.VMEM((COMP, ROWS, COLS), F32),
        pltpu.VMEM((COMP, ROWS, COLS), F32),
        pltpu.VMEM((ROWS, COLS), F32),
        pltpu.VMEM((8, ELEMS), I32),
        pltpu.VMEM((64, ELEMS), F32),
        pltpu.VMEM((64, 64), BF16),
        pltpu.VMEM((3, COMP), F32),
        pltpu.VMEM((1, IF_CAP), I32),
        pltpu.VMEM((1, IF_CAP), I32),
        pltpu.VMEM((1, IF_CAP), I32),
        pltpu.VMEM((1, 1), I32),
        dma((11,)),
        pltpu.VMEM((UP + ROWS + DOWN, 8, LANES), F32),
        pltpu.VMEM((UP + ROWS + DOWN, 8, LANES), F32),
        pltpu.VMEM((ITERS * 192, LANES), BF16),
        pltpu.VMEM((O_UP + ROWS + O_DOWN, 8, LANES), F32),
        pltpu.VMEM((O_UP + ROWS + O_DOWN, 8, LANES), F32),
        pltpu.VMEM((4, 16, LANES), F32),
        pltpu.VMEM((4, 8, LANES), F32),
        pltpu.VMEM((4, 8, LANES), F32),
        pltpu.VMEM((2, LANES, LANES), BF16),
        pltpu.VMEM((8, 384), I32),
        pltpu.VMEM((64, 384), F32),
        pltpu.VMEM((LANES, IF_CAP), BF16),
        pltpu.VMEM((D, IF_CAP), BF16),
        pltpu.VMEM((1, IF_CAP), F32),
        pltpu.VMEM((CAP, IF_CAP), BF16),
        pltpu.VMEM((32, IF_CAP), F32),
        pltpu.VMEM((D, 128), F32),
        pltpu.VMEM((UP + DOWN, 8, 128), F32),
        pltpu.SemaphoreType.REGULAR,
        pltpu.SemaphoreType.REGULAR,
        pltpu.VMEM((2, ROWS, 8, 128), F32),
        pltpu.VMEM((2, ROWS, 8, 128), F32),
        pltpu.VMEM((2, 4, 16, 128), F32),
        pltpu.VMEM((2, 4, 16, 128), F32),
        pltpu.VMEM((D, ITERS, 128), F32),
        dma((22,)),
        dma((22,)),
        dma,
        dma,
    ]
    call = pl.pallas_call(
        functools.partial(kernel, G, S),
        out_shape=(
            jax.ShapeDtypeStruct((COMP, ROWS, COLS), F32),
            jax.ShapeDtypeStruct((D, ITERS, 128), F32),
        ),
        in_specs=[hbm] * 11,
        out_specs=(hbm, hbm),
        scratch_shapes=scratch,
        compiler_params=pltpu.CompilerParams(
            collective_id=0, has_side_effects=True, vmem_limit_bytes=62 * 1024 * 1024
        ),
    )
    adjoint, arrived = call(
        adjoint_start,
        objective_grad,
        diagonal,
        connect,
        element_scale,
        element_matrix,
        traction_map,
        iface_node.reshape(1, IF_CAP),
        iface_dest.reshape(1, IF_CAP),
        iface_target.reshape(1, IF_CAP),
        iface_count.reshape(1, 1),
    )
    adjoint, load = finish(adjoint, arrived)
    return adjoint, load.transpose(1, 0, 2)


def finish_kernel(adj, arr, adj_out, load_out, adj_v, arrived, load_ref, sem):
    arr_load = pltpu.make_async_copy(arr, arrived, sem.at[0])
    adj_load = pltpu.make_async_copy(adj, adj_v, sem.at[1])
    adj_store = pltpu.make_async_copy(adj_v, adj_out, sem.at[2])
    load_store = pltpu.make_async_copy(load_ref, load_out, sem.at[3])
    arr_load.start()
    adj_load.start()
    count = arr.shape[0]
    arr_load.wait()
    got = [arrived[:, t, :].T for t in range(ITERS)]
    name = got[0][96:128]
    high = jnp.floor(name * (1.0 / 128.0))
    low = name - 128.0 * high
    upper = [v.astype(BF16).astype(F32) for v in got]
    lower = [v - u for v, u in zip(got, upper)]
    acc = jnp.zeros((192, 128), F32)
    for q in range(CAP // 4):
        left, right = [], []
        for z in range(4 * q, 4 * q + 4):
            right.append(onehot(low[z : z + 1] == iota((128, count), 0).astype(F32)))
            hit = high[z : z + 1] == iota((16, count), 0).astype(F32)
            v = [
                jnp.where(hit, part[t][32 * k + z : 32 * k + z + 1], 0.0)
                for part in (upper, lower)
                for t in range(ITERS)
                for k in range(3)
            ]
            left.append(jnp.concatenate(v, axis=0).astype(BF16))
        acc = acc + mm_nt(jnp.concatenate(left, axis=1), jnp.concatenate(right, axis=1))
    acc = acc[:96] + acc[96:]
    for t in range(ITERS):
        for k in range(3):
            for h in range(16):
                n = (3 * t + k) * 16 + h
                load_ref[k, t : t + 1, 128 * h : 128 * h + 128] = acc[n : n + 1]
    load_store.start()
    adj_load.wait()
    adj_store.start()
    load_store.wait()
    adj_store.wait()


def finish(adjoint, arrived):
    hbm = pl.BlockSpec(memory_space=pl.ANY)
    load = (3, ITERS, IF_CAP)
    return pl.pallas_call(
        finish_kernel,
        out_shape=(jax.ShapeDtypeStruct(adjoint.shape, F32), jax.ShapeDtypeStruct(load, F32)),
        in_specs=[hbm, hbm],
        out_specs=(hbm, hbm),
        scratch_shapes=[
            pltpu.VMEM(adjoint.shape, F32),
            pltpu.VMEM(arrived.shape, F32),
            pltpu.VMEM(load, F32),
            pltpu.SemaphoreType.DMA((4,)),
        ],
        compiler_params=pltpu.CompilerParams(vmem_limit_bytes=62 * 1024 * 1024),
    )(adjoint, arrived)


def solution(mesh):
    both = ("group", "sub")
    placed = (
        P(None, "group", "sub"),
        P(None, "group", "sub"),
        P("group", "sub"),
        P(None, both),
        P(None, both),
        P(),
        P(),
        P(both),
        P(both, None),
        P(both),
        P(both),
    )
    return jax.shard_map(
        functools.partial(on_device, mesh.shape["group"], mesh.shape["sub"]),
        mesh=mesh,
        in_specs=placed,
        out_specs=(P(None, "group", "sub"), P(None, None, both)),
        check_vma=False,
    )
```

```python
import functools
import jax
import jax.numpy as jnp
from jax import lax
from jax.experimental import pallas as pl
from jax.experimental.pallas import tpu as pltpu
from jax.sharding import PartitionSpec as P

COMP = 6
ROWS = 32
COLS = 384
ELEMS = 338
IF_CAP = 2048
CAP = 32
ITERS = 2
W = 8
LANES = 512
UP, DOWN = 11, 10
O_UP, O_DOWN = 8, 7
STARTS = (
    [-11, -8, -5, -2, -1] + [min(3 * i, ROWS + 2) - 3 for i in range(13)] + [29, 32, 35, 38]
)
ACTIVE = [(0, 22), (1, 21), (2, 20), (4, 18)]
UPDATED = [(-8, 39), (-5, 36), (-3, 35), (0, 32)]
F32 = jnp.float32
BF16 = jnp.bfloat16
MESH = pl.DeviceIdType.MESH
NT = (((1,), (1,)), ((), ()))


def iota(shape, dim):
    return lax.broadcasted_iota(jnp.int32, shape, dim)


def onehot(mask):
    return jnp.where(mask, 1.0, 0.0).astype(BF16)


def mm(a, b):
    return jnp.dot(a, b, preferred_element_type=F32)


def mm_nt(a, b):
    return lax.dot_general(a, b, NT, preferred_element_type=F32)


def pieces(x, n):
    out = []
    for k in range(n):
        p = x.astype(BF16)
        out.append(p)
        if k + 1 < n:
            x = x - p.astype(F32)
    return out


def total(terms):
    terms = list(terms)
    while len(terms) > 1:
        terms = [
            terms[i] + terms[i + 1] if i + 1 < len(terms) else terms[i]
            for i in range(0, len(terms), 2)
        ]
    return terms[0]


def pick(x, sel, n=3):
    return total([mm(p, sel) for p in pieces(x, n)])


def pick_rows(sel, x, n=3):
    return total([mm(sel, p) for p in pieces(x, n)])


def ext_col(lane):
    j = lane >> 4
    return jnp.where(j == 25, 374, 15 * j) + (lane & 15)


def owner(row):
    return 0 if row < 0 else (1 if row < ROWS else 2)


def block_of(e):
    return 0 if e < 5 else (1 if e < 18 else 2)


def kernel(
    G,
    S,
    adj_hbm,
    obj_hbm,
    diag_hbm,
    conn_hbm,
    scale_hbm,
    em_hbm,
    tm_hbm,
    node_hbm,
    dest_hbm,
    target_hbm,
    count_hbm,
    out_hbm,
    arrived,
    out_ref,
    out_sem,
    adj_ref,
    obj_ref,
    diag_ref,
    conn_ref,
    scale_ref,
    em_ref,
    tm_ref,
    node_ref,
    dest_ref,
    target_ref,
    count_ref,
    in_sem,
    state,
    state_1,
    state_2,
    state_3,
    state_4,
    field_s,
    oi,
    asm,
    scale_own,
    scale_up,
    scale_down,
    wmat,
    conn_pad,
    scale_pad,
    colhot,
    desthot,
    slot_s,
    slothot,
    rowhot,
    names,
    tile_0,
    know_x,
    know_y,
    side_send,
    side_recv,
    sscale_send,
    sscale_recv,
    abuf,
    halo_send,
    halo_recv,
    all_send,
    all_recv,
):
    D = G * S
    states = (state, state_1, state_2, state_3, state_4)
    g = lax.axis_index("group")
    s = lax.axis_index("sub")

    def at(dg, ds):
        return (lax.rem(g + dg + G, G), lax.rem(s + ds + S, S))

    loads = [
        pltpu.make_async_copy(src, dst, in_sem.at[n])
        for n, (src, dst) in enumerate(
            [
                (adj_hbm, adj_ref),
                (diag_hbm, diag_ref),
                (obj_hbm, obj_ref),
                (conn_hbm.at[0:8], conn_ref),
                (scale_hbm, scale_ref),
                (em_hbm, em_ref),
                (tm_hbm, tm_ref),
                (node_hbm, node_ref),
                (dest_hbm, dest_ref),
                (target_hbm, target_ref),
                (count_hbm, count_ref),
            ]
        )
    ]
    for c in loads:
        c.start()
    barrier = pltpu.get_barrier_semaphore()
    X, Z = S // W, W // 2
    x, z, core = s // W, lax.rem(s, W) // 2, lax.rem(s, 2)

    def hops(offset):
        dg, dx, dz, dc = offset
        steps = [min(dg, G - dg), min(dx, X - dx), min(dz, Z - dz)]
        return (sum(n > 0 for n in steps), sum(steps), dc)

    offsets = [
        (dg, dx, dz, dc) for dz in range(Z) for dx in range(X) for dg in range(G) for dc in range(2)
    ]
    others = [
        (
            lax.rem(g + dg, G),
            (lax.rem(x + dx, X) * Z + lax.rem(z + dz, Z)) * 2 + lax.rem(core + dc, 2),
        )
        for dg, dx, dz, dc in sorted(offsets[1:], key=hops, reverse=True)
    ]
    here = s % W
    line_w = [(g, s - here + lax.rem(here + n, W)) for n in range(1, W)]
    line_x = [at(0, W * n) for n in range(1, S // W)]
    line_y = [at(n, 0) for n in range(1, G)]
    near = line_y + [at(0, -1), at(0, 1)] + line_w + line_x
    for t in near:
        pl.semaphore_signal(barrier, inc=1, device_id=t, device_id_type=MESH)

    lane = iota((COLS, LANES), 1)
    sel = onehot((ext_col(lane) == iota((COLS, LANES), 0) + 3) & (lane < 416))
    m = iota((ROWS * 8, COMP * ROWS), 0)
    perm = onehot(((m & 7) * ROWS + (m >> 3) == iota((ROWS * 8, COMP * ROWS), 1)) & ((m & 7) < COMP))
    loads[0].wait()
    first = pick_rows(perm, adj_ref[...].reshape(COMP * ROWS, COLS))
    state[UP : UP + ROWS] = pick(first, sel).reshape(ROWS, 8, LANES)

    loads[1].wait()
    loads[2].wait()
    inverse = 1.0 / diag_ref[...]
    scaled_obj = (obj_ref[...] * inverse[None]).reshape(COMP * ROWS, COLS)
    m = iota((ROWS * 8, ROWS), 0)
    perm_inv = onehot(((m & 7) == COMP) & ((m >> 3) == iota((ROWS * 8, ROWS), 1)))
    first = pick_rows(perm, scaled_obj, 2) + pick_rows(perm_inv, inverse, 2)
    oi[O_UP : O_UP + ROWS] = pick(first, sel, 2).reshape(ROWS, 8, LANES)

    def remote(n, src, dst, dev):
        return pltpu.make_async_remote_copy(
            src_ref=src,
            dst_ref=dst,
            send_sem=halo_send.at[n],
            recv_sem=halo_recv.at[n],
            device_id=dev,
            device_id_type=MESH,
        )

    def turn(v, n):
        return pltpu.roll(v, n % 128, v.ndim - 1)

    def pack_right(two, three, start):
        lane = iota(two.shape, two.ndim - 1)
        return jnp.where(lane < start + 16, turn(two, start - 112), turn(three, start + 16))

    for p in range(0, ROWS, 8):
        st = [state[UP + p : UP + p + 8, :, 128 * q : 128 * q + 128] for q in (0, 2, 3)]
        ob = [oi[O_UP + p : O_UP + p + 8, :, 128 * q : 128 * q + 128] for q in (0, 2, 3)]
        lane = iota((8, 8, 128), 2)
        side_send[0, p : p + 8] = jnp.where(lane < 80, turn(st[0], 32), turn(ob[0], 80))
        side_send[1, p : p + 8] = jnp.where(
            lane < 80, pack_right(ob[1], ob[2], 32), pack_right(st[1], st[2], 80)
        )
    def pair(n, ref, up_to, down_rows, up_rows, cols):
        lo, hi = down_rows
        first, last = up_rows
        return [
            remote(n, ref.at[lo:hi, :, cols], ref.at[0 : hi - lo, :, cols], at(1, 0)),
            remote(
                n + 1,
                ref.at[first:last, :, cols],
                ref.at[up_to : up_to + last - first, :, cols],
                at(-1, 0),
            ),
        ]

    def state_rows(n, cols):
        return pair(n, state, UP + ROWS, (ROWS, UP + ROWS), (UP, UP + DOWN), cols)

    def oi_rows(n, cols):
        return pair(
            n, oi, O_UP + ROWS, (ROWS, O_UP + ROWS), (O_UP, O_UP + O_DOWN), cols
        )

    def scale_rows(n, cols):
        return [
            remote(n, scale_own.at[:, 8:16, cols], scale_up.at[:, :, cols], at(1, 0)),
            remote(n + 1, scale_own.at[:, 0:8, cols], scale_down.at[:, :, cols], at(-1, 0)),
        ]

    pl.semaphore_wait(barrier, len(near))
    edges = (slice(0, DOWN), slice(ROWS - UP, ROWS))
    middle = slice(DOWN, ROWS - UP)
    sides = (at(0, -1), at(0, 1))

    def side_rows(n, rows):
        return [
            remote(n + k, side_send.at[k, rows], side_recv.at[k, rows], sides[k]) for k in range(2)
        ]

    side_edges = side_rows(0, edges[0]) + side_rows(2, edges[1])
    side_edges += [remote(4 + k, sscale_send.at[k], sscale_recv.at[k], sides[k]) for k in range(2)]
    side_middle = side_rows(6, middle)
    tile_0[0:UP] = state[ROWS : UP + ROWS, :, 0:128]
    tile_0[UP:] = state[UP : UP + DOWN, :, 0:128]
    early, last_tile = slice(0, 384), slice(384, 512)
    row_early = state_rows(8, slice(128, 384)) + oi_rows(10, early) + scale_rows(12, early)
    row_early += [
        remote(14, tile_0.at[0:UP], state.at[0:UP, :, 0:128], at(1, 0)),
        remote(15, tile_0.at[UP:], state.at[UP + ROWS :, :, 0:128], at(-1, 0)),
    ]
    scale_early = side_edges[4:] + row_early[4:6]
    for c in side_edges[:4] + row_early[:4] + row_early[6:]:
        c.start()
    for t in line_x:
        pl.semaphore_signal(know_x, inc=1, device_id=t, device_id_type=MESH)

    loads[3].wait()
    loads[4].wait()
    conn_pad[...] = jnp.full_like(conn_pad, -1)
    conn_pad[:, 0:ELEMS] = conn_ref[...]
    scale_pad[...] = jnp.zeros_like(scale_pad)
    scale_pad[:, 0:ELEMS] = scale_ref[...]
    node0 = conn_pad[0:1]
    row0 = lax.div(node0, jnp.int32(390))
    col0 = node0 - row0 * 390
    elem_i = jnp.where(node0 >= 0, lax.div(row0 + 2, jnp.int32(3)), -1)
    elem_j = jnp.where(node0 >= 0, lax.div(col0 + 14, jnp.int32(15)), -1)
    row_hot = onehot(elem_i == iota((16, 384), 0))
    start_row = jnp.minimum(3 * iota((16, LANES), 0), ROWS + 2)
    lane = iota((16, LANES), 1)
    off_side = ((s == 0) & (lane < 3)) | ((s == S - 1) & (lane >= 413))
    j_mask = elem_j[:, None, :] == iota((32, 16, 384), 0)
    for a in range(4):
        sc = scale_pad[16 * a : 16 * a + 16]
        out = []
        for p in pieces(sc, 3):
            p = jnp.where(j_mask, p.astype(F32)[None], 0.0).reshape(LANES, 384)
            out.append(mm_nt(row_hot, p.astype(BF16)))
        r = start_row + a
        off = ((g == 0) & (r < 3)) | ((g == G - 1) & (r >= ROWS + 3)) | off_side
        scale_own[a] = jnp.where(off, 0.0, total(out))
    for a in range(4):
        sscale_send[0, a] = turn(scale_own[a, :, 0:128], 32)
        sscale_send[1, a] = pack_right(scale_own[a, :, 256:384], scale_own[a, :, 384:512], 80)
    for c in scale_early + side_middle:
        c.start()

    loads[5].wait()
    r, n = iota((LANES, 64), 0), iota((LANES, 64), 1)
    r_b, r_a = r & 15, (r >> 7) * 16
    left = mm(onehot(r_a + r_b == n), em_ref[...]).astype(BF16)

    def columns(mask):
        return mm_nt(left, onehot(mask))

    rr, cc = (iota((LANES, LANES), 0) >> 4) & 7, (iota((LANES, LANES), 1) >> 4) & 7
    same = jnp.where(rr == cc, columns(r_a + r_b == n), 0.0)
    after, before = rr == cc - 1, rr == cc + 1
    one_after = jnp.where(after, columns((r_a + 15 == n) & (r_b == 0)), 0.0)
    one_before = jnp.where(before, columns((r_a == n) & (r_b == 15)), 0.0)
    two_after = jnp.where(after, columns((r_a + r_b + 14 == n) & (r_b < 2)), 0.0)
    two_before = jnp.where(before, columns((r_a + r_b - 14 == n) & (r_b >= 14)), 0.0)
    wmat[0] = (same + one_after + one_before).astype(BF16)
    first, second = (cc == 0) | (cc == 6), (cc == 1) | (cc == 7)
    shared = jnp.where(second, two_after, one_after) + jnp.where(first, two_before, one_before)
    wmat[1] = (same + shared).astype(BF16)

    def sides_merge(rows):
        lo, hi = rows.start, rows.stop
        lane = iota((hi - lo, 8, 128), 2)
        right, left = side_recv[0, rows], side_recv[1, rows]
        st, ob = slice(UP + lo, UP + hi), slice(O_UP + lo, O_UP + hi)
        own = state[st, :, 384:512]
        own = jnp.where(lane < 32, own, jnp.where(lane < 80, right, left))
        state[st, :, 0:128], state[st, :, 384:512] = fill(state[st, :, 0:128], own)
        both = jnp.where(lane < 80, left, right)
        oi[ob, :, 384:512] = jnp.where(
            lane < 32,
            oi[ob, :, 384:512],
            jnp.where(lane < 80, turn(both, -48), turn(both, 48)),
        )

    def sides_merge_scale():
        lane = iota((16, 128), 1)
        for a in range(4):
            scale_own[a, :, 384:512] = jnp.where(
                lane < 32,
                scale_own[a, :, 384:512],
                jnp.where(lane < 80, sscale_recv[0, a], sscale_recv[1, a]),
            )

    def fill(first, three):
        lane = iota(first.shape, first.ndim - 1)
        ahead = turn(three, 6)
        first_new = jnp.where(lane < 3, ahead, first)
        three_new = jnp.where((lane >= 32) & (lane < 35), ahead, three)
        three_new = jnp.where((lane >= 29) & (lane < 32), turn(three, -6), three_new)
        three_new = jnp.where(lane >= 125, turn(first, -6), three_new)
        return first_new, three_new

    def fill_arrived(lo, hi):
        v = state[lo:hi, :, 0:128]
        lane = iota(v.shape, 2)
        state[lo:hi, :, 0:128] = jnp.where(lane < 3, turn(state[lo:hi, :, 384:512], 6), v)

    def scale_row(a, e, cols):
        if e < 5:
            v = scale_up[a, e : e + 1, cols]
        elif e < 18:
            v = scale_own[a, e - 5 : e - 4, cols]
        else:
            v = scale_down[a, e - 18 : e - 17, cols]
        return jnp.broadcast_to(v, (8, 128))

    def products(t, elems, rows, begun=()):
        src = states[t]
        for q in range(4):
            cols = slice(128 * q, 128 * q + 128)
            parts = []
            for a in range(4):
                v = [src[UP + STARTS[e] + a, :, cols] * scale_row(a, e, cols) for e in elems]
                parts.append(jnp.concatenate(v, axis=0).astype(BF16))
            o = mm(jnp.concatenate(parts, axis=1), wmat[q // 3])
            for row in rows:
                terms = [
                    o[8 * n : 8 * n + 8, 128 * a : 128 * a + 128]
                    for n, e in enumerate(elems)
                    for a in range(4)
                    if STARTS[e] + a == row and block_of(e) == owner(row)
                ]
                if row in begun:
                    terms.append(asm[t, O_UP + row, :, cols])
                asm[t, O_UP + row, :, cols] = total(terms)

    def update(t, first, last):
        dst = states[t + 1]
        step = 4
        for r0 in range(first, last, step):
            n = min(step, last - r0)
            lane = iota((n, 8, 128), 2)
            a0 = O_UP + r0
            tiles = [asm[t, a0 : a0 + n, :, 128 * q : 128 * q + 128] for q in range(4)]
            ahead = [turn(v, 1) for v in tiles]
            back = [turn(v, -1) for v in tiles]
            new = []
            for q in range(4):
                more = jnp.where(
                    lane == 0,
                    ahead[(q + 3) % 4],
                    jnp.where(lane == 127, back[(q + 1) % 4], 0.0),
                )
                cols = slice(128 * q, 128 * q + 128)
                rhs = oi[a0 : a0 + n, :, cols]
                inv = jnp.broadcast_to(oi[a0 : a0 + n, COMP : COMP + 1, cols], (n, 8, 128))
                new.append(rhs - (tiles[q] + more) * inv)
            if t < 3:
                new[0], new[3] = fill(new[0], new[3])
            for q in range(4):
                dst[UP + r0 : UP + r0 + n, :, 128 * q : 128 * q + 128] = new[q]

    def inner(t):
        return range(6 + t, 16 - t)

    def sweep_inner(t):
        products(t, inner(t), range(3 * t, 31 - 3 * t))
        update(t, 3 * t + 1, 30 - 3 * t)

    def sweep_outer(t):
        lo, hi = 3 * t + 1, 30 - 3 * t
        rows = [r for r in range(*UPDATED[t]) if r < lo or r >= hi]
        products(t, [e for e in range(*ACTIVE[t]) if e not in inner(t)], rows, (lo - 1, hi))
        update(t, UPDATED[t][0], lo)
        update(t, hi, UPDATED[t][1])

    CH = 512
    for c in loads[6:]:
        c.wait()
    node = node_ref[...]
    node_row = lax.div(node, jnp.int32(COLS))
    e_col = node - node_row * COLS + 3
    e_lane = jnp.where(e_col < 375, e_col + lax.div(e_col, jnp.int32(15)), e_col + 26)

    def setup_rows():
        live = iota((1, IF_CAP), 1) < count_ref[...]
        dest = jnp.where(live, dest_ref[...], -1)
        tri = onehot(iota((256, 256), 0) < iota((256, 256), 1))
        carry = jnp.zeros((D, 1), F32)
        for b in range(IF_CAP // 256):
            cols = slice(256 * b, 256 * b + 256)
            hot = jnp.where(dest[:, cols] == iota((D, 256), 0), 1.0, 0.0)
            desthot[:, cols] = hot.astype(BF16)
            before = mm(hot.astype(BF16), tri) + carry
            slot_s[:, cols] = jnp.sum(before * hot, axis=0, keepdims=True)
            carry = carry + jnp.sum(hot, axis=1, keepdims=True)
        name = jnp.zeros((D, 128), F32)
        for b in range(IF_CAP // CH):
            cols = slice(CH * b, CH * b + CH)
            colhot[:, cols] = onehot(e_lane[:, cols] == iota((LANES, CH), 0))
            slots = slot_s[:, cols].astype(jnp.int32) + 96 == iota((128, CH), 0)
            slothot[:, cols] = onehot(slot_s[:, cols].astype(jnp.int32) == iota((CAP, CH), 0))
            rowhot[:, cols] = jnp.where(node_row[:, cols] == iota((32, CH), 0), 1.0, 0.0)
            for p in pieces(target_ref[:, cols].astype(F32), 2):
                p = jnp.where(slots, p.astype(F32), 0.0).astype(BF16)
                name = name + mm_nt(desthot[:, cols], p)
        names[...] = name

    def tractions(t):
        lane = iota((1, 256), 1)
        trac = []
        for k in range(3):
            row = jnp.zeros((1, 256), F32)
            for c in range(COMP):
                row = jnp.where((lane & 7) == c, tm_ref[k : k + 1, c : c + 1], row)
            trac.append(jnp.where((iota((32, 256), 1) >> 3) == iota((32, 256), 0), row, 0.0))
        high, low = pieces(jnp.concatenate(trac, axis=0), 2)
        own = states[2 * t + 2][UP : UP + ROWS].reshape(ROWS * 8, LANES)
        own_high, own_low = pieces(own, 2)
        field = mm(high, own_high) + (mm(high, own_low) + mm(low, own_high))
        field_s[192 * t : 192 * t + 192] = jnp.concatenate(pieces(field, 2), axis=0)

    def gather():
        acc = jnp.zeros((D, 256), F32)
        for b in range(IF_CAP // CH):
            cols = slice(CH * b, CH * b + CH)
            v = mm(field_s[...], colhot[:, cols])
            v = jnp.concatenate([v[:96] + v[96:192], v[192:288] + v[288:]], axis=0)
            v = v.reshape(6, 32, CH) * rowhot[:, cols][None]
            v = jnp.sum(v, axis=1, keepdims=True)
            none = jnp.zeros((CAP, CH), BF16)
            for p in pieces(v, 2):
                p = jnp.broadcast_to(p.astype(F32), (6, CAP, CH)).astype(BF16)
                p = (p * slothot[:, cols][None]).reshape(2, 3 * CAP, CH)
                p = jnp.concatenate([p[0], none, p[1], none], axis=0)
                acc = acc + mm_nt(desthot[:, cols], p)
        abuf[:, 0, :] = acc[:, 0:128] + names[...]
        abuf[:, 1, :] = acc[:, 128:256]

    def all_to_all():
        own = pltpu.make_async_copy(abuf.at[g * S + s], arrived.at[0], out_sem.at[1])
        own.start()
        for n, (to_g, to_s) in enumerate(others):
            pltpu.make_async_remote_copy(
                src_ref=abuf.at[to_g * S + to_s],
                dst_ref=arrived.at[n + 1],
                send_sem=all_send,
                recv_sem=all_recv,
                device_id=(to_g, to_s),
                device_id_type=MESH,
            ).start()
        own.wait()
        return pltpu.make_async_remote_copy(
            src_ref=abuf.at[0 : D - 1],
            dst_ref=arrived.at[1:D],
            send_sem=all_send,
            recv_sem=all_recv,
            device_id=others[0],
            device_id_type=MESH,
        )

    def write_adjoint():
        own = states[4][UP : UP + ROWS].reshape(ROWS * 8, LANES)
        lane = iota((LANES, COLS), 0)
        j, b = lane >> 4, lane & 15
        keep = ((j < 25) & (b < 15)) | ((j == 25) & (b > 0))
        back = onehot(keep & (ext_col(lane) == iota((LANES, COLS), 1) + 3))
        n = iota((COMP * ROWS, ROWS * 8), 1)
        unperm = onehot((n & 7) * ROWS + (n >> 3) == iota((COMP * ROWS, ROWS * 8), 0))
        out_ref[...] = pick_rows(unperm, pick(own, back)).reshape(COMP, ROWS, COLS)

    setup_rows()
    for c in side_edges:
        c.wait_recv()
    for rows in edges:
        sides_merge(rows)
    sides_merge_scale()
    row_late = state_rows(16, last_tile) + oi_rows(18, last_tile) + scale_rows(20, last_tile)
    for c in row_late:
        c.start()
    pl.semaphore_wait(know_x, len(line_x))
    for t in line_y:
        pl.semaphore_signal(know_y, inc=1, device_id=t, device_id_type=MESH)
    for c in side_middle:
        c.wait_recv()
    sides_merge(middle)
    for t in range(4):
        sweep_inner(t)
    for c in row_early + row_late:
        c.wait_recv()
    fill_arrived(0, UP)
    fill_arrived(UP + ROWS, UP + ROWS + DOWN)
    sweep_outer(0)
    sweep_outer(1)
    tractions(0)
    sweep_outer(2)
    sweep_outer(3)
    tractions(1)
    gather()
    pl.semaphore_wait(know_y, len(line_y))
    exchange = all_to_all()
    write_adjoint()
    out_copy = pltpu.make_async_copy(out_ref, out_hbm, out_sem.at[0])
    out_copy.start()
    exchange.wait_recv()
    for c in side_edges + side_middle + row_early + row_late:
        c.wait_send()
    exchange.wait_send()
    out_copy.wait()


def on_device(
    G,
    S,
    adjoint_start,
    objective_grad,
    diagonal,
    connect,
    element_scale,
    element_matrix,
    traction_map,
    iface_node,
    iface_dest,
    iface_target,
    iface_count,
):
    hbm = pl.BlockSpec(memory_space=pl.ANY)
    D = G * S
    dma = pltpu.SemaphoreType.DMA
    I32 = jnp.int32
    scratch = [
        pltpu.VMEM((COMP, ROWS, COLS), F32),
        dma((2,)),
        pltpu.VMEM((COMP, ROWS, COLS), F32),
        pltpu.VMEM((COMP, ROWS, COLS), F32),
        pltpu.VMEM((ROWS, COLS), F32),
        pltpu.VMEM((8, ELEMS), I32),
        pltpu.VMEM((64, ELEMS), F32),
        pltpu.VMEM((64, 64), BF16),
        pltpu.VMEM((3, COMP), F32),
        pltpu.VMEM((1, IF_CAP), I32),
        pltpu.VMEM((1, IF_CAP), I32),
        pltpu.VMEM((1, IF_CAP), I32),
        pltpu.VMEM((1, 1), I32),
        dma((11,)),
        *[pltpu.VMEM((UP + ROWS + DOWN, 8, LANES), F32)] * 5,
        pltpu.VMEM((ITERS * 192, LANES), BF16),
        pltpu.VMEM((O_UP + ROWS + O_DOWN, 8, LANES), F32),
        pltpu.VMEM((4, O_UP + ROWS + O_DOWN, 8, LANES), F32),
        pltpu.VMEM((4, 16, LANES), F32),
        pltpu.VMEM((4, 8, LANES), F32),
        pltpu.VMEM((4, 8, LANES), F32),
        pltpu.VMEM((2, LANES, LANES), BF16),
        pltpu.VMEM((8, 384), I32),
        pltpu.VMEM((64, 384), F32),
        pltpu.VMEM((LANES, IF_CAP), BF16),
        pltpu.VMEM((D, IF_CAP), BF16),
        pltpu.VMEM((1, IF_CAP), F32),
        pltpu.VMEM((CAP, IF_CAP), BF16),
        pltpu.VMEM((32, IF_CAP), F32),
        pltpu.VMEM((D, 128), F32),
        pltpu.VMEM((UP + DOWN, 8, 128), F32),
        pltpu.SemaphoreType.REGULAR,
        pltpu.SemaphoreType.REGULAR,
        pltpu.VMEM((2, ROWS, 8, 128), F32),
        pltpu.VMEM((2, ROWS, 8, 128), F32),
        pltpu.VMEM((2, 4, 16, 128), F32),
        pltpu.VMEM((2, 4, 16, 128), F32),
        pltpu.VMEM((D, ITERS, 128), F32),
        dma((22,)),
        dma((22,)),
        dma,
        dma,
    ]
    call = pl.pallas_call(
        functools.partial(kernel, G, S),
        out_shape=(
            jax.ShapeDtypeStruct((COMP, ROWS, COLS), F32),
            jax.ShapeDtypeStruct((D, ITERS, 128), F32),
        ),
        in_specs=[hbm] * 11,
        out_specs=(hbm, hbm),
        scratch_shapes=scratch,
        compiler_params=pltpu.CompilerParams(
            collective_id=0, has_side_effects=True, vmem_limit_bytes=62 * 1024 * 1024
        ),
    )
    adjoint, arrived = call(
        adjoint_start,
        objective_grad,
        diagonal,
        connect,
        element_scale,
        element_matrix,
        traction_map,
        iface_node.reshape(1, IF_CAP),
        iface_dest.reshape(1, IF_CAP),
        iface_target.reshape(1, IF_CAP),
        iface_count.reshape(1, 1),
    )
    adjoint, load = finish(adjoint, arrived)
    return adjoint, load.transpose(1, 0, 2)


def finish_kernel(adj, arr, adj_out, load_out, adj_v, arrived, load_ref, sem):
    arr_load = pltpu.make_async_copy(arr, arrived, sem.at[0])
    adj_load = pltpu.make_async_copy(adj, adj_v, sem.at[1])
    adj_store = pltpu.make_async_copy(adj_v, adj_out, sem.at[2])
    load_store = pltpu.make_async_copy(load_ref, load_out, sem.at[3])
    arr_load.start()
    adj_load.start()
    count = arr.shape[0]
    arr_load.wait()
    got = [arrived[:, t, :].T for t in range(ITERS)]
    name = got[0][96:128]
    high = jnp.floor(name * (1.0 / 128.0))
    low = name - 128.0 * high
    upper = [v.astype(BF16).astype(F32) for v in got]
    lower = [v - u for v, u in zip(got, upper)]
    acc = jnp.zeros((192, 128), F32)
    for q in range(CAP // 4):
        left, right = [], []
        for z in range(4 * q, 4 * q + 4):
            right.append(onehot(low[z : z + 1] == iota((128, count), 0).astype(F32)))
            hit = high[z : z + 1] == iota((16, count), 0).astype(F32)
            v = [
                jnp.where(hit, part[t][32 * k + z : 32 * k + z + 1], 0.0)
                for part in (upper, lower)
                for t in range(ITERS)
                for k in range(3)
            ]
            left.append(jnp.concatenate(v, axis=0).astype(BF16))
        acc = acc + mm_nt(jnp.concatenate(left, axis=1), jnp.concatenate(right, axis=1))
    acc = acc[:96] + acc[96:]
    for t in range(ITERS):
        for k in range(3):
            for h in range(16):
                n = (3 * t + k) * 16 + h
                load_ref[k, t : t + 1, 128 * h : 128 * h + 128] = acc[n : n + 1]
    load_store.start()
    adj_load.wait()
    adj_store.start()
    load_store.wait()
    adj_store.wait()


def finish(adjoint, arrived):
    hbm = pl.BlockSpec(memory_space=pl.ANY)
    load = (3, ITERS, IF_CAP)
    return pl.pallas_call(
        finish_kernel,
        out_shape=(jax.ShapeDtypeStruct(adjoint.shape, F32), jax.ShapeDtypeStruct(load, F32)),
        in_specs=[hbm, hbm],
        out_specs=(hbm, hbm),
        scratch_shapes=[
            pltpu.VMEM(adjoint.shape, F32),
            pltpu.VMEM(arrived.shape, F32),
            pltpu.VMEM(load, F32),
            pltpu.SemaphoreType.DMA((4,)),
        ],
        compiler_params=pltpu.CompilerParams(vmem_limit_bytes=62 * 1024 * 1024),
    )(adjoint, arrived)


def solution(mesh):
    both = ("group", "sub")
    placed = (
        P(None, "group", "sub"),
        P(None, "group", "sub"),
        P("group", "sub"),
        P(None, both),
        P(None, both),
        P(),
        P(),
        P(both),
        P(both, None),
        P(both),
        P(both),
    )
    return jax.shard_map(
        functools.partial(on_device, mesh.shape["group"], mesh.shape["sub"]),
        mesh=mesh,
        in_specs=placed,
        out_specs=(P(None, "group", "sub"), P(None, None, both)),
        check_vma=False,
    )
```

```python
import functools
import jax
import jax.numpy as jnp
from jax import lax
from jax.experimental import pallas as pl
from jax.experimental.pallas import tpu as pltpu
from jax.sharding import PartitionSpec as P

COMP = 6
ROWS = 32
COLS = 384
ELEMS = 338
IF_CAP = 2048
CAP = 32
ITERS = 2
W = 8
LANES = 512
UP, DOWN = 11, 10
O_UP, O_DOWN = 8, 7
STARTS = (
    [-11, -8, -5, -2, -1] + [min(3 * i, ROWS + 2) - 3 for i in range(13)] + [29, 32, 35, 38]
)
ACTIVE = [(0, 22), (1, 21), (2, 20), (4, 18)]
UPDATED = [(-8, 39), (-5, 36), (-3, 35), (0, 32)]
F32 = jnp.float32
BF16 = jnp.bfloat16
MESH = pl.DeviceIdType.MESH
NT = (((1,), (1,)), ((), ()))


def iota(shape, dim):
    return lax.broadcasted_iota(jnp.int32, shape, dim)


def onehot(mask):
    return jnp.where(mask, 1.0, 0.0).astype(BF16)


def mm(a, b):
    return jnp.dot(a, b, preferred_element_type=F32)


def mm_nt(a, b):
    return lax.dot_general(a, b, NT, preferred_element_type=F32)


def pieces(x, n):
    out = []
    for k in range(n):
        p = x.astype(BF16)
        out.append(p)
        if k + 1 < n:
            x = x - p.astype(F32)
    return out


def total(terms):
    terms = list(terms)
    while len(terms) > 1:
        terms = [
            terms[i] + terms[i + 1] if i + 1 < len(terms) else terms[i]
            for i in range(0, len(terms), 2)
        ]
    return terms[0]


def pick(x, sel, n=3):
    return total([mm(p, sel) for p in pieces(x, n)])


def pick_rows(sel, x, n=3):
    return total([mm(sel, p) for p in pieces(x, n)])


def ext_col(lane):
    j = lane >> 4
    return jnp.where(j == 25, 374, 15 * j) + (lane & 15)


def owner(row):
    return 0 if row < 0 else (1 if row < ROWS else 2)


def block_of(e):
    return 0 if e < 5 else (1 if e < 18 else 2)


def kernel(
    G,
    S,
    adj_hbm,
    obj_hbm,
    diag_hbm,
    conn_hbm,
    scale_hbm,
    em_hbm,
    tm_hbm,
    node_hbm,
    dest_hbm,
    target_hbm,
    count_hbm,
    out_hbm,
    arrived,
    out_ref,
    out_sem,
    adj_ref,
    obj_ref,
    diag_ref,
    conn_ref,
    scale_ref,
    em_ref,
    tm_ref,
    node_ref,
    dest_ref,
    target_ref,
    count_ref,
    in_sem,
    state,
    state_1,
    state_2,
    state_3,
    state_4,
    field_s,
    oi,
    asm,
    scale_own,
    scale_up,
    scale_down,
    wmat,
    conn_pad,
    scale_pad,
    colhot,
    desthot,
    slot_s,
    trac_s,
    slothot,
    rowhot,
    names,
    tile_0,
    know_x,
    know_y,
    side_send,
    side_recv,
    sscale_send,
    sscale_recv,
    abuf,
    halo_send,
    halo_recv,
    all_send,
    all_recv,
):
    D = G * S
    states = (state, state_1, state_2, state_3, state_4)
    g = lax.axis_index("group")
    s = lax.axis_index("sub")

    def at(dg, ds):
        return (lax.rem(g + dg + G, G), lax.rem(s + ds + S, S))

    loads = [
        pltpu.make_async_copy(src, dst, in_sem.at[n])
        for n, (src, dst) in enumerate(
            [
                (adj_hbm, adj_ref),
                (diag_hbm, diag_ref),
                (obj_hbm, obj_ref),
                (conn_hbm.at[0:8], conn_ref),
                (scale_hbm, scale_ref),
                (em_hbm, em_ref),
                (tm_hbm, tm_ref),
                (node_hbm, node_ref),
                (dest_hbm, dest_ref),
                (target_hbm, target_ref),
                (count_hbm, count_ref),
            ]
        )
    ]
    for c in loads:
        c.start()
    barrier = pltpu.get_barrier_semaphore()
    X, Z = S // W, W // 2
    x, z, core = s // W, lax.rem(s, W) // 2, lax.rem(s, 2)

    def hops(offset):
        dg, dx, dz, dc = offset
        steps = [min(dg, G - dg), min(dx, X - dx), min(dz, Z - dz)]
        return (sum(n > 0 for n in steps), sum(steps), dc)

    offsets = [
        (dg, dx, dz, dc) for dz in range(Z) for dx in range(X) for dg in range(G) for dc in range(2)
    ]
    others = [
        (
            lax.rem(g + dg, G),
            (lax.rem(x + dx, X) * Z + lax.rem(z + dz, Z)) * 2 + lax.rem(core + dc, 2),
        )
        for dg, dx, dz, dc in sorted(offsets[1:], key=hops, reverse=True)
    ]
    here = s % W
    line_w = [(g, s - here + lax.rem(here + n, W)) for n in range(1, W)]
    line_x = [at(0, W * n) for n in range(1, S // W)]
    line_y = [at(n, 0) for n in range(1, G)]
    near = line_y + [at(0, -1), at(0, 1)] + line_w + line_x
    for t in near:
        pl.semaphore_signal(barrier, inc=1, device_id=t, device_id_type=MESH)

    lane = iota((COLS, LANES), 1)
    sel = onehot((ext_col(lane) == iota((COLS, LANES), 0) + 3) & (lane < 416))
    m = iota((ROWS * 8, COMP * ROWS), 0)
    perm = onehot(((m & 7) * ROWS + (m >> 3) == iota((ROWS * 8, COMP * ROWS), 1)) & ((m & 7) < COMP))
    loads[0].wait()
    first = pick_rows(perm, adj_ref[...].reshape(COMP * ROWS, COLS))
    state[UP : UP + ROWS] = pick(first, sel).reshape(ROWS, 8, LANES)

    loads[1].wait()
    loads[2].wait()
    inverse = 1.0 / diag_ref[...]
    scaled_obj = (obj_ref[...] * inverse[None]).reshape(COMP * ROWS, COLS)
    m = iota((ROWS * 8, ROWS), 0)
    perm_inv = onehot(((m & 7) == COMP) & ((m >> 3) == iota((ROWS * 8, ROWS), 1)))
    first = pick_rows(perm, scaled_obj, 2) + pick_rows(perm_inv, inverse, 2)
    oi[O_UP : O_UP + ROWS] = pick(first, sel, 2).reshape(ROWS, 8, LANES)

    def remote(n, src, dst, dev):
        return pltpu.make_async_remote_copy(
            src_ref=src,
            dst_ref=dst,
            send_sem=halo_send.at[n],
            recv_sem=halo_recv.at[n],
            device_id=dev,
            device_id_type=MESH,
        )

    def turn(v, n):
        return pltpu.roll(v, n % 128, v.ndim - 1)

    def pack_right(two, three, start):
        lane = iota(two.shape, two.ndim - 1)
        return jnp.where(lane < start + 16, turn(two, start - 112), turn(three, start + 16))

    for p in range(0, ROWS, 8):
        st = [state[UP + p : UP + p + 8, :, 128 * q : 128 * q + 128] for q in (0, 2, 3)]
        ob = [oi[O_UP + p : O_UP + p + 8, :, 128 * q : 128 * q + 128] for q in (0, 2, 3)]
        lane = iota((8, 8, 128), 2)
        side_send[0, p : p + 8] = jnp.where(lane < 80, turn(st[0], 32), turn(ob[0], 80))
        side_send[1, p : p + 8] = jnp.where(
            lane < 80, pack_right(ob[1], ob[2], 32), pack_right(st[1], st[2], 80)
        )
    def pair(n, ref, up_to, down_rows, up_rows, cols):
        lo, hi = down_rows
        first, last = up_rows
        return [
            remote(n, ref.at[lo:hi, :, cols], ref.at[0 : hi - lo, :, cols], at(1, 0)),
            remote(
                n + 1,
                ref.at[first:last, :, cols],
                ref.at[up_to : up_to + last - first, :, cols],
                at(-1, 0),
            ),
        ]

    def state_rows(n, cols):
        return pair(n, state, UP + ROWS, (ROWS, UP + ROWS), (UP, UP + DOWN), cols)

    def oi_rows(n, cols):
        return pair(
            n, oi, O_UP + ROWS, (ROWS, O_UP + ROWS), (O_UP, O_UP + O_DOWN), cols
        )

    def scale_rows(n, cols):
        return [
            remote(n, scale_own.at[:, 8:16, cols], scale_up.at[:, :, cols], at(1, 0)),
            remote(n + 1, scale_own.at[:, 0:8, cols], scale_down.at[:, :, cols], at(-1, 0)),
        ]

    pl.semaphore_wait(barrier, len(near))
    edges = (slice(0, DOWN), slice(ROWS - UP, ROWS))
    middle = slice(DOWN, ROWS - UP)
    sides = (at(0, -1), at(0, 1))

    def side_rows(n, rows):
        return [
            remote(n + k, side_send.at[k, rows], side_recv.at[k, rows], sides[k]) for k in range(2)
        ]

    side_edges = side_rows(0, edges[0]) + side_rows(2, edges[1])
    side_edges += [remote(4 + k, sscale_send.at[k], sscale_recv.at[k], sides[k]) for k in range(2)]
    side_middle = side_rows(6, middle)
    tile_0[0:UP] = state[ROWS : UP + ROWS, :, 0:128]
    tile_0[UP:] = state[UP : UP + DOWN, :, 0:128]
    early, last_tile = slice(0, 384), slice(384, 512)
    row_early = state_rows(8, slice(128, 384)) + oi_rows(10, early) + scale_rows(12, early)
    row_early += [
        remote(14, tile_0.at[0:UP], state.at[0:UP, :, 0:128], at(1, 0)),
        remote(15, tile_0.at[UP:], state.at[UP + ROWS :, :, 0:128], at(-1, 0)),
    ]
    scale_early = side_edges[4:] + row_early[4:6]
    for c in side_edges[:4] + row_early[:4] + row_early[6:]:
        c.start()
    for t in line_x:
        pl.semaphore_signal(know_x, inc=1, device_id=t, device_id_type=MESH)

    loads[3].wait()
    loads[4].wait()
    conn_pad[...] = jnp.full_like(conn_pad, -1)
    conn_pad[:, 0:ELEMS] = conn_ref[...]
    scale_pad[...] = jnp.zeros_like(scale_pad)
    scale_pad[:, 0:ELEMS] = scale_ref[...]
    node0 = conn_pad[0:1]
    row0 = lax.div(node0, jnp.int32(390))
    col0 = node0 - row0 * 390
    elem_i = jnp.where(node0 >= 0, lax.div(row0 + 2, jnp.int32(3)), -1)
    elem_j = jnp.where(node0 >= 0, lax.div(col0 + 14, jnp.int32(15)), -1)
    row_hot = onehot(elem_i == iota((16, 384), 0))
    start_row = jnp.minimum(3 * iota((16, LANES), 0), ROWS + 2)
    lane = iota((16, LANES), 1)
    off_side = ((s == 0) & (lane < 3)) | ((s == S - 1) & (lane >= 413))
    j_mask = elem_j[:, None, :] == iota((32, 16, 384), 0)
    for a in range(4):
        sc = scale_pad[16 * a : 16 * a + 16]
        out = []
        for p in pieces(sc, 3):
            p = jnp.where(j_mask, p.astype(F32)[None], 0.0).reshape(LANES, 384)
            out.append(mm_nt(row_hot, p.astype(BF16)))
        r = start_row + a
        off = ((g == 0) & (r < 3)) | ((g == G - 1) & (r >= ROWS + 3)) | off_side
        scale_own[a] = jnp.where(off, 0.0, total(out))
    for a in range(4):
        sscale_send[0, a] = turn(scale_own[a, :, 0:128], 32)
        sscale_send[1, a] = pack_right(scale_own[a, :, 256:384], scale_own[a, :, 384:512], 80)
    for c in scale_early + side_middle:
        c.start()

    loads[5].wait()
    r, n = iota((LANES, 64), 0), iota((LANES, 64), 1)
    r_b, r_a = r & 15, (r >> 7) * 16
    left = mm(onehot(r_a + r_b == n), em_ref[...]).astype(BF16)

    def columns(mask):
        return mm_nt(left, onehot(mask))

    rr, cc = (iota((LANES, LANES), 0) >> 4) & 7, (iota((LANES, LANES), 1) >> 4) & 7
    same = jnp.where(rr == cc, columns(r_a + r_b == n), 0.0)
    after, before = rr == cc - 1, rr == cc + 1
    one_after = jnp.where(after, columns((r_a + 15 == n) & (r_b == 0)), 0.0)
    one_before = jnp.where(before, columns((r_a == n) & (r_b == 15)), 0.0)
    two_after = jnp.where(after, columns((r_a + r_b + 14 == n) & (r_b < 2)), 0.0)
    two_before = jnp.where(before, columns((r_a + r_b - 14 == n) & (r_b >= 14)), 0.0)
    wmat[0] = (same + one_after + one_before).astype(BF16)
    first, second = (cc == 0) | (cc == 6), (cc == 1) | (cc == 7)
    shared = jnp.where(second, two_after, one_after) + jnp.where(first, two_before, one_before)
    wmat[1] = (same + shared).astype(BF16)

    def sides_merge(rows):
        lo, hi = rows.start, rows.stop
        lane = iota((hi - lo, 8, 128), 2)
        right, left = side_recv[0, rows], side_recv[1, rows]
        st, ob = slice(UP + lo, UP + hi), slice(O_UP + lo, O_UP + hi)
        own = state[st, :, 384:512]
        own = jnp.where(lane < 32, own, jnp.where(lane < 80, right, left))
        state[st, :, 0:128], state[st, :, 384:512] = fill(state[st, :, 0:128], own)
        both = jnp.where(lane < 80, left, right)
        oi[ob, :, 384:512] = jnp.where(
            lane < 32,
            oi[ob, :, 384:512],
            jnp.where(lane < 80, turn(both, -48), turn(both, 48)),
        )

    def sides_merge_scale():
        lane = iota((16, 128), 1)
        for a in range(4):
            scale_own[a, :, 384:512] = jnp.where(
                lane < 32,
                scale_own[a, :, 384:512],
                jnp.where(lane < 80, sscale_recv[0, a], sscale_recv[1, a]),
            )

    def fill(first, three):
        lane = iota(first.shape, first.ndim - 1)
        ahead = turn(three, 6)
        first_new = jnp.where(lane < 3, ahead, first)
        three_new = jnp.where((lane >= 32) & (lane < 35), ahead, three)
        three_new = jnp.where((lane >= 29) & (lane < 32), turn(three, -6), three_new)
        three_new = jnp.where(lane >= 125, turn(first, -6), three_new)
        return first_new, three_new

    def fill_arrived(lo, hi):
        v = state[lo:hi, :, 0:128]
        lane = iota(v.shape, 2)
        state[lo:hi, :, 0:128] = jnp.where(lane < 3, turn(state[lo:hi, :, 384:512], 6), v)

    def scale_row(a, e, cols):
        if e < 5:
            v = scale_up[a, e : e + 1, cols]
        elif e < 18:
            v = scale_own[a, e - 5 : e - 4, cols]
        else:
            v = scale_down[a, e - 18 : e - 17, cols]
        return jnp.broadcast_to(v, (8, 128))

    def products(t, elems, rows, begun=()):
        src = states[t]
        for q in range(4):
            cols = slice(128 * q, 128 * q + 128)
            parts = []
            for a in range(4):
                v = [src[UP + STARTS[e] + a, :, cols] * scale_row(a, e, cols) for e in elems]
                parts.append(jnp.concatenate(v, axis=0).astype(BF16))
            o = mm(jnp.concatenate(parts, axis=1), wmat[q // 3])
            for row in rows:
                terms = [
                    o[8 * n : 8 * n + 8, 128 * a : 128 * a + 128]
                    for n, e in enumerate(elems)
                    for a in range(4)
                    if STARTS[e] + a == row and block_of(e) == owner(row)
                ]
                if row in begun:
                    terms.append(asm[t, O_UP + row, :, cols])
                asm[t, O_UP + row, :, cols] = total(terms)

    def update(t, first, last):
        dst = states[t + 1]
        step = 4
        for r0 in range(first, last, step):
            n = min(step, last - r0)
            lane = iota((n, 8, 128), 2)
            a0 = O_UP + r0
            tiles = [asm[t, a0 : a0 + n, :, 128 * q : 128 * q + 128] for q in range(4)]
            ahead = [turn(v, 1) for v in tiles]
            back = [turn(v, -1) for v in tiles]
            new = []
            for q in range(4):
                more = jnp.where(
                    lane == 0,
                    ahead[(q + 3) % 4],
                    jnp.where(lane == 127, back[(q + 1) % 4], 0.0),
                )
                cols = slice(128 * q, 128 * q + 128)
                rhs = oi[a0 : a0 + n, :, cols]
                inv = jnp.broadcast_to(oi[a0 : a0 + n, COMP : COMP + 1, cols], (n, 8, 128))
                new.append(rhs - (tiles[q] + more) * inv)
            if t < 3:
                new[0], new[3] = fill(new[0], new[3])
            for q in range(4):
                dst[UP + r0 : UP + r0 + n, :, 128 * q : 128 * q + 128] = new[q]

    def inner(t):
        return range(6 + t, 16 - t)

    def sweep_inner(t):
        products(t, inner(t), range(3 * t, 31 - 3 * t))
        update(t, 3 * t + 1, 30 - 3 * t)

    def sweep_outer(t):
        lo, hi = 3 * t + 1, 30 - 3 * t
        rows = [r for r in range(*UPDATED[t]) if r < lo or r >= hi]
        products(t, [e for e in range(*ACTIVE[t]) if e not in inner(t)], rows, (lo - 1, hi))
        update(t, UPDATED[t][0], lo)
        update(t, hi, UPDATED[t][1])

    CH = 512
    for c in loads[6:]:
        c.wait()
    node = node_ref[...]
    node_row = lax.div(node, jnp.int32(COLS))
    e_col = node - node_row * COLS + 3
    e_lane = jnp.where(e_col < 375, e_col + lax.div(e_col, jnp.int32(15)), e_col + 26)

    def setup_rows():
        live = iota((1, IF_CAP), 1) < count_ref[...]
        dest = jnp.where(live, dest_ref[...], -1)
        tri = onehot(iota((256, 256), 0) < iota((256, 256), 1))
        carry = jnp.zeros((D, 1), F32)
        for b in range(IF_CAP // 256):
            cols = slice(256 * b, 256 * b + 256)
            hot = jnp.where(dest[:, cols] == iota((D, 256), 0), 1.0, 0.0)
            desthot[:, cols] = hot.astype(BF16)
            before = mm(hot.astype(BF16), tri) + carry
            slot_s[:, cols] = jnp.sum(before * hot, axis=0, keepdims=True)
            carry = carry + jnp.sum(hot, axis=1, keepdims=True)
        name = jnp.zeros((D, 128), F32)
        for b in range(IF_CAP // CH):
            cols = slice(CH * b, CH * b + CH)
            colhot[:, cols] = onehot(e_lane[:, cols] == iota((LANES, CH), 0))
            slots = slot_s[:, cols].astype(jnp.int32) + 96 == iota((128, CH), 0)
            slothot[:, cols] = onehot(slot_s[:, cols].astype(jnp.int32) == iota((CAP, CH), 0))
            rowhot[:, cols] = jnp.where(node_row[:, cols] == iota((32, CH), 0), 1.0, 0.0)
            for p in pieces(target_ref[:, cols].astype(F32), 2):
                p = jnp.where(slots, p.astype(F32), 0.0).astype(BF16)
                name = name + mm_nt(desthot[:, cols], p)
        names[...] = name
        lane = iota((1, 256), 1)
        trac = []
        for k in range(3):
            row = jnp.zeros((1, 256), F32)
            for c in range(COMP):
                row = jnp.where((lane & 7) == c, tm_ref[k : k + 1, c : c + 1], row)
            trac.append(jnp.where((iota((32, 256), 1) >> 3) == iota((32, 256), 0), row, 0.0))
        trac_s[...] = jnp.concatenate(pieces(jnp.concatenate(trac, axis=0), 2), axis=0)

    def tractions(t):
        high, low = trac_s[0:96], trac_s[96:192]
        own = states[2 * t + 2][UP : UP + ROWS].reshape(ROWS * 8, LANES)
        own_high, own_low = pieces(own, 2)
        field = mm(high, own_high) + (mm(high, own_low) + mm(low, own_high))
        field_s[192 * t : 192 * t + 192] = jnp.concatenate(pieces(field, 2), axis=0)

    def gather():
        acc = jnp.zeros((D, 256), F32)
        for b in range(IF_CAP // CH):
            cols = slice(CH * b, CH * b + CH)
            v = mm(field_s[...], colhot[:, cols])
            v = jnp.concatenate([v[:96] + v[96:192], v[192:288] + v[288:]], axis=0)
            v = v.reshape(6, 32, CH) * rowhot[:, cols][None]
            v = jnp.sum(v, axis=1, keepdims=True)
            none = jnp.zeros((CAP, CH), BF16)
            for p in pieces(v, 2):
                p = jnp.broadcast_to(p.astype(F32), (6, CAP, CH)).astype(BF16)
                p = (p * slothot[:, cols][None]).reshape(2, 3 * CAP, CH)
                p = jnp.concatenate([p[0], none, p[1], none], axis=0)
                acc = acc + mm_nt(desthot[:, cols], p)
        abuf[:, 0, :] = acc[:, 0:128] + names[...]
        abuf[:, 1, :] = acc[:, 128:256]

    def all_to_all():
        own = pltpu.make_async_copy(abuf.at[g * S + s], arrived.at[0], out_sem.at[1])
        own.start()
        for n, (to_g, to_s) in enumerate(others):
            pltpu.make_async_remote_copy(
                src_ref=abuf.at[to_g * S + to_s],
                dst_ref=arrived.at[n + 1],
                send_sem=all_send,
                recv_sem=all_recv,
                device_id=(to_g, to_s),
                device_id_type=MESH,
            ).start()
        own.wait()
        return pltpu.make_async_remote_copy(
            src_ref=abuf.at[0 : D - 1],
            dst_ref=arrived.at[1:D],
            send_sem=all_send,
            recv_sem=all_recv,
            device_id=others[0],
            device_id_type=MESH,
        )

    def write_adjoint():
        own = states[4][UP : UP + ROWS].reshape(ROWS * 8, LANES)
        lane = iota((LANES, COLS), 0)
        j, b = lane >> 4, lane & 15
        keep = ((j < 25) & (b < 15)) | ((j == 25) & (b > 0))
        back = onehot(keep & (ext_col(lane) == iota((LANES, COLS), 1) + 3))
        n = iota((COMP * ROWS, ROWS * 8), 1)
        unperm = onehot((n & 7) * ROWS + (n >> 3) == iota((COMP * ROWS, ROWS * 8), 0))
        out_ref[...] = pick_rows(unperm, pick(own, back)).reshape(COMP, ROWS, COLS)

    setup_rows()
    for c in side_edges:
        c.wait_recv()
    for rows in edges:
        sides_merge(rows)
    sides_merge_scale()
    row_late = state_rows(16, last_tile) + oi_rows(18, last_tile) + scale_rows(20, last_tile)
    for c in row_late:
        c.start()
    pl.semaphore_wait(know_x, len(line_x))
    for t in line_y:
        pl.semaphore_signal(know_y, inc=1, device_id=t, device_id_type=MESH)
    for c in side_middle:
        c.wait_recv()
    sides_merge(middle)
    for t in range(4):
        sweep_inner(t)
    for c in row_early + row_late:
        c.wait_recv()
    fill_arrived(0, UP)
    fill_arrived(UP + ROWS, UP + ROWS + DOWN)
    sweep_outer(0)
    sweep_outer(1)
    tractions(0)
    sweep_outer(2)
    sweep_outer(3)
    tractions(1)
    gather()
    pl.semaphore_wait(know_y, len(line_y))
    exchange = all_to_all()
    write_adjoint()
    out_copy = pltpu.make_async_copy(out_ref, out_hbm, out_sem.at[0])
    out_copy.start()
    exchange.wait_recv()
    for c in side_edges + side_middle + row_early + row_late:
        c.wait_send()
    exchange.wait_send()
    out_copy.wait()


def on_device(
    G,
    S,
    adjoint_start,
    objective_grad,
    diagonal,
    connect,
    element_scale,
    element_matrix,
    traction_map,
    iface_node,
    iface_dest,
    iface_target,
    iface_count,
):
    hbm = pl.BlockSpec(memory_space=pl.ANY)
    D = G * S
    dma = pltpu.SemaphoreType.DMA
    I32 = jnp.int32
    scratch = [
        pltpu.VMEM((COMP, ROWS, COLS), F32),
        dma((2,)),
        pltpu.VMEM((COMP, ROWS, COLS), F32),
        pltpu.VMEM((COMP, ROWS, COLS), F32),
        pltpu.VMEM((ROWS, COLS), F32),
        pltpu.VMEM((8, ELEMS), I32),
        pltpu.VMEM((64, ELEMS), F32),
        pltpu.VMEM((64, 64), BF16),
        pltpu.VMEM((3, COMP), F32),
        pltpu.VMEM((1, IF_CAP), I32),
        pltpu.VMEM((1, IF_CAP), I32),
        pltpu.VMEM((1, IF_CAP), I32),
        pltpu.VMEM((1, 1), I32),
        dma((11,)),
        *[pltpu.VMEM((UP + ROWS + DOWN, 8, LANES), F32)] * 5,
        pltpu.VMEM((ITERS * 192, LANES), BF16),
        pltpu.VMEM((O_UP + ROWS + O_DOWN, 8, LANES), F32),
        pltpu.VMEM((4, O_UP + ROWS + O_DOWN, 8, LANES), F32),
        pltpu.VMEM((4, 16, LANES), F32),
        pltpu.VMEM((4, 8, LANES), F32),
        pltpu.VMEM((4, 8, LANES), F32),
        pltpu.VMEM((2, LANES, LANES), BF16),
        pltpu.VMEM((8, 384), I32),
        pltpu.VMEM((64, 384), F32),
        pltpu.VMEM((LANES, IF_CAP), BF16),
        pltpu.VMEM((D, IF_CAP), BF16),
        pltpu.VMEM((1, IF_CAP), F32),
        pltpu.VMEM((192, 256), BF16),
        pltpu.VMEM((CAP, IF_CAP), BF16),
        pltpu.VMEM((32, IF_CAP), F32),
        pltpu.VMEM((D, 128), F32),
        pltpu.VMEM((UP + DOWN, 8, 128), F32),
        pltpu.SemaphoreType.REGULAR,
        pltpu.SemaphoreType.REGULAR,
        pltpu.VMEM((2, ROWS, 8, 128), F32),
        pltpu.VMEM((2, ROWS, 8, 128), F32),
        pltpu.VMEM((2, 4, 16, 128), F32),
        pltpu.VMEM((2, 4, 16, 128), F32),
        pltpu.VMEM((D, ITERS, 128), F32),
        dma((22,)),
        dma((22,)),
        dma,
        dma,
    ]
    call = pl.pallas_call(
        functools.partial(kernel, G, S),
        out_shape=(
            jax.ShapeDtypeStruct((COMP, ROWS, COLS), F32),
            jax.ShapeDtypeStruct((D, ITERS, 128), F32),
        ),
        in_specs=[hbm] * 11,
        out_specs=(hbm, hbm),
        scratch_shapes=scratch,
        compiler_params=pltpu.CompilerParams(
            collective_id=0, has_side_effects=True, vmem_limit_bytes=62 * 1024 * 1024
        ),
    )
    adjoint, arrived = call(
        adjoint_start,
        objective_grad,
        diagonal,
        connect,
        element_scale,
        element_matrix,
        traction_map,
        iface_node.reshape(1, IF_CAP),
        iface_dest.reshape(1, IF_CAP),
        iface_target.reshape(1, IF_CAP),
        iface_count.reshape(1, 1),
    )
    adjoint, load = finish(adjoint, arrived)
    return adjoint, load.transpose(1, 0, 2)


def finish_kernel(adj, arr, adj_out, load_out, adj_v, arrived, load_ref, sem):
    arr_load = pltpu.make_async_copy(arr, arrived, sem.at[0])
    adj_load = pltpu.make_async_copy(adj, adj_v, sem.at[1])
    adj_store = pltpu.make_async_copy(adj_v, adj_out, sem.at[2])
    load_store = pltpu.make_async_copy(load_ref, load_out, sem.at[3])
    arr_load.start()
    adj_load.start()
    count = arr.shape[0]
    arr_load.wait()
    got = [arrived[:, t, :].T for t in range(ITERS)]
    name = got[0][96:128]
    high = jnp.floor(name * (1.0 / 128.0))
    low = name - 128.0 * high
    upper = [v.astype(BF16).astype(F32) for v in got]
    lower = [v - u for v, u in zip(got, upper)]
    acc = jnp.zeros((192, 128), F32)
    for q in range(CAP // 4):
        left, right = [], []
        for z in range(4 * q, 4 * q + 4):
            right.append(onehot(low[z : z + 1] == iota((128, count), 0).astype(F32)))
            hit = high[z : z + 1] == iota((16, count), 0).astype(F32)
            v = [
                jnp.where(hit, part[t][32 * k + z : 32 * k + z + 1], 0.0)
                for part in (upper, lower)
                for t in range(ITERS)
                for k in range(3)
            ]
            left.append(jnp.concatenate(v, axis=0).astype(BF16))
        acc = acc + mm_nt(jnp.concatenate(left, axis=1), jnp.concatenate(right, axis=1))
    acc = acc[:96] + acc[96:]
    for t in range(ITERS):
        for k in range(3):
            for h in range(16):
                n = (3 * t + k) * 16 + h
                load_ref[k, t : t + 1, 128 * h : 128 * h + 128] = acc[n : n + 1]
    load_store.start()
    adj_load.wait()
    adj_store.start()
    load_store.wait()
    adj_store.wait()


def finish(adjoint, arrived):
    hbm = pl.BlockSpec(memory_space=pl.ANY)
    load = (3, ITERS, IF_CAP)
    return pl.pallas_call(
        finish_kernel,
        out_shape=(jax.ShapeDtypeStruct(adjoint.shape, F32), jax.ShapeDtypeStruct(load, F32)),
        in_specs=[hbm, hbm],
        out_specs=(hbm, hbm),
        scratch_shapes=[
            pltpu.VMEM(adjoint.shape, F32),
            pltpu.VMEM(arrived.shape, F32),
            pltpu.VMEM(load, F32),
            pltpu.SemaphoreType.DMA((4,)),
        ],
        compiler_params=pltpu.CompilerParams(vmem_limit_bytes=62 * 1024 * 1024),
    )(adjoint, arrived)


def solution(mesh):
    both = ("group", "sub")
    placed = (
        P(None, "group", "sub"),
        P(None, "group", "sub"),
        P("group", "sub"),
        P(None, both),
        P(None, both),
        P(),
        P(),
        P(both),
        P(both, None),
        P(both),
        P(both),
    )
    return jax.shard_map(
        functools.partial(on_device, mesh.shape["group"], mesh.shape["sub"]),
        mesh=mesh,
        in_specs=placed,
        out_specs=(P(None, "group", "sub"), P(None, None, both)),
        check_vma=False,
    )
```
